128 devices in a mesh: tile: 16 (over x, y), field: 8 (over z, core).
Axes of the slice: x: 4, y: 4, z: 4, core: 2. Of those that a mesh axis runs over, the one named last changes fastest.
Arguments:
- right_side: float32 [8, 256, 16384], P(None, 'tile', 'field'), may hold values from -6 to 6
- kappa_field: float32 [8, 256, 16384], P(None, 'tile', 'field'), may hold values from 0.05 to 2
- tau_field: float32 [8, 256, 16384], P(None, 'tile', 'field'), may hold values from 0.03 to 0.3
- curvature: float32 [8, 256, 16384], P(None, 'tile', 'field'), may hold values from 0.2 to 2
- detect_prob: float32 [8], replicated, may hold values from 0.2 to 0.7
- site_cells: int32 [16, 8, 16, 128], P('tile', 'field'), may hold values from 0 to 32767
- site_offsets: float32 [16, 8, 16, 2, 128], P('tile', 'field'), may hold values from 0 to 1
- site_count: int32 [16, 8, 16], P('tile', 'field'), may hold values from 0 to 128, as said below
- visit_count: int32 [16, 8, 16, 128], P('tile', 'field'), may hold values from 1 to 8
- detections: int32 [16, 8, 16, 8, 128], P('tile', 'field'), may hold values from 0 to 8, as said below
- surveyed: int32 [16, 8, 16, 8, 128], P('tile', 'field'), may hold values 0 or 1
Outputs:
- latent: float32 [8, 256, 16384], P(None, 'tile', 'field')
- site_grad: float32 [16, 8, 16, 8, 128], P('tile', 'field')
The draws below stay inside these ranges and needn't reach their ends.
Inputs may be any that keep to these rules, and one draw needn't show every extreme that they name: `site_count`: some block holds exactly 128 live slots. `detections`: at most the site's visit count.
All inputs are finite; a program needn't handle non-finite values. No bound on the sum of `surveyed` on one device may be relied on, other than what follows from the above.
Results may differ from the reference program's by a relative error of at most 0.0001.
Values sent between devices are 32-bit elements; how exact they have to be, the bound alone decides.
No kernel may reach another device: no remote copies, remote signals or barrier semaphores. Data moves between devices by JAX's collectives and lax.ppermute only.
A program may use at most 128 MiB of HBM per device.

```python
import math
import jax
import jax.numpy as jnp
from jax import lax

F = 8
RD = 16
CD = 2048
CAP = 128
ITERS = 8
TILES = 16
BANDS = 8
NR = 256
NC = 16384


def visit_pair(key):
    first, second = jax.random.split(key)
    visits = jax.random.randint(first, (TILES, BANDS, TILES, CAP), 1, 9)
    raw = jax.random.randint(second, (TILES, BANDS, TILES, F, CAP), 0, 9)
    found = raw % (visits[:, :, :, None, :] + 1)
    return (visits, found)


def draw_visit_count(key, part):
    visits, found = visit_pair(key)
    return visits


def draw_detections(key, part):
    visits, found = visit_pair(key)
    return found


def draw_site_count(key, part):
    key = jax.random.fold_in(key, 5)
    first, second = jax.random.split(key)
    level = jax.random.randint(first, (1, 1, TILES), 1, 5)
    cut = jax.random.randint(second, (TILES, BANDS, TILES), 0, CAP // 4 + 1)
    count = jnp.maximum(CAP * level // 4 - cut, 0)
    anchor = (lax.broadcasted_iota(jnp.int32, (TILES, BANDS, TILES), 0) == 0) & (lax.broadcasted_iota(jnp.int32, (TILES, BANDS, TILES), 1) == 0) & (lax.broadcasted_iota(jnp.int32, (TILES, BANDS, TILES), 2) == 0)
    return jnp.where(anchor, CAP, count).astype(jnp.int32)


def place_ends(values, rng, low, top_value):
    place = [jax.random.randint(jax.random.fold_in(rng, axis), (), 0, length) for axis, length in enumerate(values.shape)]
    longest = values.shape.index(max(values.shape))
    beside = place[:longest] + [(place[longest] + 1) % values.shape[longest]] + place[longest + 1:]
    return values.at[tuple(place)].set(low).at[tuple(beside)].set(top_value)


def steps_of(stream_key, shape, shards, smallest, top_value):
    factor_of = 1.0
    for axis_at, shards_of in shards:
        heights = jax.random.uniform(jax.random.fold_in(jax.random.fold_in(stream_key, 6), axis_at), (shards_of,), jnp.float32, smallest / len(shards), top_value / len(shards))
        factor_of = factor_of * jnp.repeat(jnp.exp(heights), shape[axis_at] // shards_of).reshape((-1,) + (1,) * (len(shape) - 1 - axis_at))
    return factor_of


def normal_values(key, extent, spread, limit, pieces=(), held_as=jnp.bfloat16):
    loudness = steps_of(key, extent, pieces, -0.22, 0.18) if pieces else 1.0
    drawn = jax.random.normal(key, extent, jnp.float32) * spread * loudness
    return jnp.minimum(jnp.maximum(drawn, -limit), limit).astype(held_as)


def setup_inputs(seed: int = 0) -> dict:
    arg_keys = jax.random.split(jax.random.key(seed), 12)
    return {
        "right_side": normal_values(arg_keys[0], (F, NR, NC), 1.0, 6.0, ((1, 16), (2, 8)), jnp.float32),
        "kappa_field": jnp.clip(jnp.exp(math.log(2.0) - 3.6888794 * jax.random.uniform(arg_keys[1], (F, NR, NC), jnp.float32) ** steps_of(arg_keys[1], (F, NR, NC), ((1, 16), (2, 8)), -0.2, 0.2)), 0.05, 2.0),
        "tau_field": jnp.clip(jnp.exp(math.log(0.3) - 2.3025852 * jax.random.uniform(arg_keys[2], (F, NR, NC), jnp.float32) ** steps_of(arg_keys[2], (F, NR, NC), ((1, 16), (2, 8)), -0.2, 0.2)), 0.03, 0.3),
        "curvature": jnp.clip(jnp.exp(math.log(2.0) - 2.3025851 * jax.random.uniform(arg_keys[3], (F, NR, NC), jnp.float32) ** steps_of(arg_keys[3], (F, NR, NC), ((1, 16), (2, 8)), -0.2, 0.2)), 0.2, 2.0),
        "detect_prob": jnp.clip(jax.random.uniform(arg_keys[4], (F,), jnp.float32, 0.2, 0.7), 0.2, 0.7),
        "site_cells": place_ends(jax.random.randint(arg_keys[5], (TILES, BANDS, TILES, CAP), 0, RD * CD), jax.random.fold_in(arg_keys[5], 1), 0, (RD * CD) - 1).astype(jnp.int32),
        "site_offsets": jnp.clip(1.0 * jax.random.uniform(arg_keys[6], (TILES, BANDS, TILES, 2, CAP), jnp.float32) ** steps_of(arg_keys[6], (TILES, BANDS, TILES, 2, CAP), ((0, 16), (1, 8)), -0.2, 0.2), 0.0, 1.0),
        "site_count": draw_site_count(jax.random.fold_in(arg_keys[11], 71), 0),
        "visit_count": draw_visit_count(jax.random.fold_in(arg_keys[11], 71), 0),
        "detections": draw_detections(jax.random.fold_in(arg_keys[11], 71), 0),
        "surveyed": place_ends((jax.random.randint(arg_keys[10], (TILES, BANDS, TILES, F, CAP), 0, 4) < 3).astype(jnp.int32), jax.random.fold_in(arg_keys[10], 1), 0, 1),
    }


def neighbours(padded):
    return padded[:, 2:, 1:-1] + padded[:, :-2, 1:-1] + padded[:, 1:-1, 2:] + padded[:, 1:-1, :-2]


def stencil(values, kappa_field):
    padded = jnp.pad(values, ((0, 0), (1, 1), (1, 1)))
    return (kappa_field + 4.0) * values - neighbours(padded)


def operate(values, kappa_field, tau_field, curvature):
    return stencil(tau_field * stencil(values, kappa_field), kappa_field) + curvature * values


def reference(right_side, kappa_field, tau_field, curvature, detect_prob, site_cells, site_offsets, site_count, visit_count, detections, surveyed):
    latent = jnp.zeros_like(right_side)
    residual = right_side
    direction = right_side
    norm_now = jnp.sum(residual * residual, axis=(1, 2), keepdims=True)
    for sweep in range(ITERS):
        image = operate(direction, kappa_field, tau_field, curvature)
        alpha = norm_now / jnp.sum(direction * image, axis=(1, 2), keepdims=True)
        latent = latent + alpha * direction
        residual = residual - alpha * image
        norm_next = jnp.sum(residual * residual, axis=(1, 2), keepdims=True)
        direction = residual + (norm_next / norm_now) * direction
        norm_now = norm_next
    padded = jnp.pad(latent, ((0, 0), (0, 1), (0, 1)))
    width = NC + 1
    flat = padded.reshape(F, -1)
    dest = lax.broadcasted_iota(jnp.int32, site_cells.shape, 2)
    band = lax.broadcasted_iota(jnp.int32, site_cells.shape, 1)
    row_index = (dest * RD + site_cells // CD).astype(jnp.int32)
    col_index = (band * CD + site_cells % CD).astype(jnp.int32)
    base = (row_index * width + col_index).astype(jnp.int32)

    def corner(offset):
        return jnp.moveaxis(jnp.take(flat, base + offset, axis=1), 0, 3)

    row_frac = site_offsets[:, :, :, 0:1, :]
    col_frac = site_offsets[:, :, :, 1:2, :]
    predictor = ((1.0 - row_frac) * (1.0 - col_frac) * corner(0) + row_frac * (1.0 - col_frac) * corner(width)
                 + (1.0 - row_frac) * col_frac * corner(1) + row_frac * col_frac * corner(width + 1))
    slots = lax.broadcasted_iota(jnp.int32, site_cells.shape, 3)
    live = (slots < site_count[..., None]).astype(jnp.float32)[:, :, :, None, :]
    visits = visit_count.astype(jnp.float32)[:, :, :, None, :]
    miss_prob = jnp.exp(visits * jnp.log(1.0 - detect_prob)[:, None])
    expo = jnp.exp(predictor)
    seen_grad = 1.0 / (1.0 + expo)
    miss_grad = -(1.0 - miss_prob) * expo / ((1.0 + expo) * (1.0 + miss_prob * expo))
    site_grad = jnp.where(detections > 0, seen_grad, miss_grad) * surveyed.astype(jnp.float32) * live
    return latent, site_grad
```

```python
import functools

import jax
import jax.numpy as jnp
from jax import lax
from jax.experimental import pallas as pl
from jax.experimental.pallas import tpu as pltpu
from jax.sharding import PartitionSpec as P

ITERS = 8
F = 8
PAD = 4
SIDE = 16
LANES = 128
LOW, HIGH = 0.2, 15.0
MID, HALF = 0.5 * (HIGH + LOW), 0.5 * (HIGH - LOW)
PIVOT = 3e-4
VMEM = pl.BlockSpec(memory_space=pltpu.VMEM)
SMEM = pl.BlockSpec(memory_space=pltpu.SMEM)
PARAMS = pltpu.CompilerParams(vmem_limit_bytes=16 * 1024 * 1024)


def held(x):
    return pltpu.with_memory_space_constraint(x, pltpu.VMEM)


def columns_kernel(*refs):
    firsts, lasts, (to_left, to_right) = refs[0:4], refs[4:8], refs[8:]
    lane = lax.broadcasted_iota(jnp.int32, (16, F, LANES), 2)
    for out, blocks, start in ((to_left, firsts, 0), (to_right, lasts, LANES - SIDE)):
        packed = jnp.zeros((16, F, LANES), jnp.float32)
        for a, ref in enumerate(blocks):
            block = jnp.swapaxes(ref[...], 0, 1)
            shift = (SIDE * a - start) % LANES
            moved = pltpu.roll(block, shift, 2) if shift else block
            mine = (lane >= SIDE * a) & (lane < SIDE * (a + 1))
            packed = jnp.where(mine, moved, packed)
        out[...] = packed


def columns_of(fields):
    rows, cols = fields[0].shape[1:]
    first = pl.BlockSpec((F, rows, LANES), lambda i: (0, 0, 0))
    last = pl.BlockSpec((F, rows, LANES), lambda i: (0, 0, cols // LANES - 1))
    out = pl.BlockSpec((rows, F, LANES), lambda i: (0, 0, 0))
    shape = jax.ShapeDtypeStruct((rows, F, LANES), jnp.float32)
    return pl.pallas_call(
        columns_kernel,
        grid=(1,),
        in_specs=[first] * 4 + [last] * 4,
        out_specs=[out, out],
        out_shape=[shape, shape],
        name="columns",
    )(*fields, *fields)


DEPTHS = (4, 3, 3, 2)


def prepare_kernel(rows, cols, flags, *refs):
    fields, (left, right), outs, (to_up, to_down) = refs[0:4], refs[4:6], refs[6:10], refs[10:]
    lane = lax.broadcasted_iota(jnp.int32, (rows, F, LANES), 2)

    def shaped(a, x):
        if a == 1:
            return x + 4.0
        if a == 2:
            return x * (1.0 / HALF)
        if a == 3:
            return (x - MID) * (1.0 / HALF)
        return x

    def store(a, at, block):
        if a == 0:
            outs[0][0, PAD : PAD + rows, :, at] = block
        else:
            outs[a][PAD : PAD + rows, :, at] = block
        base, depth = sum(DEPTHS[:a]), DEPTHS[a]
        to_up[base : base + depth, :, at] = block[:depth]
        to_down[base : base + depth, :, at] = block[rows - depth :]

    for a in range(4):

        def step(c, carry, a=a):
            at = pl.ds(pl.multiple_of(c * LANES, LANES), LANES)
            store(a, at, shaped(a, jnp.swapaxes(fields[a][:, :, at], 0, 1)))
            return carry

        lax.fori_loop(0, cols // LANES, step, 0)
        shift = (-SIDE * a) % LANES
        after = shaped(a, pltpu.roll(right[...], shift, 2) if shift else right[...])
        before = shaped(a, pltpu.roll(left[...], (LANES - SIDE * (a + 1)) % LANES, 2))
        extra = jnp.where(lane < SIDE, after * flags[1], 0.0) + jnp.where(lane >= LANES - SIDE, before * flags[0], 0.0)
        store(a, pl.ds(cols, LANES), extra)


def prepare(flags, fields, left, right):
    rows, cols = fields[0].shape[1:]
    wide = cols + LANES
    f32 = jnp.float32
    ext = (rows + 2 * PAD, F, wide)
    packed = jax.ShapeDtypeStruct((sum(DEPTHS), F, wide), f32)
    return pl.pallas_call(
        functools.partial(prepare_kernel, rows, cols),
        in_specs=[SMEM] + [VMEM] * 6,
        out_specs=[VMEM] * 6,
        out_shape=[pltpu.VMEM((ITERS,) + ext, f32)] + [pltpu.VMEM(ext, f32)] * 3 + [packed, packed],
        compiler_params=PARAMS,
        name="prepare",
    )(flags, *fields, left, right)


def phase_kernel(p, rows, cols, flags, mask, basis_in, k_in, t_in, c_in, up, down, *refs):
    first, last = p == 0, p == ITERS // 2 - 1
    basis, refs = refs[0], refs[1:]
    if first:
        kap, tau, cur, refs = refs[0], refs[1], refs[2], refs[3:]
    else:
        kap, tau, cur = k_in, t_in, c_in
    if last:
        sums, scaled, one = refs
    else:
        to_up, to_down, sums, scaled, one = refs
    wide = cols + LANES
    now = 2 * p

    for source, flag, begin in ((up, 2, None), (down, 3, PAD + rows)):
        base = 0
        for a, depth in enumerate(DEPTHS if first else (PAD,)):
            at = PAD - depth if begin is None else begin
            for i in range(depth):
                row = source[base + i] * flags[flag]
                if a == 0:
                    basis[now, at + i] = row
                else:
                    (None, kap, tau, cur)[a][at + i] = row
            base += depth

    def around(ref, r):
        v = ref[r]
        sides = pltpu.roll(v, 1, 1) + pltpu.roll(v, wide - 1, 1)
        return v, ref[r - 1] + ref[r + 1] + sides

    def scale_rows(ref, low, high):
        def step(r, carry):
            v, near = around(ref, r)
            scaled[r] = tau[r] * (kap[r] * v - near)
            return carry

        lax.fori_loop(low, high, step, 0)

    side = mask[...]

    def image(ref, r):
        s, near = around(scaled, r)
        out = kap[r] * s - near + cur[r] * ref[r]
        flag = jnp.where(r < PAD, flags[2], jnp.where(r >= PAD + rows, flags[3], 1.0))
        return jnp.concatenate([out[:, :cols], out[:, cols:] * side], axis=1) * flag

    def folded(x):
        parts = [x[:, c : c + LANES] for c in range(0, cols, LANES)]
        while len(parts) > 1:
            parts = [a + b for a, b in zip(parts[::2], parts[1::2])]
        return parts[0]

    zero = jnp.zeros((F, LANES), jnp.float32)
    current = basis.at[now]
    own_low, own_high = PAD, PAD + rows

    scale_rows(current, own_low - 3, own_high + 3)

    def outer(r, carry):
        one[r] = image(current, r)
        return carry

    lax.fori_loop(own_low - 2, own_low - 1, outer, 0)
    lax.fori_loop(own_high + 1, own_high + 2, outer, 0)

    def advance(r):
        new = image(current, r)
        one[r] = new
        if not first:
            new = 2.0 * new - basis[now - 1, r]
        basis[now + 1, r] = new
        return new

    def beside(r, carry):
        advance(r)
        return carry

    lax.fori_loop(own_low - 1, own_low, beside, 0)
    lax.fori_loop(own_high, own_high + 1, beside, 0)

    def first_rows(r, carry):
        new = advance(r)
        old = current[r]
        out = (carry[0] + folded(new * new), carry[1] + folded(new * old))
        return out + ((carry[2] + folded(old * old),) if first else ())

    squares = lax.fori_loop(own_low, own_high, first_rows, (zero,) * (3 if first else 2))
    sums[0] = squares[1]
    sums[1] = squares[0]
    if first:
        sums[4] = squares[2]

    if last:
        after = basis.at[now + 1]

        def final_rows(r, carry):
            v, near = around(after, r)
            k = kap[r] * v - near
            return carry + folded(tau[r] * k * k + cur[r] * v * v)

        sums[2] = lax.fori_loop(own_low, own_high, final_rows, zero)
        return

    scale_rows(one, own_low - 1, own_high + 1)

    def second_rows(r, carry):
        new = 2.0 * image(one, r) - current[r]
        if not first:
            new = 2.0 * new - basis[now - 2, r]
        basis[now + 2, r] = new
        return carry[0] + folded(new * basis[now + 1, r]), carry[1] + folded(new * new)

    squares = lax.fori_loop(own_low, own_high, second_rows, (zero, zero))
    sums[2] = squares[0]
    sums[3] = squares[1]
    to_up[...] = basis[now + 2, own_low : own_low + PAD]
    to_down[...] = basis[now + 2, own_high - PAD : own_high]


def phase(p, rows, cols, flags, mask, basis, coefs, up, down):
    first, last = p == 0, p == ITERS // 2 - 1
    f32 = jnp.float32
    wide = cols + LANES
    ext = (rows + 2 * PAD, F, wide)
    out_shape = [pltpu.VMEM(basis.shape, f32)]
    aliases = {2: 0}
    if first:
        out_shape += [pltpu.VMEM(ext, f32)] * 3
        aliases.update({3: 1, 4: 2, 5: 3})
    if not last:
        out_shape += [jax.ShapeDtypeStruct((PAD, F, wide), f32)] * 2
    out_shape += [jax.ShapeDtypeStruct((5 if first else 4, F, LANES), f32)]
    outs = pl.pallas_call(
        functools.partial(phase_kernel, p, rows, cols),
        in_specs=[SMEM] + [VMEM] * 7,
        out_specs=[VMEM] * len(out_shape),
        out_shape=out_shape,
        scratch_shapes=[pltpu.VMEM(ext, f32), pltpu.VMEM(ext, f32)],
        input_output_aliases=aliases,
        compiler_params=PARAMS,
        name=f"phase{p}",
    )(flags, mask, held(basis), *[held(c) for c in coefs], up, down)
    basis, outs = outs[0], outs[1:]
    if first:
        coefs, outs = outs[:3], outs[3:]
    if last:
        return basis, coefs, None, None, outs[0]
    return basis, coefs, outs[0], outs[1], outs[2]


def pack_kernel(s0, s1, s2, s3, out):
    lane = lax.broadcasted_iota(jnp.int32, (F, LANES), 1)
    order = [s0[4], s0[0], s0[1], s0[2], s0[3]]
    for s in (s1, s2):
        order += [s[0], s[1], s[2], s[3]]
    order += [s3[0], s3[1], s3[2]]
    table = jnp.zeros((F, LANES), jnp.float32)
    for k, entry in enumerate(order):
        table = jnp.where(lane == k, jnp.sum(entry, axis=1, keepdims=True), table)
    line = table[0:1]
    for f in range(1, F):
        line = line + pltpu.roll(table[f : f + 1], 2 * ITERS * f, 1)
    out[...] = line


def packed_sums(sums):
    return pl.pallas_call(
        pack_kernel,
        in_specs=[VMEM] * 4,
        out_specs=VMEM,
        out_shape=jax.ShapeDtypeStruct((1, LANES), jnp.float32),
        name="sums",
    )(*sums)


def coefficients(line):
    raw = [jnp.sum(jnp.where(lax.broadcasted_iota(jnp.int32, (F, LANES), 1)
                             == 2 * ITERS * lax.broadcasted_iota(jnp.int32, (F, LANES), 0) + k,
                             jnp.broadcast_to(line, (F, LANES)), 0.0), axis=1, keepdims=True)
           for k in range(2 * ITERS)]
    raw = [jnp.broadcast_to(v, (F, LANES)) for v in raw]
    m = [raw[0], raw[1]] + [2.0 * raw[k] - raw[k % 2] for k in range(2, 2 * ITERS - 1)]
    m.append(4.0 * raw[2 * ITERS - 1] - m[2 * ITERS - 3] - 2.0 * m[1])
    zero = jnp.zeros((F, LANES), jnp.float32)
    one = jnp.ones((F, LANES), jnp.float32)

    def moved(v):
        out = [MID * e for e in v] + [zero]
        out[1] = out[1] + HALF * v[0]
        for k in range(1, len(v)):
            out[k - 1] = out[k - 1] + 0.5 * HALF * v[k]
            out[k + 1] = out[k + 1] + 0.5 * HALF * v[k]
        return out

    def against(v, l):
        return MID * v[l] + 0.5 * HALF * (v[l + 1] + v[abs(l - 1)])

    res, way = list(m), list(m)
    res_in, way_in, lat_in = [one], [one], [zero] * ITERS
    lead = one
    now = m[0]
    worst = one
    for it in range(ITERS):
        image = [against(way, l) for l in range(len(way) - 1)]
        alpha = now / (lead * image[it])
        for k in range(it + 1):
            lat_in[k] = lat_in[k] + alpha * way_in[k]
        if it == ITERS - 1:
            break
        res = [res[l] - alpha * image[l] for l in range(len(image))]
        step = moved(way_in)
        res_in = [a - alpha * b for a, b in zip(res_in + [zero], step)]
        lead = res_in[it + 1]
        new = lead * res[it + 1]
        worst = jnp.minimum(worst, res[it + 1] / (lead * m[0]))
        beta = new / now
        way = [res[l] + beta * way[l] for l in range(len(res))]
        way_in = [a + beta * b for a, b in zip(res_in, way_in + [zero])]
        now = new
    return lat_in, worst, now / (m[0])


def weights_kernel(cells, fracs, high, low):
    col = lax.rem(cells[...], high.shape[0] - LANES)
    frac = fracs[...]

    def step(b, carry):
        at = pl.ds(pl.multiple_of(b * LANES, LANES), LANES)
        row = lax.broadcasted_iota(jnp.int32, (LANES, cells.shape[1]), 0) + b * LANES
        w = jnp.where(row == col, 1.0 - frac, jnp.where(row == col + 1, frac, 0.0))
        part = w.astype(jnp.bfloat16)
        high[at] = part
        low[at] = (w - part.astype(jnp.float32)).astype(jnp.bfloat16)
        return carry

    lax.fori_loop(0, high.shape[0] // LANES, step, 0)


def column_weights(cells, fracs, wide):
    shape = pltpu.VMEM((wide, cells.shape[1]), jnp.bfloat16)
    return pl.pallas_call(
        weights_kernel,
        in_specs=[VMEM] * 2,
        out_specs=[VMEM] * 2,
        out_shape=[shape, shape],
        compiler_params=PARAMS,
        name="column_weights",
    )(cells, fracs)


def finish_kernel(rows, cols, line, basis, high, low, cells, fracs, latent, predictor, fine, x_high, x_low, keep):
    wide = cols + LANES
    lat_in, worst, left = coefficients(line[...])
    fine[...] = jnp.where(worst >= PIVOT, 1.0, 0.0)
    for k in range(ITERS):
        keep[k] = lat_in[k]

    def step(c, carry):
        at = pl.ds(pl.multiple_of(c * LANES, LANES), LANES)
        total = keep[0] * basis[0, PAD : PAD + rows + 1, :, at]
        for k in range(1, ITERS):
            total = total + keep[k] * basis[k, PAD : PAD + rows + 1, :, at]
        part = total.astype(jnp.bfloat16)
        rest = (total - part.astype(jnp.float32)).astype(jnp.bfloat16)
        x_high[:, at] = part.reshape((rows + 1) * F, LANES)
        x_low[:, at] = rest.reshape((rows + 1) * F, LANES)

        @pl.when(c < cols // LANES)
        def _():
            latent[:, :, at] = jnp.swapaxes(total[:rows], 0, 1)

        return carry

    lax.fori_loop(0, wide // LANES, step, 0)
    chunk = 4 * LANES
    for c in range(0, cells.shape[1], chunk):
        at = slice(c, c + chunk)
        dot = functools.partial(jnp.dot, preferred_element_type=jnp.float32)
        both = dot(x_high[...], high[:, at]) + dot(x_low[...], high[:, at]) + dot(x_high[...], low[:, at])
        row = cells[:, at] // cols
        frac = fracs[:, at]
        out = jnp.zeros((F, chunk), jnp.float32)
        for r in range(rows + 1):
            w = jnp.where(row == r, 1.0 - frac, jnp.where(row + 1 == r, frac, 0.0))
            out = out + w * both[r * F : (r + 1) * F]
        for i in range(chunk // LANES):
            predictor[c // LANES + i] = out[:, i * LANES : (i + 1) * LANES]


def finish(rows, cols, line, basis, high, low, cells, fracs):
    f32 = jnp.float32
    wide = cols + LANES
    return pl.pallas_call(
        functools.partial(finish_kernel, rows, cols),
        in_specs=[VMEM] * 6,
        out_specs=[VMEM] * 3,
        out_shape=[
            jax.ShapeDtypeStruct((F, rows, cols), f32),
            jax.ShapeDtypeStruct((cells.shape[1] // LANES, F, LANES), f32),
            jax.ShapeDtypeStruct((F, LANES), f32),
        ],
        scratch_shapes=[
            pltpu.VMEM(((rows + 1) * F, wide), jnp.bfloat16),
            pltpu.VMEM(((rows + 1) * F, wide), jnp.bfloat16),
            pltpu.VMEM((ITERS, F, LANES), f32),
        ],
        compiler_params=PARAMS,
        name="finish",
    )(line, held(basis), held(high), held(low), cells, fracs)


def extended(x, sides, width):
    for axis, dim in sides:
        size, length = (lax.axis_size(axis), x.shape[dim])
        up = [(i, (i + 1) % size) for i in range(size - 1)]
        down = [(j, i) for i, j in up]
        last = lax.slice_in_dim(x, length - width, length, axis=dim)
        leading = lax.slice_in_dim(x, 0, width, axis=dim)
        before = lax.ppermute(last, axis, up)
        after = lax.ppermute(leading, axis, down)
        x = jnp.concatenate([before, x, after], axis=dim)
    return x


def passed_along(x, axis, by):
    length = lax.axis_size(axis)
    pairs = [(i, i + by) for i in range(length) if 0 <= i + by < length]
    return lax.ppermute(x, axis, pairs)


def neighbours(padded):
    return padded[:, 2:, 1:-1] + padded[:, :-2, 1:-1] + padded[:, 1:-1, 2:] + padded[:, 1:-1, :-2]


def plain(right_side, kappa_field, tau_field, curvature, got_cells, got_row, got_col):
    def squares(values):
        return lax.psum(jnp.sum(values * values, axis=(1, 2)), ("tile", "field"))[:, None, None]

    def sweep(_, state):
        latent, residual, direction, norm_now = state
        padded = extended(direction, (("tile", 1), ("field", 2)), 1)
        scaled = tau_field * ((kappa_field + 4.0) * direction - neighbours(padded))
        spread = extended(scaled, (("tile", 1), ("field", 2)), 1)
        image = (kappa_field + 4.0) * scaled - neighbours(spread) + curvature * direction
        inner = lax.psum(jnp.sum(direction * image, axis=(1, 2)), ("tile", "field"))[:, None, None]
        alpha = norm_now / inner
        latent = latent + alpha * direction
        residual = residual - alpha * image
        norm_next = squares(residual)
        direction = residual + norm_next / norm_now * direction
        return latent, residual, direction, norm_next

    state = (jnp.zeros_like(right_side), right_side, right_side, squares(right_side))
    latent = lax.fori_loop(0, ITERS, sweep, state)[0]
    upper = passed_along(latent[:, :1, :], "tile", -1)
    tall = jnp.concatenate([latent, upper], axis=1)
    beside = passed_along(tall[:, :, :1], "field", -1)
    wide = jnp.concatenate([tall, beside], axis=2)
    columns = latent.shape[2]
    width = columns + 1
    flat = wide.reshape(wide.shape[0], -1)
    base = (got_cells // columns * width + got_cells % columns).astype(jnp.int32)

    def corner(offset):
        return jnp.take(flat, base + offset, axis=1)

    row_frac = got_row[None]
    col_frac = got_col[None]
    predictor = (
        (1.0 - row_frac) * (1.0 - col_frac) * corner(0)
        + row_frac * (1.0 - col_frac) * corner(width)
        + (1.0 - row_frac) * col_frac * corner(1)
        + row_frac * col_frac * corner(width + 1)
    )
    return latent, jnp.transpose(predictor, (1, 0, 2))


def turned(x, axis, by):
    size = lax.axis_size(axis)
    return lax.ppermute(x, axis, [(i, (i + by) % size) for i in range(size)])


def local(
    right_side,
    kappa_field,
    tau_field,
    curvature,
    detect_prob,
    site_cells,
    site_offsets,
    site_count,
    visit_count,
    detections,
    surveyed,
):
    rows, cols = right_side.shape[1:]
    wide = cols + LANES
    tiles, bands = lax.axis_size("tile"), lax.axis_size("field")
    tile, band = lax.axis_index("tile"), lax.axis_index("field")
    flags = jnp.stack([band > 0, band < bands - 1, tile > 0, tile < tiles - 1]).astype(jnp.float32)
    lane = lax.broadcasted_iota(jnp.int32, (F, LANES), 1)
    mask = jnp.where(lane < SIDE, flags[1], jnp.where(lane >= LANES - SIDE, flags[0], 0.0))

    fields = (right_side, kappa_field, tau_field, curvature)
    to_left, to_right = columns_of(fields)
    from_right = turned(to_left, "field", -1)
    from_left = turned(to_right, "field", 1)
    basis, kap, tau, cur, to_up, to_down = prepare(flags, fields, from_left, from_right)
    coefs = (kap, tau, cur)

    cells = site_cells[0, 0]
    sent = jnp.concatenate([cells.astype(jnp.float32)[:, None], site_offsets[0, 0]], axis=1)
    got = None
    sums = []
    for p in range(ITERS // 2):
        from_down = turned(to_up, "tile", -1)
        from_up = turned(to_down, "tile", 1)
        if p == 0:
            sent, to_up = lax.optimization_barrier((sent, to_up))
            got = lax.all_to_all(sent, "tile", split_axis=0, concat_axis=0, tiled=True)
            got_cells = got[:, 0].astype(jnp.int32)
            got_row, got_col = got[:, 1], got[:, 2]
            high, low = column_weights(got_cells.reshape(1, -1), got_col.reshape(1, -1), wide)
        basis, coefs, to_up, to_down, part = phase(p, rows, cols, flags, mask, basis, coefs, from_up, from_down)
        sums.append(part)

    line = packed_sums(sums)
    spread = jnp.broadcast_to(line[None], (tiles * bands, 1, LANES))
    line = jnp.sum(lax.all_to_all(spread, ("tile", "field"), split_axis=0, concat_axis=0, tiled=True), axis=0)
    latent, predictor, fine = finish(
        rows, cols, line, basis, high, low, got_cells.reshape(1, -1), got_row.reshape(1, -1)
    )
    latent, predictor, _ = lax.while_loop(
        lambda state: state[2],
        lambda state: plain(*fields, got_cells, got_row, got_col) + (False,),
        (latent, predictor, jnp.logical_not(jnp.all(fine > 0.5))),
    )
    returned = lax.all_to_all(predictor, "tile", split_axis=0, concat_axis=0, tiled=True)

    slots = lax.broadcasted_iota(jnp.int32, cells.shape, 1)
    live = (slots < site_count[0, 0][:, None]).astype(jnp.float32)[:, None, :]
    visits = visit_count[0, 0].astype(jnp.float32)[:, None, :]
    miss_prob = jnp.exp(visits * jnp.log(1.0 - detect_prob)[:, None])
    expo = jnp.exp(returned)
    seen_grad = 1.0 / (1.0 + expo)
    miss_grad = -(1.0 - miss_prob) * expo / ((1.0 + expo) * (1.0 + miss_prob * expo))
    site_grad = (
        jnp.where(detections[0, 0] > 0, seen_grad, miss_grad)
        * surveyed[0, 0].astype(jnp.float32)
        * live
    )
    return (latent, site_grad[None, None])


def solution(mesh):
    in_specs = (
        P(None, "tile", "field"),
        P(None, "tile", "field"),
        P(None, "tile", "field"),
        P(None, "tile", "field"),
        P(),
        P("tile", "field", None, None),
        P("tile", "field", None, None, None),
        P("tile", "field", None),
        P("tile", "field", None, None),
        P("tile", "field", None, None, None),
        P("tile", "field", None, None, None),
    )
    out_specs = (P(None, "tile", "field"), P("tile", "field", None, None, None))
    return jax.shard_map(local, mesh=mesh, in_specs=in_specs, out_specs=out_specs, check_vma=False)
```

```python
import functools

import jax
import jax.numpy as jnp
from jax import lax
from jax.experimental import pallas as pl
from jax.experimental.pallas import tpu as pltpu
from jax.sharding import PartitionSpec as P

ITERS = 8
F = 8
PAD = 4
SIDE = 16
LANES = 128
LOW, HIGH = 0.2, 15.0
MID, HALF = 0.5 * (HIGH + LOW), 0.5 * (HIGH - LOW)
VMEM = pl.BlockSpec(memory_space=pltpu.VMEM)
SMEM = pl.BlockSpec(memory_space=pltpu.SMEM)
PARAMS = pltpu.CompilerParams(vmem_limit_bytes=10 * 1024 * 1024)


def held(x):
    return pltpu.with_memory_space_constraint(x, pltpu.VMEM)


def columns_kernel(*refs):
    firsts, lasts, (to_left, to_right) = refs[0:4], refs[4:8], refs[8:]
    lane = lax.broadcasted_iota(jnp.int32, (16, F, LANES), 2)
    for out, blocks, start in ((to_left, firsts, 0), (to_right, lasts, LANES - SIDE)):
        packed = jnp.zeros((16, F, LANES), jnp.float32)
        for a, ref in enumerate(blocks):
            block = jnp.swapaxes(ref[...], 0, 1)
            shift = (SIDE * a - start) % LANES
            moved = pltpu.roll(block, shift, 2) if shift else block
            mine = (lane >= SIDE * a) & (lane < SIDE * (a + 1))
            packed = jnp.where(mine, moved, packed)
        out[...] = packed


def columns_of(fields):
    rows, cols = fields[0].shape[1:]
    first = pl.BlockSpec((F, rows, LANES), lambda i: (0, 0, 0))
    last = pl.BlockSpec((F, rows, LANES), lambda i: (0, 0, cols // LANES - 1))
    out = pl.BlockSpec((rows, F, LANES), lambda i: (0, 0, 0))
    shape = jax.ShapeDtypeStruct((rows, F, LANES), jnp.float32)
    return pl.pallas_call(
        columns_kernel,
        grid=(1,),
        in_specs=[first] * 4 + [last] * 4,
        out_specs=[out, out],
        out_shape=[shape, shape],
        name="columns",
    )(*fields, *fields)


DEPTHS = (4, 3, 3, 2)


def prepare_kernel(rows, cols, flags, *refs):
    fields, (left, right), outs, (to_up, to_down) = refs[0:4], refs[4:6], refs[6:10], refs[10:]
    lane = lax.broadcasted_iota(jnp.int32, (rows, F, LANES), 2)

    def shaped(a, x):
        if a == 1:
            return x + 4.0
        if a == 2:
            return x * (1.0 / HALF)
        if a == 3:
            return (x - MID) * (1.0 / HALF)
        return x

    def store(a, at, block):
        if a == 0:
            outs[0][0, PAD : PAD + rows, :, at] = block
        else:
            outs[a][PAD : PAD + rows, :, at] = block
        base, depth = sum(DEPTHS[:a]), DEPTHS[a]
        to_up[base : base + depth, :, at] = block[:depth]
        to_down[base : base + depth, :, at] = block[rows - depth :]

    for a in range(4):

        def step(c, carry, a=a):
            at = pl.ds(pl.multiple_of(c * LANES, LANES), LANES)
            store(a, at, shaped(a, jnp.swapaxes(fields[a][:, :, at], 0, 1)))
            return carry

        lax.fori_loop(0, cols // LANES, step, 0)
        shift = (-SIDE * a) % LANES
        after = shaped(a, pltpu.roll(right[...], shift, 2) if shift else right[...])
        before = shaped(a, pltpu.roll(left[...], (LANES - SIDE * (a + 1)) % LANES, 2))
        extra = jnp.where(lane < SIDE, after * flags[1], 0.0) + jnp.where(lane >= LANES - SIDE, before * flags[0], 0.0)
        store(a, pl.ds(cols, LANES), extra)


def prepare(flags, fields, left, right):
    rows, cols = fields[0].shape[1:]
    wide = cols + LANES
    f32 = jnp.float32
    ext = (rows + 2 * PAD, F, wide)
    packed = jax.ShapeDtypeStruct((sum(DEPTHS), F, wide), f32)
    return pl.pallas_call(
        functools.partial(prepare_kernel, rows, cols),
        in_specs=[SMEM] + [VMEM] * 6,
        out_specs=[VMEM] * 6,
        out_shape=[pltpu.VMEM((ITERS,) + ext, f32)] + [pltpu.VMEM(ext, f32)] * 3 + [packed, packed],
        compiler_params=PARAMS,
        name="prepare",
    )(flags, *fields, left, right)


def walk(ref, r, count, wide):
    tiles = wide // LANES
    lane = lax.broadcasted_iota(jnp.int32, (F, LANES), 1)
    leftmost, rightmost = lane == 0, lane == LANES - 1

    def load(c):
        return [ref[r - 1 + i, :, c * LANES : (c + 1) * LANES] for i in range(count + 2)]

    def turn(tile, by):
        return [pltpu.roll(v, by, 1) for v in tile[1:-1]]

    now = load(0)
    before = turn([ref[r - 1 + i, :, wide - LANES :] for i in range(count + 2)], 1)
    right, left = turn(now, 1), turn(now, LANES - 1)
    start = left
    for c in range(tiles):
        after = load(c + 1) if c + 1 < tiles else None
        following = turn(after, LANES - 1) if after else start
        near = [
            (now[i] + now[i + 2])
            + (jnp.where(leftmost, before[i], right[i]) + jnp.where(rightmost, following[i], left[i]))
            for i in range(count)
        ]
        yield slice(c * LANES, (c + 1) * LANES), now[1:-1], near
        if after:
            before, right, left, now = right, turn(after, 1), following, after


def pairs(low, high, body, carry):
    return lax.fori_loop(0, (high - low) // 2, lambda i, carry: body(low + 2 * i, carry), carry)


def phase_kernel(p, rows, cols, flags, mask, basis_in, k_in, t_in, c_in, up, down, *refs):
    first, last = p == 0, p == ITERS // 2 - 1
    if last:
        earlier, refs = refs[: ITERS // 2 - 1], refs[ITERS // 2 - 1 :]
    basis, refs = refs[0], refs[1:]
    if first:
        kap, tau, cur, refs = refs[0], refs[1], refs[2], refs[3:]
    else:
        kap, tau, cur = k_in, t_in, c_in
    if last:
        line, scaled, one = refs
    else:
        to_up, to_down, sums, scaled, one = refs
    wide = cols + LANES
    now = 2 * p
    own_low, own_high = PAD, PAD + rows

    for source, flag, begin in ((up, 2, None), (down, 3, own_high)):
        base = 0
        for a, depth in enumerate(DEPTHS if first else (PAD,)):
            at = PAD - depth if begin is None else begin
            for i in range(depth):
                row = source[base + i] * flags[flag]
                if a == 0:
                    basis[now, at + i] = row
                else:
                    (None, kap, tau, cur)[a][at + i] = row
            base += depth

    zero = jnp.zeros((F, LANES), jnp.float32)
    current = basis.at[now]

    def scale(ref, low, high):
        def body(r, carry):
            for at, v, near in walk(ref, r, 2, wide):
                for i in range(2):
                    scaled[r + i, :, at] = tau[r + i, :, at] * (kap[r + i, :, at] * v[i] - near[i])
            return carry

        pairs(low, high, body, 0)

    def image(ref, r):
        for at, s, near in walk(scaled, r, 2, wide):
            out = []
            for i in range(2):
                new = (kap[r + i, :, at] * s[i] - near[i]) + cur[r + i, :, at] * ref[r + i, :, at]
                out.append(new * mask[...] if at.start == cols else new)
            yield at, out

    scale(current, own_low - 3, own_high + 3)
    for r, flag, inner in ((own_low - 2, flags[2], 1), (own_high, flags[3], 0)):
        for at, new in image(current, r):
            for i in range(2):
                value = new[i] * flag
                one[r + i, :, at] = value
                if i == inner:
                    basis[now + 1, r + i, :, at] = value if first else 2.0 * value - basis[now - 1, r + i, :, at]

    def first_rows(r, carry):
        cross = square = start = zero
        for at, new in image(current, r):
            for i in range(2):
                one[r + i, :, at] = new[i]
                value = new[i] if first else 2.0 * new[i] - basis[now - 1, r + i, :, at]
                basis[now + 1, r + i, :, at] = value
                if at.start < cols:
                    old = current[r + i, :, at]
                    cross += value * old
                    square += value * value
                    if first:
                        start += old * old
        out = (carry[0] + cross, carry[1] + square)
        return out + ((carry[2] + start,) if first else ())

    found = pairs(own_low, own_high, first_rows, (zero,) * (3 if first else 2))

    if last:
        after = basis.at[now + 1]

        def final_rows(r, carry):
            total = zero
            for at, v, near in walk(after, r, 2, wide):
                if at.start < cols:
                    for i in range(2):
                        k = kap[r + i, :, at] * v[i] - near[i]
                        total += tau[r + i, :, at] * k * k + cur[r + i, :, at] * v[i] * v[i]
            return carry + total

        found += (pairs(own_low, own_high, final_rows, zero),)
        entries = [earlier[0][4]]
        for s in earlier:
            entries += [s[i] for i in range(4)]
        lane = lax.broadcasted_iota(jnp.int32, (F, LANES), 1)
        table = zero
        for k, entry in enumerate(entries + list(found)):
            table = jnp.where(lane == k, jnp.sum(entry, axis=1, keepdims=True), table)
        total = table[0:1]
        for f in range(1, F):
            total = total + pltpu.roll(table[f : f + 1], 2 * ITERS * f, 1)
        line[...] = jnp.broadcast_to(total[None], line.shape)
        return

    sums[0] = found[0]
    sums[1] = found[1]
    if first:
        sums[4] = found[2]

    scale(one, own_low - 1, own_high + 1)

    def second_rows(r, carry):
        cross = square = zero
        for at, new in image(one, r):
            for i in range(2):
                value = 2.0 * new[i] - current[r + i, :, at]
                if not first:
                    value = 2.0 * value - basis[now - 2, r + i, :, at]
                basis[now + 2, r + i, :, at] = value
                if at.start < cols:
                    cross += value * basis[now + 1, r + i, :, at]
                    square += value * value
        return carry[0] + cross, carry[1] + square

    sums[2], sums[3] = pairs(own_low, own_high, second_rows, (zero, zero))
    to_up[...] = basis[now + 2, own_low : own_low + PAD]
    to_down[...] = basis[now + 2, own_high - PAD : own_high]


def phase(p, rows, cols, flags, mask, basis, coefs, up, down, earlier=(), devices=1):
    first, last = p == 0, p == ITERS // 2 - 1
    f32 = jnp.float32
    wide = cols + LANES
    ext = (rows + 2 * PAD, F, wide)
    out_shape = [pltpu.VMEM(basis.shape, f32)]
    aliases = {2: 0}
    if first:
        out_shape += [pltpu.VMEM(ext, f32)] * 3
        aliases.update({3: 1, 4: 2, 5: 3})
    if last:
        out_shape += [jax.ShapeDtypeStruct((devices, 1, LANES), f32)]
    else:
        out_shape += [jax.ShapeDtypeStruct((PAD, F, wide), f32)] * 2
        out_shape += [jax.ShapeDtypeStruct((5 if first else 4, F, LANES), f32)]
    outs = pl.pallas_call(
        functools.partial(phase_kernel, p, rows, cols),
        in_specs=[SMEM] + [VMEM] * (7 + len(earlier)),
        out_specs=[VMEM] * len(out_shape),
        out_shape=out_shape,
        scratch_shapes=[pltpu.VMEM(ext, f32), pltpu.VMEM(ext, f32)],
        input_output_aliases=aliases,
        compiler_params=PARAMS,
        name=f"phase{p}",
    )(flags, mask, held(basis), *[held(c) for c in coefs], up, down, *earlier)
    basis, outs = outs[0], outs[1:]
    if first:
        coefs, outs = outs[:3], outs[3:]
    if last:
        return basis, outs[0]
    return basis, coefs, outs[0], outs[1], outs[2]


def coefficients(line):
    raw = [jnp.sum(jnp.where(lax.broadcasted_iota(jnp.int32, (F, LANES), 1)
                             == 2 * ITERS * lax.broadcasted_iota(jnp.int32, (F, LANES), 0) + k,
                             jnp.broadcast_to(line, (F, LANES)), 0.0), axis=1, keepdims=True)
           for k in range(2 * ITERS)]
    raw = [jnp.broadcast_to(v, (F, LANES)) for v in raw]
    m = [raw[0], raw[1]] + [2.0 * raw[k] - raw[k % 2] for k in range(2, 2 * ITERS - 1)]
    m.append(4.0 * raw[2 * ITERS - 1] - m[2 * ITERS - 3] - 2.0 * m[1])
    zero = jnp.zeros((F, LANES), jnp.float32)
    one = jnp.ones((F, LANES), jnp.float32)

    def moved(v):
        out = [MID * e for e in v] + [zero]
        out[1] = out[1] + HALF * v[0]
        for k in range(1, len(v)):
            out[k - 1] = out[k - 1] + 0.5 * HALF * v[k]
            out[k + 1] = out[k + 1] + 0.5 * HALF * v[k]
        return out

    def against(v, l):
        return MID * v[l] + 0.5 * HALF * (v[l + 1] + v[abs(l - 1)])

    res, way = list(m), list(m)
    res_in, way_in, lat_in = [one], [one], [zero] * ITERS
    lead = one
    now = m[0]
    pivots = []
    for it in range(ITERS):
        image = [against(way, l) for l in range(len(way) - 1)]
        alpha = now / (lead * image[it])
        for k in range(it + 1):
            lat_in[k] = lat_in[k] + alpha * way_in[k]
        if it == ITERS - 1:
            break
        res = [res[l] - alpha * image[l] for l in range(len(image))]
        step = moved(way_in)
        res_in = [a - alpha * b for a, b in zip(res_in + [zero], step)]
        lead = res_in[it + 1]
        new = lead * res[it + 1]
        pivots.append(res[it + 1] / (lead * m[0]))
        beta = new / now
        way = [res[l] + beta * way[l] for l in range(len(res))]
        way_in = [a + beta * b for a, b in zip(res_in, way_in + [zero])]
        now = new
    fine = pivots[-1] >= 0.3 * pivots[0]
    for pivot in pivots:
        fine = fine & (pivot >= 5e-3) & (pivot <= 20.0)
    return lat_in, fine


def columns_hot_kernel(cells, hot):
    col = lax.rem(cells[...], hot.shape[0] - LANES)

    def step(b, carry):
        at = pl.ds(pl.multiple_of(b * LANES, LANES), LANES)
        row = lax.broadcasted_iota(jnp.int32, (LANES, cells.shape[1]), 0) + b * LANES
        hot[at] = jnp.where(row == col, 1.0, 0.0).astype(jnp.bfloat16)
        return carry

    lax.fori_loop(0, hot.shape[0] // LANES, step, 0)


def columns_hot(cells, wide):
    return pl.pallas_call(
        columns_hot_kernel,
        in_specs=[VMEM],
        out_specs=VMEM,
        out_shape=pltpu.VMEM((wide, cells.shape[1]), jnp.bfloat16),
        compiler_params=PARAMS,
        name="columns_hot",
    )(cells)


def finish_kernel(rows, cols, line, basis, hot, cells, row_frac, col_frac, latent, predictor, fine, parts, keep):
    wide = cols + LANES
    lat_in, good = coefficients(line[...])
    fine[...] = jnp.where(good, 1.0, 0.0)
    for k in range(ITERS):
        keep[k] = lat_in[k]
    lane = lax.broadcasted_iota(jnp.int32, (rows + 1, F, LANES), 2)
    tall = (rows + 1) * F

    def split(x, at, base):
        part = x.astype(jnp.bfloat16)
        rest = (x - part.astype(jnp.float32)).astype(jnp.bfloat16)
        parts[base : base + tall, at] = part.reshape(tall, LANES)
        parts[base + tall : base + 2 * tall, at] = rest.reshape(tall, LANES)

    def step(c, after):
        c = wide // LANES - 1 - c
        at = pl.ds(pl.multiple_of(c * LANES, LANES), LANES)
        total = keep[0] * basis[0, PAD : PAD + rows + 1, :, at]
        for k in range(1, ITERS):
            total = total + keep[k] * basis[k, PAD : PAD + rows + 1, :, at]
        turned = pltpu.roll(total, LANES - 1, 2)
        split(total, at, 0)
        split(jnp.where(lane == LANES - 1, after, turned), at, 2 * tall)

        @pl.when(c < cols // LANES)
        def _():
            latent[:, :, at] = jnp.swapaxes(total[:rows], 0, 1)

        return turned

    lax.fori_loop(0, wide // LANES, step, jnp.zeros((rows + 1, F, LANES), jnp.float32))
    chunk = 4 * LANES
    for c in range(0, cells.shape[1], chunk):
        at = slice(c, c + chunk)
        both = jnp.dot(parts[...], hot[:, at], preferred_element_type=jnp.float32)
        here = both[:tall] + both[tall : 2 * tall]
        beside = both[2 * tall : 3 * tall] + both[3 * tall :]
        row = cells[:, at] // cols
        frac = row_frac[:, at]
        low = jnp.zeros((F, chunk), jnp.float32)
        high = jnp.zeros((F, chunk), jnp.float32)
        for r in range(rows + 1):
            w = jnp.where(row == r, 1.0 - frac, jnp.where(row + 1 == r, frac, 0.0))
            low = low + w * here[r * F : (r + 1) * F]
            high = high + w * beside[r * F : (r + 1) * F]
        side = col_frac[:, at]
        out = (1.0 - side) * low + side * high
        for i in range(chunk // LANES):
            base = (c // LANES + i) * F
            predictor[base : base + F] = out[:, i * LANES : (i + 1) * LANES]


def finish(rows, cols, line, basis, hot, cells, row_frac, col_frac):
    f32 = jnp.float32
    wide = cols + LANES
    return pl.pallas_call(
        functools.partial(finish_kernel, rows, cols),
        in_specs=[VMEM] * 6,
        out_specs=[VMEM] * 3,
        out_shape=[
            jax.ShapeDtypeStruct((F, rows, cols), f32),
            jax.ShapeDtypeStruct((cells.shape[1] // LANES * F, LANES), f32),
            jax.ShapeDtypeStruct((F, LANES), f32),
        ],
        scratch_shapes=[
            pltpu.VMEM((4 * (rows + 1) * F, wide), jnp.bfloat16),
            pltpu.VMEM((ITERS, F, LANES), f32),
        ],
        compiler_params=PARAMS,
        name="finish",
    )(line, held(basis), held(hot), cells, row_frac, col_frac)


def extended(x, sides, width):
    for axis, dim in sides:
        size, length = (lax.axis_size(axis), x.shape[dim])
        up = [(i, (i + 1) % size) for i in range(size - 1)]
        down = [(j, i) for i, j in up]
        last = lax.slice_in_dim(x, length - width, length, axis=dim)
        leading = lax.slice_in_dim(x, 0, width, axis=dim)
        before = lax.ppermute(last, axis, up)
        after = lax.ppermute(leading, axis, down)
        x = jnp.concatenate([before, x, after], axis=dim)
    return x


def passed_along(x, axis, by):
    length = lax.axis_size(axis)
    pairs = [(i, i + by) for i in range(length) if 0 <= i + by < length]
    return lax.ppermute(x, axis, pairs)


def neighbours(padded):
    return padded[:, 2:, 1:-1] + padded[:, :-2, 1:-1] + padded[:, 1:-1, 2:] + padded[:, 1:-1, :-2]


def plain(right_side, kappa_field, tau_field, curvature, got_cells, got_row, got_col):
    def squares(values):
        return lax.psum(jnp.sum(values * values, axis=(1, 2)), ("tile", "field"))[:, None, None]

    def sweep(_, state):
        latent, residual, direction, norm_now = state
        padded = extended(direction, (("tile", 1), ("field", 2)), 1)
        scaled = tau_field * ((kappa_field + 4.0) * direction - neighbours(padded))
        spread = extended(scaled, (("tile", 1), ("field", 2)), 1)
        image = (kappa_field + 4.0) * scaled - neighbours(spread) + curvature * direction
        inner = lax.psum(jnp.sum(direction * image, axis=(1, 2)), ("tile", "field"))[:, None, None]
        alpha = norm_now / inner
        latent = latent + alpha * direction
        residual = residual - alpha * image
        norm_next = squares(residual)
        direction = residual + norm_next / norm_now * direction
        return latent, residual, direction, norm_next

    state = (jnp.zeros_like(right_side), right_side, right_side, squares(right_side))
    latent = lax.fori_loop(0, ITERS, sweep, state)[0]
    upper = passed_along(latent[:, :1, :], "tile", -1)
    tall = jnp.concatenate([latent, upper], axis=1)
    beside = passed_along(tall[:, :, :1], "field", -1)
    wide = jnp.concatenate([tall, beside], axis=2)
    columns = latent.shape[2]
    width = columns + 1
    flat = wide.reshape(wide.shape[0], -1)
    base = (got_cells // columns * width + got_cells % columns).astype(jnp.int32)

    def corner(offset):
        return jnp.take(flat, base + offset, axis=1)

    row_frac = got_row[None]
    col_frac = got_col[None]
    predictor = (
        (1.0 - row_frac) * (1.0 - col_frac) * corner(0)
        + row_frac * (1.0 - col_frac) * corner(width)
        + (1.0 - row_frac) * col_frac * corner(1)
        + row_frac * col_frac * corner(width + 1)
    )
    return latent, jnp.transpose(predictor, (1, 0, 2)).reshape(-1, predictor.shape[2])


def turned(x, axis, by):
    size = lax.axis_size(axis)
    return lax.ppermute(x, axis, [(i, (i + by) % size) for i in range(size)])


def local(
    right_side,
    kappa_field,
    tau_field,
    curvature,
    detect_prob,
    site_cells,
    site_offsets,
    site_count,
    visit_count,
    detections,
    surveyed,
):
    rows, cols = right_side.shape[1:]
    wide = cols + LANES
    tiles, bands = lax.axis_size("tile"), lax.axis_size("field")
    tile, band = lax.axis_index("tile"), lax.axis_index("field")
    flags = jnp.stack([band > 0, band < bands - 1, tile > 0, tile < tiles - 1]).astype(jnp.float32)
    lane = lax.broadcasted_iota(jnp.int32, (F, LANES), 1)
    mask = jnp.where(lane < SIDE, flags[1], jnp.where(lane >= LANES - SIDE, flags[0], 0.0))

    fields = (right_side, kappa_field, tau_field, curvature)
    to_left, to_right = columns_of(fields)
    from_right = turned(to_left, "field", -1)
    from_left = turned(to_right, "field", 1)
    basis, kap, tau, cur, to_up, to_down = prepare(flags, fields, from_left, from_right)
    coefs = (kap, tau, cur)

    cells = site_cells[0, 0]
    sent = jnp.concatenate([cells.astype(jnp.float32)[:, None], site_offsets[0, 0]], axis=1)
    sums = []
    for p in range(ITERS // 2):
        from_down = turned(to_up, "tile", -1)
        from_up = turned(to_down, "tile", 1)
        if p == 0:
            sent, to_up = lax.optimization_barrier((sent, to_up))
            got = lax.all_to_all(sent, "tile", split_axis=0, concat_axis=0, tiled=True)
            got_cells = got[:, 0].astype(jnp.int32)
            got_row, got_col = got[:, 1], got[:, 2]
            hot = columns_hot(got_cells.reshape(1, -1), wide)
            flags, hot = lax.optimization_barrier((flags, hot))
        state = (p, rows, cols, flags, mask, basis, coefs, from_up, from_down)
        if p < ITERS // 2 - 1:
            basis, coefs, to_up, to_down, part = phase(*state)
            sums.append(part)
        else:
            basis, spread = phase(*state, earlier=sums, devices=tiles * bands)

    spread = lax.all_to_all(spread, ("tile", "field"), split_axis=0, concat_axis=0, tiled=True)
    line = jnp.sum(spread, axis=0)
    latent, predictor, fine = finish(
        rows, cols, line, basis, hot, got_cells.reshape(1, -1), got_row.reshape(1, -1), got_col.reshape(1, -1)
    )
    latent, predictor, _ = lax.while_loop(
        lambda state: state[2],
        lambda state: plain(*fields, got_cells, got_row, got_col) + (False,),
        (latent, predictor, jnp.logical_not(jnp.all(fine > 0.5))),
    )
    predictor = predictor.reshape(tiles, F, LANES)
    returned = lax.all_to_all(predictor, "tile", split_axis=0, concat_axis=0, tiled=True)

    slots = lax.broadcasted_iota(jnp.int32, cells.shape, 1)
    live = (slots < site_count[0, 0][:, None]).astype(jnp.float32)[:, None, :]
    visits = visit_count[0, 0].astype(jnp.float32)[:, None, :]
    miss_prob = jnp.exp(visits * jnp.log(1.0 - detect_prob)[:, None])
    expo = jnp.exp(returned)
    seen_grad = 1.0 / (1.0 + expo)
    miss_grad = -(1.0 - miss_prob) * expo / ((1.0 + expo) * (1.0 + miss_prob * expo))
    site_grad = (
        jnp.where(detections[0, 0] > 0, seen_grad, miss_grad)
        * surveyed[0, 0].astype(jnp.float32)
        * live
    )
    return (latent, site_grad[None, None])


def solution(mesh):
    in_specs = (
        P(None, "tile", "field"),
        P(None, "tile", "field"),
        P(None, "tile", "field"),
        P(None, "tile", "field"),
        P(),
        P("tile", "field", None, None),
        P("tile", "field", None, None, None),
        P("tile", "field", None),
        P("tile", "field", None, None),
        P("tile", "field", None, None, None),
        P("tile", "field", None, None, None),
    )
    out_specs = (P(None, "tile", "field"), P("tile", "field", None, None, None))
    return jax.shard_map(local, mesh=mesh, in_specs=in_specs, out_specs=out_specs, check_vma=False)
```

```python
import functools

import jax
import jax.numpy as jnp
from jax import lax
from jax.experimental import pallas as pl
from jax.experimental.pallas import tpu as pltpu
from jax.sharding import PartitionSpec as P

ITERS = 8
F = 8
PAD = 4
SKIP = PAD - 1
SIDE = 16
LANES = 128
LOW, HIGH = 0.2, 15.0
MID, HALF = 0.5 * (HIGH + LOW), 0.5 * (HIGH - LOW)
VMEM = pl.BlockSpec(memory_space=pltpu.VMEM)
SMEM = pl.BlockSpec(memory_space=pltpu.SMEM)
PARAMS = pltpu.CompilerParams(vmem_limit_bytes=10 * 1024 * 1024)


def held(x):
    return pltpu.with_memory_space_constraint(x, pltpu.VMEM)


def columns_kernel(*refs):
    firsts, lasts, (to_left, to_right) = refs[0:4], refs[4:8], refs[8:]
    lane = lax.broadcasted_iota(jnp.int32, (16, F, LANES), 2)
    for out, blocks, start in ((to_left, firsts, 0), (to_right, lasts, LANES - SIDE)):
        packed = jnp.zeros((16, F, LANES), jnp.float32)
        for a, ref in enumerate(blocks):
            block = jnp.swapaxes(ref[...], 0, 1)
            shift = (SIDE * a - start) % LANES
            moved = pltpu.roll(block, shift, 2) if shift else block
            mine = (lane >= SIDE * a) & (lane < SIDE * (a + 1))
            packed = jnp.where(mine, moved, packed)
        out[...] = packed


def columns_of(fields):
    rows, cols = fields[0].shape[1:]
    first = pl.BlockSpec((F, rows, LANES), lambda i: (0, 0, 0))
    last = pl.BlockSpec((F, rows, LANES), lambda i: (0, 0, cols // LANES - 1))
    out = pl.BlockSpec((rows, F, LANES), lambda i: (0, 0, 0))
    shape = jax.ShapeDtypeStruct((rows, F, LANES), jnp.float32)
    return pl.pallas_call(
        columns_kernel,
        grid=(1,),
        in_specs=[first] * 4 + [last] * 4,
        out_specs=[out, out],
        out_shape=[shape, shape],
        name="columns",
    )(*fields, *fields)


DEPTHS = (4, 3, 3, 2)


def shaped(a, x):
    if a == 1:
        return x + 4.0
    if a == 2:
        return x * (1.0 / HALF)
    if a == 3:
        return (x - MID) * (1.0 / HALF)
    return x


def place(a, at, block, outs, to_up, to_down):
    rows = block.shape[0]
    outs[a][PAD : PAD + rows, :, at] = block
    base, depth = sum(DEPTHS[:a]), DEPTHS[a]
    to_up[base : base + depth, :, at] = block[:depth]
    to_down[base : base + depth, :, at] = block[rows - depth :]


def prepare_kernel(cols, *refs):
    fields, outs, (to_up, to_down) = refs[0:4], refs[4:8], refs[8:]

    def step(c, carry):
        at = pl.ds(pl.multiple_of(c * LANES, LANES), LANES)
        for a in range(4):
            place(a, at, shaped(a, jnp.swapaxes(fields[a][:, :, at], 0, 1)), outs, to_up, to_down)
        return carry

    lax.fori_loop(0, cols // LANES, step, 0)


def prepare(fields):
    rows, cols = fields[0].shape[1:]
    wide = cols + LANES
    f32 = jnp.float32
    ext = pltpu.VMEM((rows + 2 * PAD, F, wide), f32)
    packed = pltpu.VMEM((sum(DEPTHS), F, wide), f32)
    return pl.pallas_call(
        functools.partial(prepare_kernel, cols),
        in_specs=[VMEM] * 4,
        out_specs=[VMEM] * 6,
        out_shape=[ext] * 4 + [packed] * 2,
        compiler_params=PARAMS,
        name="prepare",
    )(*fields)


def sides_kernel(rows, cols, flags, left, right, *refs):
    outs, (to_up, to_down) = refs[6:10], refs[10:]
    lane = lax.broadcasted_iota(jnp.int32, (rows, F, LANES), 2)
    for a in range(4):
        shift = (-SIDE * a) % LANES
        after = shaped(a, pltpu.roll(right[...], shift, 2) if shift else right[...])
        before = shaped(a, pltpu.roll(left[...], LANES - SIDE * (a + 1), 2))
        extra = jnp.where(lane < SIDE, after * flags[1], 0.0) + jnp.where(lane >= LANES - SIDE, before * flags[0], 0.0)
        place(a, pl.ds(cols, LANES), extra, outs, to_up, to_down)


def sides(rows, cols, flags, left, right, prepared):
    return pl.pallas_call(
        functools.partial(sides_kernel, rows, cols),
        in_specs=[SMEM] + [VMEM] * 8,
        out_specs=[VMEM] * 6,
        out_shape=[pltpu.VMEM(x.shape, x.dtype) for x in prepared],
        input_output_aliases={3 + i: i for i in range(6)},
        compiler_params=PARAMS,
        name="sides",
    )(flags, left, right, *[held(x) for x in prepared])


def walk(ref, r, count, wide):
    tiles = wide // LANES
    lane = lax.broadcasted_iota(jnp.int32, (F, LANES), 1)
    leftmost, rightmost = lane == 0, lane == LANES - 1

    def load(c):
        return [ref[r - 1 + i, :, c * LANES : (c + 1) * LANES] for i in range(count + 2)]

    def turn(tile, by):
        return [pltpu.roll(v, by, 1) for v in tile[1:-1]]

    now = load(0)
    before = turn([ref[r - 1 + i, :, wide - LANES :] for i in range(count + 2)], 1)
    right, left = turn(now, 1), turn(now, LANES - 1)
    start = left
    for c in range(tiles):
        after = load(c + 1) if c + 1 < tiles else None
        following = turn(after, LANES - 1) if after else start
        near = [
            (now[i] + now[i + 2])
            + (jnp.where(leftmost, before[i], right[i]) + jnp.where(rightmost, following[i], left[i]))
            for i in range(count)
        ]
        yield slice(c * LANES, (c + 1) * LANES), now[1:-1], near
        if after:
            before, right, left, now = right, turn(after, 1), following, after


def pairs(low, high, body, carry):
    return lax.fori_loop(0, (high - low) // 2, lambda i, carry: body(low + 2 * i, carry), carry, unroll=True)


def phase_kernel(p, rows, cols, *refs):
    first, last = p == 0, p == ITERS // 2 - 1
    refs = list(refs)
    take = lambda n: [refs.pop(0) for _ in range(n)]
    flags, mask, current, kap, tau, cur, up, down = take(8)
    if not first:
        older, old = take(2)
    if last:
        earlier = take(ITERS // 2 - 1)
    (current,) = take(1)
    if first:
        kap, tau, cur = take(3)
    (middle,) = take(1)
    if last:
        line, scaled, one = refs
    else:
        newest, to_up, to_down, sums, scaled, one = refs
    wide = cols + LANES
    own_low, own_high = PAD, PAD + rows

    for source, flag, begin in ((up, 2, None), (down, 3, own_high)):
        base = 0
        for a, depth in enumerate(DEPTHS if first else (PAD,)):
            at = PAD - depth if begin is None else begin
            for i in range(depth):
                row = source[base + i] * flags[flag]
                (current, kap, tau, cur)[a][at + i] = row
            base += depth

    zero = jnp.zeros((F, LANES), jnp.float32)

    def scale(ref, low, high):
        def body(r, carry):
            for at, v, near in walk(ref, r, 2, wide):
                for i in range(2):
                    scaled[r + i, :, at] = tau[r + i, :, at] * (kap[r + i, :, at] * v[i] - near[i])
            return carry

        pairs(low, high, body, 0)

    def image(ref, r):
        for at, s, near in walk(scaled, r, 2, wide):
            out = []
            for i in range(2):
                new = (kap[r + i, :, at] * s[i] - near[i]) + cur[r + i, :, at] * ref[r + i, :, at]
                out.append(new * mask[...] if at.start == cols else new)
            yield at, out

    scale(current, own_low - 3, own_high + 3)
    for r, flag, inner in ((own_low - 2, flags[2], 1), (own_high, flags[3], 0)):
        for at, new in image(current, r):
            for i in range(2):
                value = new[i] * flag
                one[r + i, :, at] = value
                if i == inner:
                    middle[r + i - SKIP, :, at] = value if first else 2.0 * value - old[r + i - SKIP, :, at]

    def first_rows(r, carry):
        cross = square = start = zero
        for at, new in image(current, r):
            for i in range(2):
                one[r + i, :, at] = new[i]
                value = new[i] if first else 2.0 * new[i] - old[r + i - SKIP, :, at]
                middle[r + i - SKIP, :, at] = value
                if at.start < cols:
                    source = current[r + i, :, at]
                    cross += value * source
                    square += value * value
                    if first:
                        start += source * source
        out = (carry[0] + cross, carry[1] + square)
        return out + ((carry[2] + start,) if first else ())

    found = pairs(own_low, own_high, first_rows, (zero,) * (3 if first else 2))

    if last:

        def final_rows(r, carry):
            total = zero
            for at, v, near in walk(middle, r - SKIP, 2, wide):
                if at.start < cols:
                    for i in range(2):
                        k = kap[r + i, :, at] * v[i] - near[i]
                        total += tau[r + i, :, at] * k * k + cur[r + i, :, at] * v[i] * v[i]
            return carry + total

        found += (pairs(own_low, own_high, final_rows, zero),)
        entries = [earlier[0][4]]
        for s in earlier:
            entries += [s[i] for i in range(4)]
        lane = lax.broadcasted_iota(jnp.int32, (F, LANES), 1)
        table = zero
        for k, entry in enumerate(entries + list(found)):
            table = jnp.where(lane == k, jnp.sum(entry, axis=1, keepdims=True), table)
        total = table[0:1]
        for f in range(1, F):
            total = total + pltpu.roll(table[f : f + 1], 2 * ITERS * f, 1)
        line[...] = jnp.broadcast_to(total[None], line.shape)
        return

    sums[0] = found[0]
    sums[1] = found[1]
    if first:
        sums[4] = found[2]

    scale(one, own_low - 1, own_high + 1)

    def second_rows(r, carry):
        cross = square = zero
        for at, new in image(one, r):
            for i in range(2):
                value = 2.0 * new[i] - current[r + i, :, at]
                if not first:
                    value = 2.0 * value - older[r + i, :, at]
                newest[r + i, :, at] = value
                if at.start < cols:
                    cross += value * middle[r + i - SKIP, :, at]
                    square += value * value
        return carry[0] + cross, carry[1] + square

    sums[2], sums[3] = pairs(own_low, own_high, second_rows, (zero, zero))
    to_up[...] = newest[own_low : own_low + PAD]
    to_down[...] = newest[own_high - PAD : own_high]


def phase(p, rows, cols, flags, mask, basis, coefs, up, down, earlier=(), devices=1):
    first, last = p == 0, p == ITERS // 2 - 1
    f32 = jnp.float32
    wide = cols + LANES
    ext = (rows + 2 * PAD, F, wide)
    out_shape = [pltpu.VMEM(ext, f32)]
    aliases = {2: 0}
    if first:
        out_shape += [pltpu.VMEM(ext, f32)] * 3
        aliases.update({3: 1, 4: 2, 5: 3})
    out_shape += [pltpu.VMEM((rows + 2, F, wide), f32)]
    if last:
        out_shape += [jax.ShapeDtypeStruct((devices, 1, LANES), f32)]
    else:
        out_shape += [pltpu.VMEM(ext, f32)]
        out_shape += [pltpu.VMEM((PAD, F, wide), f32)] * 2
        out_shape += [jax.ShapeDtypeStruct((5 if first else 4, F, LANES), f32)]
    older = [] if first else [held(basis[-3]), held(basis[-2])]
    outs = pl.pallas_call(
        functools.partial(phase_kernel, p, rows, cols),
        in_specs=[SMEM] + [VMEM] * (7 + len(older) + len(earlier)),
        out_specs=[VMEM] * len(out_shape),
        out_shape=out_shape,
        scratch_shapes=[pltpu.VMEM(ext, f32), pltpu.VMEM(ext, f32)],
        input_output_aliases=aliases,
        compiler_params=PARAMS,
        name=f"phase{p}",
    )(flags, mask, held(basis[-1]), *[held(c) for c in coefs], held(up), held(down), *older, *earlier)
    current, outs = outs[0], list(outs[1:])
    if first:
        coefs, outs = outs[:3], outs[3:]
    basis = basis[:-1] + [current, outs[0]]
    if last:
        return basis, outs[1]
    return basis + [outs[1]], coefs, outs[2], outs[3], outs[4]


def coefficients(line):
    raw = [jnp.sum(jnp.where(lax.broadcasted_iota(jnp.int32, (F, LANES), 1)
                             == 2 * ITERS * lax.broadcasted_iota(jnp.int32, (F, LANES), 0) + k,
                             jnp.broadcast_to(line, (F, LANES)), 0.0), axis=1, keepdims=True)
           for k in range(2 * ITERS)]
    raw = [jnp.broadcast_to(v, (F, LANES)) for v in raw]
    m = [raw[0], raw[1]] + [2.0 * raw[k] - raw[k % 2] for k in range(2, 2 * ITERS - 1)]
    m.append(4.0 * raw[2 * ITERS - 1] - m[2 * ITERS - 3] - 2.0 * m[1])
    zero = jnp.zeros((F, LANES), jnp.float32)
    one = jnp.ones((F, LANES), jnp.float32)

    def moved(v):
        out = [MID * e for e in v] + [zero]
        out[1] = out[1] + HALF * v[0]
        for k in range(1, len(v)):
            out[k - 1] = out[k - 1] + 0.5 * HALF * v[k]
            out[k + 1] = out[k + 1] + 0.5 * HALF * v[k]
        return out

    def against(v, l):
        return MID * v[l] + 0.5 * HALF * (v[l + 1] + v[abs(l - 1)])

    res, way = list(m), list(m)
    res_in, way_in, lat_in = [one], [one], [zero] * ITERS
    lead = one
    now = m[0]
    pivots = []
    for it in range(ITERS):
        image = [against(way, l) for l in range(len(way) - 1)]
        alpha = now / (lead * image[it])
        for k in range(it + 1):
            lat_in[k] = lat_in[k] + alpha * way_in[k]
        if it == ITERS - 1:
            break
        res = [res[l] - alpha * image[l] for l in range(len(image))]
        step = moved(way_in)
        res_in = [a - alpha * b for a, b in zip(res_in + [zero], step)]
        lead = res_in[it + 1]
        new = lead * res[it + 1]
        pivots.append(res[it + 1] / (lead * m[0]))
        beta = new / now
        way = [res[l] + beta * way[l] for l in range(len(res))]
        way_in = [a + beta * b for a, b in zip(res_in, way_in + [zero])]
        now = new
    fine = pivots[-1] >= 0.3 * pivots[0]
    for pivot in pivots:
        fine = fine & (pivot >= 5e-3) & (pivot <= 20.0)
    return lat_in, fine


CHUNK = 4 * LANES


def columns_hot_kernel(cols, cells, hot):
    col = lax.rem(cells[...], cols)

    def step(b, carry):
        at = pl.ds(pl.multiple_of(b * LANES, LANES), LANES)
        row = lax.broadcasted_iota(jnp.int32, (LANES, CHUNK), 0) + b * LANES
        hot[0, at] = jnp.where(row == col, 1.0, 0.0).astype(jnp.bfloat16)
        return carry

    lax.fori_loop(0, hot.shape[1] // LANES, step, 0)


def columns_hot(cells, cols):
    chunks, wide = cells.shape[1] // CHUNK, cols + LANES
    return pl.pallas_call(
        functools.partial(columns_hot_kernel, cols),
        grid=(chunks,),
        in_specs=[pl.BlockSpec((1, CHUNK), lambda i: (0, i))],
        out_specs=pl.BlockSpec((1, wide, CHUNK), lambda i: (i, 0, 0)),
        out_shape=pltpu.HBM((chunks, wide, CHUNK), jnp.bfloat16),
        compiler_params=PARAMS,
        name="columns_hot",
    )(cells)


def finish_kernel(rows, cols, line, hot, cells, row_frac, col_frac, *refs):
    basis, refs = refs[:ITERS], refs[ITERS:]
    latent, predictor, fine, parts, keep, held_hot, arrived = refs
    wide = cols + LANES
    chunks = hot.shape[0]
    copies = [pltpu.make_async_copy(hot.at[i], held_hot.at[i], arrived.at[i]) for i in range(chunks)]
    for copy in copies:
        copy.start()
    lat_in, good = coefficients(line[...])
    fine[...] = jnp.where(good, 1.0, 0.0)
    for k in range(ITERS):
        keep[k] = lat_in[k]
    lane = lax.broadcasted_iota(jnp.int32, (rows + 1, F, LANES), 2)
    tall = (rows + 1) * F

    def split(x, at, base):
        part = x.astype(jnp.bfloat16)
        rest = (x - part.astype(jnp.float32)).astype(jnp.bfloat16)
        parts[base : base + tall, at] = part.reshape(tall, LANES)
        parts[base + tall : base + 2 * tall, at] = rest.reshape(tall, LANES)

    def step(c, after):
        c = wide // LANES - 1 - c
        at = pl.ds(pl.multiple_of(c * LANES, LANES), LANES)
        total = None
        for k in range(ITERS):
            begin = PAD - SKIP * (k % 2)
            term = keep[k] * basis[k][begin : begin + rows + 1, :, at]
            total = term if total is None else total + term
        turned = pltpu.roll(total, LANES - 1, 2)
        split(total, at, 0)
        split(jnp.where(lane == LANES - 1, after, turned), at, 2 * tall)

        @pl.when(c < cols // LANES)
        def _():
            latent[:, :, at] = jnp.swapaxes(total[:rows], 0, 1)

        return turned

    lax.fori_loop(0, wide // LANES, step, jnp.zeros((rows + 1, F, LANES), jnp.float32))
    for c in range(chunks):
        copies[c].wait()
        at = slice(c * CHUNK, (c + 1) * CHUNK)
        both = jnp.dot(parts[...], held_hot[c], preferred_element_type=jnp.float32)
        here = both[:tall] + both[tall : 2 * tall]
        beside = both[2 * tall : 3 * tall] + both[3 * tall :]
        row = cells[:, at] // cols
        frac = row_frac[:, at]
        low = jnp.zeros((F, CHUNK), jnp.float32)
        high = jnp.zeros((F, CHUNK), jnp.float32)
        for r in range(rows + 1):
            w = jnp.where(row == r, 1.0 - frac, jnp.where(row + 1 == r, frac, 0.0))
            low = low + w * here[r * F : (r + 1) * F]
            high = high + w * beside[r * F : (r + 1) * F]
        side = col_frac[:, at]
        out = (1.0 - side) * low + side * high
        for i in range(CHUNK // LANES):
            base = (c * CHUNK // LANES + i) * F
            predictor[base : base + F] = out[:, i * LANES : (i + 1) * LANES]


def finish(rows, cols, line, basis, hot, cells, row_frac, col_frac):
    f32 = jnp.float32
    wide = cols + LANES
    chunks = hot.shape[0]
    return pl.pallas_call(
        functools.partial(finish_kernel, rows, cols),
        in_specs=[VMEM, pl.BlockSpec(memory_space=pl.ANY)] + [VMEM] * (3 + ITERS),
        out_specs=[VMEM] * 3,
        out_shape=[
            jax.ShapeDtypeStruct((F, rows, cols), f32),
            jax.ShapeDtypeStruct((cells.shape[1] // LANES * F, LANES), f32),
            jax.ShapeDtypeStruct((F, LANES), f32),
        ],
        scratch_shapes=[
            pltpu.VMEM((4 * (rows + 1) * F, wide), jnp.bfloat16),
            pltpu.VMEM((ITERS, F, LANES), f32),
            pltpu.VMEM((chunks, wide, CHUNK), jnp.bfloat16),
            pltpu.SemaphoreType.DMA((chunks,)),
        ],
        compiler_params=pltpu.CompilerParams(vmem_limit_bytes=20 * 1024 * 1024),
        name="finish",
    )(line, pltpu.with_memory_space_constraint(hot, pltpu.HBM), cells, row_frac, col_frac, *[held(b) for b in basis])


def extended(x, sides, width):
    for axis, dim in sides:
        size, length = (lax.axis_size(axis), x.shape[dim])
        up = [(i, (i + 1) % size) for i in range(size - 1)]
        down = [(j, i) for i, j in up]
        last = lax.slice_in_dim(x, length - width, length, axis=dim)
        leading = lax.slice_in_dim(x, 0, width, axis=dim)
        before = lax.ppermute(last, axis, up)
        after = lax.ppermute(leading, axis, down)
        x = jnp.concatenate([before, x, after], axis=dim)
    return x


def passed_along(x, axis, by):
    length = lax.axis_size(axis)
    pairs = [(i, i + by) for i in range(length) if 0 <= i + by < length]
    return lax.ppermute(x, axis, pairs)


def neighbours(padded):
    return padded[:, 2:, 1:-1] + padded[:, :-2, 1:-1] + padded[:, 1:-1, 2:] + padded[:, 1:-1, :-2]


def plain(right_side, kappa_field, tau_field, curvature, got_cells, got_row, got_col):
    def squares(values):
        return lax.psum(jnp.sum(values * values, axis=(1, 2)), ("tile", "field"))[:, None, None]

    def sweep(_, state):
        latent, residual, direction, norm_now = state
        padded = extended(direction, (("tile", 1), ("field", 2)), 1)
        scaled = tau_field * ((kappa_field + 4.0) * direction - neighbours(padded))
        spread = extended(scaled, (("tile", 1), ("field", 2)), 1)
        image = (kappa_field + 4.0) * scaled - neighbours(spread) + curvature * direction
        inner = lax.psum(jnp.sum(direction * image, axis=(1, 2)), ("tile", "field"))[:, None, None]
        alpha = norm_now / inner
        latent = latent + alpha * direction
        residual = residual - alpha * image
        norm_next = squares(residual)
        direction = residual + norm_next / norm_now * direction
        return latent, residual, direction, norm_next

    state = (jnp.zeros_like(right_side), right_side, right_side, squares(right_side))
    latent = lax.fori_loop(0, ITERS, sweep, state)[0]
    upper = passed_along(latent[:, :1, :], "tile", -1)
    tall = jnp.concatenate([latent, upper], axis=1)
    beside = passed_along(tall[:, :, :1], "field", -1)
    wide = jnp.concatenate([tall, beside], axis=2)
    columns = latent.shape[2]
    width = columns + 1
    flat = wide.reshape(wide.shape[0], -1)
    base = (got_cells // columns * width + got_cells % columns).astype(jnp.int32)

    def corner(offset):
        return jnp.take(flat, base + offset, axis=1)

    row_frac = got_row[None]
    col_frac = got_col[None]
    predictor = (
        (1.0 - row_frac) * (1.0 - col_frac) * corner(0)
        + row_frac * (1.0 - col_frac) * corner(width)
        + (1.0 - row_frac) * col_frac * corner(1)
        + row_frac * col_frac * corner(width + 1)
    )
    return latent, jnp.transpose(predictor, (1, 0, 2)).reshape(-1, predictor.shape[2])


def turned(x, axis, by):
    size = lax.axis_size(axis)
    return lax.ppermute(x, axis, [(i, (i + by) % size) for i in range(size)])


def local(
    right_side,
    kappa_field,
    tau_field,
    curvature,
    detect_prob,
    site_cells,
    site_offsets,
    site_count,
    visit_count,
    detections,
    surveyed,
):
    rows, cols = right_side.shape[1:]
    wide = cols + LANES
    tiles, bands = lax.axis_size("tile"), lax.axis_size("field")
    tile, band = lax.axis_index("tile"), lax.axis_index("field")
    flags = jnp.stack([band > 0, band < bands - 1, tile > 0, tile < tiles - 1]).astype(jnp.float32)
    lane = lax.broadcasted_iota(jnp.int32, (F, LANES), 1)
    mask = jnp.where(lane < SIDE, flags[1], jnp.where(lane >= LANES - SIDE, flags[0], 0.0))

    fields = (right_side, kappa_field, tau_field, curvature)
    cells = site_cells[0, 0]
    sent = jnp.concatenate([cells.astype(jnp.float32)[:, None], site_offsets[0, 0]], axis=1)
    to_left, to_right = columns_of(fields)
    sent, to_left, to_right = lax.optimization_barrier((sent, to_left, to_right))
    from_right = turned(to_left, "field", -1)
    from_left = turned(to_right, "field", 1)
    got = lax.all_to_all(sent, "tile", split_axis=0, concat_axis=0, tiled=True)
    got_cells = got[:, 0].astype(jnp.int32)
    got_row, got_col = got[:, 1], got[:, 2]
    hot = columns_hot(got_cells.reshape(1, -1), cols)
    prepared = sides(rows, cols, flags, from_left, from_right, prepare(fields))
    basis, coefs, to_up, to_down = [prepared[0]], prepared[1:4], prepared[4], prepared[5]

    sums = []
    for p in range(ITERS // 2):
        from_down = turned(to_up, "tile", -1)
        from_up = turned(to_down, "tile", 1)
        if p == 0:
            flags, hot = lax.optimization_barrier((flags, hot))
        state = (p, rows, cols, flags, mask, basis, coefs, from_up, from_down)
        if p < ITERS // 2 - 1:
            basis, coefs, to_up, to_down, part = phase(*state)
            sums.append(part)
        else:
            basis, spread = phase(*state, earlier=sums, devices=tiles * bands)

    spread = lax.all_to_all(spread, ("tile", "field"), split_axis=0, concat_axis=0, tiled=True)
    line = jnp.sum(spread, axis=0)
    latent, predictor, fine = finish(
        rows, cols, line, basis, hot, got_cells.reshape(1, -1), got_row.reshape(1, -1), got_col.reshape(1, -1)
    )
    latent, predictor, _ = lax.while_loop(
        lambda state: state[2],
        lambda state: plain(*fields, got_cells, got_row, got_col) + (False,),
        (latent, predictor, jnp.logical_not(jnp.all(fine > 0.5))),
    )
    predictor = predictor.reshape(tiles, F, LANES)
    returned = lax.all_to_all(predictor, "tile", split_axis=0, concat_axis=0, tiled=True)

    slots = lax.broadcasted_iota(jnp.int32, cells.shape, 1)
    live = (slots < site_count[0, 0][:, None]).astype(jnp.float32)[:, None, :]
    visits = visit_count[0, 0].astype(jnp.float32)[:, None, :]
    miss_prob = jnp.exp(visits * jnp.log(1.0 - detect_prob)[:, None])
    expo = jnp.exp(returned)
    seen_grad = 1.0 / (1.0 + expo)
    miss_grad = -(1.0 - miss_prob) * expo / ((1.0 + expo) * (1.0 + miss_prob * expo))
    site_grad = (
        jnp.where(detections[0, 0] > 0, seen_grad, miss_grad)
        * surveyed[0, 0].astype(jnp.float32)
        * live
    )
    return (latent, site_grad[None, None])


def solution(mesh):
    in_specs = (
        P(None, "tile", "field"),
        P(None, "tile", "field"),
        P(None, "tile", "field"),
        P(None, "tile", "field"),
        P(),
        P("tile", "field", None, None),
        P("tile", "field", None, None, None),
        P("tile", "field", None),
        P("tile", "field", None, None),
        P("tile", "field", None, None, None),
        P("tile", "field", None, None, None),
    )
    out_specs = (P(None, "tile", "field"), P("tile", "field", None, None, None))
    return jax.shard_map(local, mesh=mesh, in_specs=in_specs, out_specs=out_specs, check_vma=False)
```

```python
import functools

import jax
import jax.numpy as jnp
from jax import lax
from jax.experimental import pallas as pl
from jax.experimental.pallas import tpu as pltpu
from jax.sharding import PartitionSpec as P

ITERS = 8
F = 8
PAD = 4
SKIP = PAD - 1
SIDE = 16
LANES = 128
LOW, HIGH = 0.2, 15.0
MID, HALF = 0.5 * (HIGH + LOW), 0.5 * (HIGH - LOW)
VMEM = pl.BlockSpec(memory_space=pltpu.VMEM)
SMEM = pl.BlockSpec(memory_space=pltpu.SMEM)
HBM = pl.BlockSpec(memory_space=pl.ANY)
PARAMS = pltpu.CompilerParams(vmem_limit_bytes=12 * 1024 * 1024)


def held(x):
    return pltpu.with_memory_space_constraint(x, pltpu.VMEM)


def columns_kernel(*refs):
    firsts, lasts, (to_left, to_right) = refs[0:4], refs[4:8], refs[8:]
    lane = lax.broadcasted_iota(jnp.int32, (16, F, LANES), 2)
    for out, blocks, start in ((to_left, firsts, 0), (to_right, lasts, LANES - SIDE)):
        packed = jnp.zeros((16, F, LANES), jnp.float32)
        for a, ref in enumerate(blocks):
            block = jnp.swapaxes(ref[...], 0, 1)
            shift = (SIDE * a - start) % LANES
            moved = pltpu.roll(block, shift, 2) if shift else block
            mine = (lane >= SIDE * a) & (lane < SIDE * (a + 1))
            packed = jnp.where(mine, moved, packed)
        out[...] = packed


def columns_of(fields):
    rows, cols = fields[0].shape[1:]
    first = pl.BlockSpec((F, rows, LANES), lambda i: (0, 0, 0))
    last = pl.BlockSpec((F, rows, LANES), lambda i: (0, 0, cols // LANES - 1))
    out = pl.BlockSpec((rows, F, LANES), lambda i: (0, 0, 0))
    shape = jax.ShapeDtypeStruct((rows, F, LANES), jnp.float32)
    return pl.pallas_call(
        columns_kernel,
        grid=(1,),
        in_specs=[first] * 4 + [last] * 4,
        out_specs=[out, out],
        out_shape=[shape, shape],
        name="columns",
    )(*fields, *fields)


DEPTHS = (4, 3, 3, 2)


def shaped(a, x):
    if a == 1:
        return x + 4.0
    if a == 2:
        return x * (1.0 / HALF)
    if a == 3:
        return (x - MID) * (1.0 / HALF)
    return x


def extra_tile(a, flags, left, right):
    lane = lax.broadcasted_iota(jnp.int32, left.shape, 2)
    shift = (-SIDE * a) % LANES
    after = shaped(a, pltpu.roll(right[...], shift, 2) if shift else right[...])
    before = shaped(a, pltpu.roll(left[...], LANES - SIDE * (a + 1), 2))
    return jnp.where(lane < SIDE, after * flags[1], 0.0) + jnp.where(lane >= LANES - SIDE, before * flags[0], 0.0)


def prepare_kernel(*refs):
    fields, outs, (top, bottom) = refs[0:4], refs[4:8], refs[8:]
    rows = fields[0].shape[1]
    for a in range(4):
        base, depth = sum(DEPTHS[:a]), DEPTHS[a]
        for c in range(0, fields[a].shape[2], LANES):
            at = slice(c, c + LANES)
            block = shaped(a, jnp.swapaxes(fields[a][:, :, at], 0, 1))
            outs[a][:, :, at] = block
            top[base : base + depth, :, at] = block[:depth]
            bottom[base : base + depth, :, at] = block[rows - depth :]


def prepare(fields):
    rows, cols = fields[0].shape[1:]
    f32 = jnp.float32
    step = 4 * LANES
    edge = sum(DEPTHS)
    return pl.pallas_call(
        prepare_kernel,
        grid=(cols // step,),
        in_specs=[pl.BlockSpec((F, rows, step), lambda i: (0, 0, i))] * 4,
        out_specs=[pl.BlockSpec((rows, F, step), lambda i: (0, 0, i))] * 4
        + [pl.BlockSpec((edge, F, step), lambda i: (0, 0, i))] * 2,
        out_shape=[jax.ShapeDtypeStruct((rows, F, cols), f32)] * 4
        + [jax.ShapeDtypeStruct((edge, F, cols), f32)] * 2,
        compiler_params=PARAMS,
        name="prepare",
    )(*fields)


def sides_kernel(flags, left, right, top, bottom, to_up, to_down):
    rows, cols = left.shape[0], top.shape[2]
    to_up[:, :, :cols] = top[...]
    to_down[:, :, :cols] = bottom[...]
    for a in range(4):
        base, depth = sum(DEPTHS[:a]), DEPTHS[a]
        extra = extra_tile(a, flags, left, right)
        to_up[base : base + depth, :, cols:] = extra[:depth]
        to_down[base : base + depth, :, cols:] = extra[rows - depth :]


def sides(flags, left, right, top, bottom):
    edge, _, cols = top.shape
    return pl.pallas_call(
        sides_kernel,
        in_specs=[SMEM] + [VMEM] * 4,
        out_specs=[VMEM] * 2,
        out_shape=[jax.ShapeDtypeStruct((edge, F, cols + LANES), jnp.float32)] * 2,
        compiler_params=PARAMS,
        name="sides",
    )(flags, left, right, top, bottom)


def walk(ref, r, count, wide):
    tiles = wide // LANES
    lane = lax.broadcasted_iota(jnp.int32, (F, LANES), 1)
    leftmost, rightmost = lane == 0, lane == LANES - 1

    def load(c):
        return [ref[r - 1 + i, :, c * LANES : (c + 1) * LANES] for i in range(count + 2)]

    def turn(tile, by):
        return [pltpu.roll(v, by, 1) for v in tile[1:-1]]

    now = load(0)
    before = turn([ref[r - 1 + i, :, wide - LANES :] for i in range(count + 2)], 1)
    right, left = turn(now, 1), turn(now, LANES - 1)
    start = left
    for c in range(tiles):
        after = load(c + 1) if c + 1 < tiles else None
        following = turn(after, LANES - 1) if after else start
        near = [
            (now[i] + now[i + 2])
            + (jnp.where(leftmost, before[i], right[i]) + jnp.where(rightmost, following[i], left[i]))
            for i in range(count)
        ]
        yield slice(c * LANES, (c + 1) * LANES), now[1:-1], near
        if after:
            before, right, left, now = right, turn(after, 1), following, after


def pairs(low, high, body, carry):
    return lax.fori_loop(0, (high - low) // 2, lambda i, carry: body(low + 2 * i, carry), carry, unroll=True)


def phase_kernel(p, rows, cols, *refs):
    first, last = p == 0, p == ITERS // 2 - 1
    refs = list(refs)
    take = lambda n: [refs.pop(0) for _ in range(n)]
    flags, mask, up, down = take(4)
    if first:
        left, right = take(2)
        mains = take(4)
    else:
        own, kap, tau, cur, older, old = take(6)
        begin = PAD if p == 1 else 0
    if last:
        earlier = take(ITERS // 2 - 1)
        saved, (line, current, middle) = take(3), take(3)
    elif first:
        saved, (kap, tau, cur, current, middle, newest, to_up, to_down, sums) = take(1), take(9)
    else:
        saved, (middle, newest, to_up, to_down, sums, current) = take(2), take(6)
    scaled, one, arrived = refs
    wide = cols + LANES
    own_low, own_high = PAD, PAD + rows

    work = (current, kap, tau, cur)
    if first:
        for a, source in enumerate(mains):
            work[a][own_low:own_high, :, :cols] = source[...]
            work[a][own_low:own_high, :, cols:] = extra_tile(a, flags, left, right)
    else:
        current[own_low:own_high] = own[...]
    base = 0
    for a, depth in enumerate(DEPTHS if first else (PAD,)):
        for i in range(depth):
            work[a][own_low - depth + i] = up[base + i] * flags[2]
            work[a][own_high + i] = down[base + i] * flags[3]
        base += depth

    def save(i, ref, low):
        copy = pltpu.make_async_copy(ref.at[low : low + rows + 1], saved[i], arrived.at[i])
        copy.start()
        return copy

    copies = [] if first else [save(0, old, 1)]
    copies.append(save(len(copies), current, own_low))

    zero = jnp.zeros((F, LANES), jnp.float32)

    def scale(ref, low, high):
        def body(r, carry):
            for at, v, near in walk(ref, r, 2, wide):
                for i in range(2):
                    scaled[r + i, :, at] = tau[r + i, :, at] * (kap[r + i, :, at] * v[i] - near[i])
            return carry

        pairs(low, high, body, 0)

    def image(ref, r):
        for at, s, near in walk(scaled, r, 2, wide):
            out = []
            for i in range(2):
                new = (kap[r + i, :, at] * s[i] - near[i]) + cur[r + i, :, at] * ref[r + i, :, at]
                out.append(new * mask[...] if at.start == cols else new)
            yield at, out

    scale(current, own_low - 3, own_high + 3)
    for r, flag, inner in ((own_low - 2, flags[2], 1), (own_high, flags[3], 0)):
        for at, new in image(current, r):
            for i in range(2):
                value = new[i] * flag
                one[r + i, :, at] = value
                if i == inner:
                    middle[r + i - SKIP, :, at] = value if first else 2.0 * value - old[r + i - SKIP, :, at]

    def first_rows(r, carry):
        cross = square = start = zero
        for at, new in image(current, r):
            for i in range(2):
                one[r + i, :, at] = new[i]
                value = new[i] if first else 2.0 * new[i] - old[r + i - SKIP, :, at]
                middle[r + i - SKIP, :, at] = value
                if at.start < cols:
                    source = current[r + i, :, at]
                    cross += value * source
                    square += value * value
                    if first:
                        start += source * source
        out = (carry[0] + cross, carry[1] + square)
        return out + ((carry[2] + start,) if first else ())

    found = pairs(own_low, own_high, first_rows, (zero,) * (3 if first else 2))

    if last:
        copies.append(save(2, middle, 1))

        def final_rows(r, carry):
            total = zero
            for at, v, near in walk(middle, r - SKIP, 2, wide):
                if at.start < cols:
                    for i in range(2):
                        k = kap[r + i, :, at] * v[i] - near[i]
                        total += tau[r + i, :, at] * k * k + cur[r + i, :, at] * v[i] * v[i]
            return carry + total

        found += (pairs(own_low, own_high, final_rows, zero),)
        entries = [earlier[0][4]]
        for s in earlier:
            entries += [s[i] for i in range(4)]
        lane = lax.broadcasted_iota(jnp.int32, (F, LANES), 1)
        table = zero
        for k, entry in enumerate(entries + list(found)):
            table = jnp.where(lane == k, jnp.sum(entry, axis=1, keepdims=True), table)
        total = table[0:1]
        for f in range(1, F):
            total = total + pltpu.roll(table[f : f + 1], 2 * ITERS * f, 1)
        line[...] = jnp.broadcast_to(total[None], line.shape)
        for copy in copies:
            copy.wait()
        return

    sums[0] = found[0]
    sums[1] = found[1]
    if first:
        sums[4] = found[2]

    scale(one, own_low - 1, own_high + 1)

    def second_rows(r, carry):
        cross = square = zero
        for at, new in image(one, r):
            for i in range(2):
                value = 2.0 * new[i] - current[r + i, :, at]
                if not first:
                    value = 2.0 * value - older[r + i - PAD + begin, :, at]
                newest[r + i - PAD, :, at] = value
                if at.start < cols:
                    cross += value * middle[r + i - SKIP, :, at]
                    square += value * value
        return carry[0] + cross, carry[1] + square

    sums[2], sums[3] = pairs(own_low, own_high, second_rows, (zero, zero))
    to_up[...] = newest[:PAD]
    to_down[...] = newest[rows - PAD :]
    for copy in copies:
        copy.wait()


def phase(p, rows, cols, flags, mask, up, down, state, earlier=(), devices=1):
    first, last = p == 0, p == ITERS // 2 - 1
    f32 = jnp.float32
    wide = cols + LANES
    ext, ring = (rows + 2 * PAD, F, wide), (rows + 2, F, wide)
    saved = 1 if first else 3 if last else 2
    out_shape = [pltpu.HBM((rows + 1, F, wide), f32)] * saved
    scratch = []
    if last:
        out_shape += [jax.ShapeDtypeStruct((devices, 1, LANES), f32)]
        scratch += [pltpu.VMEM(ext, f32), pltpu.VMEM(ring, f32)]
    else:
        if first:
            out_shape += [pltpu.VMEM(ext, f32)] * 4
        else:
            scratch += [pltpu.VMEM(ext, f32)]
        out_shape += [pltpu.VMEM(ring, f32), pltpu.VMEM((rows, F, wide), f32)]
        out_shape += [jax.ShapeDtypeStruct((PAD, F, wide), f32)] * 2
        out_shape += [jax.ShapeDtypeStruct((5 if first else 4, F, LANES), f32)]
    operands = list(state) if first else [held(x) for x in state]
    outs = pl.pallas_call(
        functools.partial(phase_kernel, p, rows, cols),
        in_specs=[SMEM] + [VMEM] * (3 + len(operands) + len(earlier)),
        out_specs=[HBM] * saved + [VMEM] * (len(out_shape) - saved),
        out_shape=out_shape,
        scratch_shapes=scratch + [pltpu.VMEM(ext, f32), pltpu.VMEM(ext, f32), pltpu.SemaphoreType.DMA((saved,))],
        compiler_params=PARAMS,
        name=f"phase{p}",
    )(flags, mask, up, down, *operands, *earlier)
    return list(outs[:saved]), list(outs[saved:])


def coefficients(line):
    raw = [jnp.sum(jnp.where(lax.broadcasted_iota(jnp.int32, (F, LANES), 1)
                             == 2 * ITERS * lax.broadcasted_iota(jnp.int32, (F, LANES), 0) + k,
                             jnp.broadcast_to(line, (F, LANES)), 0.0), axis=1, keepdims=True)
           for k in range(2 * ITERS)]
    raw = [jnp.broadcast_to(v, (F, LANES)) for v in raw]
    m = [raw[0], raw[1]] + [2.0 * raw[k] - raw[k % 2] for k in range(2, 2 * ITERS - 1)]
    m.append(4.0 * raw[2 * ITERS - 1] - m[2 * ITERS - 3] - 2.0 * m[1])
    zero = jnp.zeros((F, LANES), jnp.float32)
    one = jnp.ones((F, LANES), jnp.float32)

    def moved(v):
        out = [MID * e for e in v] + [zero]
        out[1] = out[1] + HALF * v[0]
        for k in range(1, len(v)):
            out[k - 1] = out[k - 1] + 0.5 * HALF * v[k]
            out[k + 1] = out[k + 1] + 0.5 * HALF * v[k]
        return out

    def against(v, l):
        return MID * v[l] + 0.5 * HALF * (v[l + 1] + v[abs(l - 1)])

    res, way = list(m), list(m)
    res_in, way_in, lat_in = [one], [one], [zero] * ITERS
    lead = one
    now = m[0]
    pivots = []
    for it in range(ITERS):
        image = [against(way, l) for l in range(len(way) - 1)]
        alpha = now / (lead * image[it])
        for k in range(it + 1):
            lat_in[k] = lat_in[k] + alpha * way_in[k]
        if it == ITERS - 1:
            break
        res = [res[l] - alpha * image[l] for l in range(len(image))]
        step = moved(way_in)
        res_in = [a - alpha * b for a, b in zip(res_in + [zero], step)]
        lead = res_in[it + 1]
        new = lead * res[it + 1]
        pivots.append(res[it + 1] / (lead * m[0]))
        beta = new / now
        way = [res[l] + beta * way[l] for l in range(len(res))]
        way_in = [a + beta * b for a, b in zip(res_in, way_in + [zero])]
        now = new
    fine = pivots[-1] >= 0.3 * pivots[0]
    for pivot in pivots:
        fine = fine & (pivot >= 5e-3) & (pivot <= 20.0)
    return lat_in, fine


CHUNK = 4 * LANES


def columns_hot_kernel(cols, cells, hot):
    col = lax.rem(cells[...], cols)

    def step(b, carry):
        at = pl.ds(pl.multiple_of(b * LANES, LANES), LANES)
        row = lax.broadcasted_iota(jnp.int32, (LANES, CHUNK), 0) + b * LANES
        hot[0, at] = jnp.where(row == col, 1.0, 0.0).astype(jnp.bfloat16)
        return carry

    lax.fori_loop(0, hot.shape[1] // LANES, step, 0)


def columns_hot(cells, cols):
    chunks, wide = cells.shape[1] // CHUNK, cols + LANES
    return pl.pallas_call(
        functools.partial(columns_hot_kernel, cols),
        grid=(chunks,),
        in_specs=[pl.BlockSpec((1, CHUNK), lambda i: (0, i))],
        out_specs=pl.BlockSpec((1, wide, CHUNK), lambda i: (i, 0, 0)),
        out_shape=pltpu.HBM((chunks, wide, CHUNK), jnp.bfloat16),
        compiler_params=PARAMS,
        name="columns_hot",
    )(cells)


def finish_kernel(rows, cols, line, cells, row_frac, col_frac, hot, *refs):
    basis, refs = refs[:ITERS], refs[ITERS:]
    latent, predictor, fine, parts, keep, vectors, held_hot, vectors_in, hot_in = refs
    wide = cols + LANES
    chunks = hot.shape[0]
    half = rows // 2
    bands = [(0, half), (half, half), (rows, 1)]
    copies = [
        [
            pltpu.make_async_copy(
                basis[k].at[low : low + count], vectors.at[k, low : low + count], vectors_in.at[b, k]
            )
            for k in range(ITERS)
        ]
        for b, (low, count) in enumerate(bands)
    ]
    hot_copies = [pltpu.make_async_copy(hot.at[i], held_hot.at[i], hot_in.at[i]) for i in range(chunks)]
    for band in copies:
        for copy in band:
            copy.start()
    for copy in hot_copies:
        copy.start()
    lat_in, good = coefficients(line[...])
    fine[...] = jnp.where(good, 1.0, 0.0)
    for k in range(ITERS):
        keep[k] = lat_in[k]
    tall = (rows + 2) * F

    for (low, count), band in zip(bands, copies):
        for copy in band:
            copy.wait()
        fill = count % 2
        lane = lax.broadcasted_iota(jnp.int32, (count + fill, F, LANES), 2)

        def split(x, at, base):
            part = x.astype(jnp.bfloat16)
            rest = (x - part.astype(jnp.float32)).astype(jnp.bfloat16)
            size = (count + fill) * F
            parts[base : base + size, at] = part.reshape(size, LANES)
            parts[base + tall : base + tall + size, at] = rest.reshape(size, LANES)

        def step(c, after):
            c = wide // LANES - 1 - c
            at = pl.ds(pl.multiple_of(c * LANES, LANES), LANES)
            total = keep[0] * vectors[0, low : low + count, :, at]
            for k in range(1, ITERS):
                total = total + keep[k] * vectors[k, low : low + count, :, at]
            if fill:
                total = jnp.concatenate([total, jnp.zeros_like(total)], axis=0)
            turned = pltpu.roll(total, LANES - 1, 2)
            split(total, at, low * F)
            split(jnp.where(lane == LANES - 1, after, turned), at, 2 * tall + low * F)
            if low < rows:

                @pl.when(c < cols // LANES)
                def _():
                    latent[:, low : low + count, at] = jnp.swapaxes(total, 0, 1)

            return turned

        lax.fori_loop(0, wide // LANES, step, jnp.zeros((count + fill, F, LANES), jnp.float32))
    for c in range(chunks):
        hot_copies[c].wait()
        at = slice(c * CHUNK, (c + 1) * CHUNK)
        both = jnp.dot(parts[...], held_hot[c], preferred_element_type=jnp.float32)
        here = both[:tall] + both[tall : 2 * tall]
        beside = both[2 * tall : 3 * tall] + both[3 * tall :]
        row = cells[:, at] // cols
        frac = row_frac[:, at]
        low = jnp.zeros((F, CHUNK), jnp.float32)
        high = jnp.zeros((F, CHUNK), jnp.float32)
        for r in range(rows + 1):
            w = jnp.where(row == r, 1.0 - frac, jnp.where(row + 1 == r, frac, 0.0))
            low = low + w * here[r * F : (r + 1) * F]
            high = high + w * beside[r * F : (r + 1) * F]
        side = col_frac[:, at]
        out = (1.0 - side) * low + side * high
        for i in range(CHUNK // LANES):
            base = (c * CHUNK // LANES + i) * F
            predictor[base : base + F] = out[:, i * LANES : (i + 1) * LANES]


def finish(rows, cols, line, cells, row_frac, col_frac, hot, basis):
    f32 = jnp.float32
    wide = cols + LANES
    chunks = hot.shape[0]
    return pl.pallas_call(
        functools.partial(finish_kernel, rows, cols),
        in_specs=[VMEM] * 4 + [HBM] * (1 + ITERS),
        out_specs=[VMEM] * 3,
        out_shape=[
            jax.ShapeDtypeStruct((F, rows, cols), f32),
            jax.ShapeDtypeStruct((cells.shape[1] // LANES * F, LANES), f32),
            jax.ShapeDtypeStruct((F, LANES), f32),
        ],
        scratch_shapes=[
            pltpu.VMEM((4 * (rows + 2) * F, wide), jnp.bfloat16),
            pltpu.VMEM((ITERS, F, LANES), f32),
            pltpu.VMEM((ITERS, rows + 1, F, wide), f32),
            pltpu.VMEM((chunks, wide, CHUNK), jnp.bfloat16),
            pltpu.SemaphoreType.DMA((3, ITERS)),
            pltpu.SemaphoreType.DMA((chunks,)),
        ],
        compiler_params=pltpu.CompilerParams(vmem_limit_bytes=32 * 1024 * 1024),
        name="finish",
    )(line, cells, row_frac, col_frac, *[pltpu.with_memory_space_constraint(x, pltpu.HBM) for x in (hot, *basis)])


def extended(x, sides, width):
    for axis, dim in sides:
        size, length = (lax.axis_size(axis), x.shape[dim])
        up = [(i, (i + 1) % size) for i in range(size - 1)]
        down = [(j, i) for i, j in up]
        last = lax.slice_in_dim(x, length - width, length, axis=dim)
        leading = lax.slice_in_dim(x, 0, width, axis=dim)
        before = lax.ppermute(last, axis, up)
        after = lax.ppermute(leading, axis, down)
        x = jnp.concatenate([before, x, after], axis=dim)
    return x


def passed_along(x, axis, by):
    length = lax.axis_size(axis)
    pairs = [(i, i + by) for i in range(length) if 0 <= i + by < length]
    return lax.ppermute(x, axis, pairs)


def neighbours(padded):
    return padded[:, 2:, 1:-1] + padded[:, :-2, 1:-1] + padded[:, 1:-1, 2:] + padded[:, 1:-1, :-2]


def plain(right_side, kappa_field, tau_field, curvature, got_cells, got_row, got_col):
    def squares(values):
        return lax.psum(jnp.sum(values * values, axis=(1, 2)), ("tile", "field"))[:, None, None]

    def sweep(_, state):
        latent, residual, direction, norm_now = state
        padded = extended(direction, (("tile", 1), ("field", 2)), 1)
        scaled = tau_field * ((kappa_field + 4.0) * direction - neighbours(padded))
        spread = extended(scaled, (("tile", 1), ("field", 2)), 1)
        image = (kappa_field + 4.0) * scaled - neighbours(spread) + curvature * direction
        inner = lax.psum(jnp.sum(direction * image, axis=(1, 2)), ("tile", "field"))[:, None, None]
        alpha = norm_now / inner
        latent = latent + alpha * direction
        residual = residual - alpha * image
        norm_next = squares(residual)
        direction = residual + norm_next / norm_now * direction
        return latent, residual, direction, norm_next

    state = (jnp.zeros_like(right_side), right_side, right_side, squares(right_side))
    latent = lax.fori_loop(0, ITERS, sweep, state)[0]
    upper = passed_along(latent[:, :1, :], "tile", -1)
    tall = jnp.concatenate([latent, upper], axis=1)
    beside = passed_along(tall[:, :, :1], "field", -1)
    wide = jnp.concatenate([tall, beside], axis=2)
    columns = latent.shape[2]
    width = columns + 1
    flat = wide.reshape(wide.shape[0], -1)
    base = (got_cells // columns * width + got_cells % columns).astype(jnp.int32)

    def corner(offset):
        return jnp.take(flat, base + offset, axis=1)

    row_frac = got_row[None]
    col_frac = got_col[None]
    predictor = (
        (1.0 - row_frac) * (1.0 - col_frac) * corner(0)
        + row_frac * (1.0 - col_frac) * corner(width)
        + (1.0 - row_frac) * col_frac * corner(1)
        + row_frac * col_frac * corner(width + 1)
    )
    return latent, jnp.transpose(predictor, (1, 0, 2)).reshape(-1, predictor.shape[2])


def turned(x, axis, by):
    size = lax.axis_size(axis)
    return lax.ppermute(x, axis, [(i, (i + by) % size) for i in range(size)])


def local(
    right_side,
    kappa_field,
    tau_field,
    curvature,
    detect_prob,
    site_cells,
    site_offsets,
    site_count,
    visit_count,
    detections,
    surveyed,
):
    rows, cols = right_side.shape[1:]
    wide = cols + LANES
    tiles, bands = lax.axis_size("tile"), lax.axis_size("field")
    tile, band = lax.axis_index("tile"), lax.axis_index("field")
    flags = jnp.stack([band > 0, band < bands - 1, tile > 0, tile < tiles - 1]).astype(jnp.float32)
    lane = lax.broadcasted_iota(jnp.int32, (F, LANES), 1)
    mask = jnp.where(lane < SIDE, flags[1], jnp.where(lane >= LANES - SIDE, flags[0], 0.0))

    fields = (right_side, kappa_field, tau_field, curvature)
    to_left, to_right = columns_of(fields)
    from_right = turned(to_left, "field", -1)
    from_left = turned(to_right, "field", 1)
    *mains, top, bottom = prepare(fields)
    to_up, to_down = sides(flags, from_left, from_right, top, bottom)

    cells = site_cells[0, 0]
    sent = jnp.concatenate([cells.astype(jnp.float32)[:, None], site_offsets[0, 0]], axis=1)
    sent, to_up, to_down = lax.optimization_barrier((sent, to_up, to_down))
    got = lax.all_to_all(sent, "tile", split_axis=0, concat_axis=0, tiled=True)
    got_cells = got[:, 0].astype(jnp.int32)
    got_row, got_col = got[:, 1], got[:, 2]
    sites = (got_cells.reshape(1, -1), got_row.reshape(1, -1), got_col.reshape(1, -1))

    common = (rows, cols, flags, mask)

    def exchanged(to_up, to_down):
        return turned(to_down, "tile", 1), turned(to_up, "tile", -1)

    up, down = exchanged(to_up, to_down)
    basis, outs = phase(0, *common, up, down, (from_left, from_right, *mains))
    *coefs, older, old, own, to_up, to_down, part = outs
    sums = [part]
    for p in range(1, ITERS // 2 - 1):
        up, down = exchanged(to_up, to_down)
        if p == 1:
            hot = columns_hot(sites[0], cols)
            mask, hot = lax.optimization_barrier((mask, hot))
            common = (rows, cols, flags, mask)
        saved, (old, newest, to_up, to_down, part) = phase(p, *common, up, down, (own, *coefs, older, old))
        older, own = own, newest
        basis += saved
        sums.append(part)
    up, down = exchanged(to_up, to_down)
    saved, (spread,) = phase(
        ITERS // 2 - 1, *common, up, down, (own, *coefs, older, old), earlier=sums, devices=tiles * bands
    )
    basis += saved

    spread = lax.all_to_all(spread, ("tile", "field"), split_axis=0, concat_axis=0, tiled=True)
    line = jnp.sum(spread, axis=0)
    latent, predictor, fine = finish(rows, cols, line, *sites, hot, basis)
    latent, predictor, _ = lax.while_loop(
        lambda state: state[2],
        lambda state: plain(*fields, got_cells, got_row, got_col) + (False,),
        (latent, predictor, jnp.logical_not(jnp.all(fine > 0.5))),
    )
    predictor = predictor.reshape(tiles, F, LANES)
    returned = lax.all_to_all(predictor, "tile", split_axis=0, concat_axis=0, tiled=True)

    slots = lax.broadcasted_iota(jnp.int32, cells.shape, 1)
    live = (slots < site_count[0, 0][:, None]).astype(jnp.float32)[:, None, :]
    visits = visit_count[0, 0].astype(jnp.float32)[:, None, :]
    miss_prob = jnp.exp(visits * jnp.log(1.0 - detect_prob)[:, None])
    expo = jnp.exp(returned)
    seen_grad = 1.0 / (1.0 + expo)
    miss_grad = -(1.0 - miss_prob) * expo / ((1.0 + expo) * (1.0 + miss_prob * expo))
    site_grad = (
        jnp.where(detections[0, 0] > 0, seen_grad, miss_grad)
        * surveyed[0, 0].astype(jnp.float32)
        * live
    )
    return (latent, site_grad[None, None])


def solution(mesh):
    in_specs = (
        P(None, "tile", "field"),
        P(None, "tile", "field"),
        P(None, "tile", "field"),
        P(None, "tile", "field"),
        P(),
        P("tile", "field", None, None),
        P("tile", "field", None, None, None),
        P("tile", "field", None),
        P("tile", "field", None, None),
        P("tile", "field", None, None, None),
        P("tile", "field", None, None, None),
    )
    out_specs = (P(None, "tile", "field"), P("tile", "field", None, None, None))
    return jax.shard_map(local, mesh=mesh, in_specs=in_specs, out_specs=out_specs, check_vma=False)
```

```python
import functools

import jax
import jax.numpy as jnp
from jax import lax
from jax.experimental import pallas as pl
from jax.experimental.pallas import tpu as pltpu
from jax.sharding import PartitionSpec as P

ITERS = 8
F = 8
PAD = 4
SKIP = PAD - 1
SIDE = 16
LANES = 128
LOW, HIGH = 0.2, 15.0
MID, HALF = 0.5 * (HIGH + LOW), 0.5 * (HIGH - LOW)
VMEM = pl.BlockSpec(memory_space=pltpu.VMEM)
SMEM = pl.BlockSpec(memory_space=pltpu.SMEM)
HBM = pl.BlockSpec(memory_space=pl.ANY)
PARAMS = pltpu.CompilerParams(vmem_limit_bytes=12 * 1024 * 1024)


def held(x):
    return pltpu.with_memory_space_constraint(x, pltpu.VMEM)


def columns_kernel(*refs):
    firsts, lasts, (to_left, to_right) = refs[0:4], refs[4:8], refs[8:]
    lane = lax.broadcasted_iota(jnp.int32, (16, F, LANES), 2)
    for out, blocks, start in ((to_left, firsts, 0), (to_right, lasts, LANES - SIDE)):
        packed = jnp.zeros((16, F, LANES), jnp.float32)
        for a, ref in enumerate(blocks):
            block = jnp.swapaxes(ref[...], 0, 1)
            shift = (SIDE * a - start) % LANES
            moved = pltpu.roll(block, shift, 2) if shift else block
            mine = (lane >= SIDE * a) & (lane < SIDE * (a + 1))
            packed = jnp.where(mine, moved, packed)
        out[...] = packed


def columns_of(fields):
    rows, cols = fields[0].shape[1:]
    first = pl.BlockSpec((F, rows, LANES), lambda i: (0, 0, 0))
    last = pl.BlockSpec((F, rows, LANES), lambda i: (0, 0, cols // LANES - 1))
    out = pl.BlockSpec((rows, F, LANES), lambda i: (0, 0, 0))
    shape = jax.ShapeDtypeStruct((rows, F, LANES), jnp.float32)
    return pl.pallas_call(
        columns_kernel,
        grid=(1,),
        in_specs=[first] * 4 + [last] * 4,
        out_specs=[out, out],
        out_shape=[shape, shape],
        name="columns",
    )(*fields, *fields)


DEPTHS = (4, 3, 3, 2)


def shaped(a, x):
    if a == 1:
        return x + 4.0
    if a == 2:
        return x * (1.0 / HALF)
    if a == 3:
        return (x - MID) * (1.0 / HALF)
    return x


def extra_tile(a, flags, left, right):
    lane = lax.broadcasted_iota(jnp.int32, left.shape, 2)
    shift = (-SIDE * a) % LANES
    after = shaped(a, pltpu.roll(right[...], shift, 2) if shift else right[...])
    before = shaped(a, pltpu.roll(left[...], LANES - SIDE * (a + 1), 2))
    return jnp.where(lane < SIDE, after * flags[1], 0.0) + jnp.where(lane >= LANES - SIDE, before * flags[0], 0.0)


def prepare_kernel(*refs):
    fields, outs, (top, bottom) = refs[0:4], refs[4:8], refs[8:]
    rows = fields[0].shape[1]
    for a in range(4):
        base, depth = sum(DEPTHS[:a]), DEPTHS[a]
        for c in range(0, fields[a].shape[2], LANES):
            at = slice(c, c + LANES)
            block = shaped(a, jnp.swapaxes(fields[a][:, :, at], 0, 1))
            outs[a][:, :, at] = block
            top[base : base + depth, :, at] = block[:depth]
            bottom[base : base + depth, :, at] = block[rows - depth :]


def prepare(fields):
    rows, cols = fields[0].shape[1:]
    f32 = jnp.float32
    step = 4 * LANES
    edge = sum(DEPTHS)
    return pl.pallas_call(
        prepare_kernel,
        grid=(cols // step,),
        in_specs=[pl.BlockSpec((F, rows, step), lambda i: (0, 0, i))] * 4,
        out_specs=[pl.BlockSpec((rows, F, step), lambda i: (0, 0, i))] * 4
        + [pl.BlockSpec((edge, F, step), lambda i: (0, 0, i))] * 2,
        out_shape=[pltpu.HBM((rows, F, cols), f32)] * 4 + [pltpu.HBM((edge, F, cols), f32)] * 2,
        compiler_params=PARAMS,
        name="prepare",
    )(*fields)


def sides_kernel(flags, left, right, top, bottom, to_up, to_down):
    rows, cols = left.shape[0], top.shape[2]
    to_up[:, :, :cols] = top[...]
    to_down[:, :, :cols] = bottom[...]
    for a in range(4):
        base, depth = sum(DEPTHS[:a]), DEPTHS[a]
        extra = extra_tile(a, flags, left, right)
        to_up[base : base + depth, :, cols:] = extra[:depth]
        to_down[base : base + depth, :, cols:] = extra[rows - depth :]


def sides(flags, left, right, top, bottom):
    edge, _, cols = top.shape
    return pl.pallas_call(
        sides_kernel,
        in_specs=[SMEM] + [VMEM] * 4,
        out_specs=[VMEM] * 2,
        out_shape=[jax.ShapeDtypeStruct((edge, F, cols + LANES), jnp.float32)] * 2,
        compiler_params=PARAMS,
        name="sides",
    )(flags, left, right, top, bottom)


def walk(ref, r, count, wide):
    tiles = wide // LANES
    lane = lax.broadcasted_iota(jnp.int32, (F, LANES), 1)
    leftmost, rightmost = lane == 0, lane == LANES - 1

    def load(c):
        return [ref[r - 1 + i, :, c * LANES : (c + 1) * LANES] for i in range(count + 2)]

    def turn(tile, by):
        return [pltpu.roll(v, by, 1) for v in tile[1:-1]]

    now = load(0)
    before = turn([ref[r - 1 + i, :, wide - LANES :] for i in range(count + 2)], 1)
    right, left = turn(now, 1), turn(now, LANES - 1)
    start = left
    for c in range(tiles):
        after = load(c + 1) if c + 1 < tiles else None
        following = turn(after, LANES - 1) if after else start
        near = [
            (now[i] + now[i + 2])
            + (jnp.where(leftmost, before[i], right[i]) + jnp.where(rightmost, following[i], left[i]))
            for i in range(count)
        ]
        yield slice(c * LANES, (c + 1) * LANES), now[1:-1], near
        if after:
            before, right, left, now = right, turn(after, 1), following, after


def pairs(low, high, body, carry):
    return lax.fori_loop(0, (high - low) // 2, lambda i, carry: body(low + 2 * i, carry), carry, unroll=True)


def phase_kernel(p, rows, cols, *refs):
    first, last = p == 0, p == ITERS // 2 - 1
    refs = list(refs)
    take = lambda n: [refs.pop(0) for _ in range(n)]
    flags, mask, up, down = take(4)
    if first:
        left, right = take(2)
        mains = take(4)
    else:
        own, kap, tau, cur, older, old = take(6)
    if last:
        earlier = take(ITERS // 2 - 1)
        line, current, middle = take(3)
    elif first:
        kap, tau, cur, current, middle, newest, to_up, to_down, sums = take(9)
    else:
        current, middle, newest, to_up, to_down, sums = take(6)
    scaled, one = refs
    wide = cols + LANES
    own_low, own_high = PAD, PAD + rows

    work = (current, kap, tau, cur)
    if first:
        for a, source in enumerate(mains):
            work[a][own_low:own_high, :, :cols] = source[...]
            work[a][own_low:own_high, :, cols:] = extra_tile(a, flags, left, right)
    else:
        current[own_low:own_high] = own[...]
    base = 0
    for a, depth in enumerate(DEPTHS if first else (PAD,)):
        for i in range(depth):
            work[a][own_low - depth + i] = up[base + i] * flags[2]
            work[a][own_high + i] = down[base + i] * flags[3]
        base += depth

    zero = jnp.zeros((F, LANES), jnp.float32)

    def scale(ref, low, high):
        def body(r, carry):
            for at, v, near in walk(ref, r, 2, wide):
                for i in range(2):
                    scaled[r + i, :, at] = tau[r + i, :, at] * (kap[r + i, :, at] * v[i] - near[i])
            return carry

        pairs(low, high, body, 0)

    def image(ref, r):
        for at, s, near in walk(scaled, r, 2, wide):
            out = []
            for i in range(2):
                new = (kap[r + i, :, at] * s[i] - near[i]) + cur[r + i, :, at] * ref[r + i, :, at]
                out.append(new * mask[...] if at.start == cols else new)
            yield at, out

    scale(current, own_low - 3, own_high + 3)
    for r, flag, inner in ((own_low - 2, flags[2], 1), (own_high, flags[3], 0)):
        for at, new in image(current, r):
            for i in range(2):
                value = new[i] * flag
                one[r + i, :, at] = value
                if i == inner:
                    middle[r + i - SKIP, :, at] = value if first else 2.0 * value - old[r + i - SKIP, :, at]

    def first_rows(r, carry):
        cross = square = start = zero
        for at, new in image(current, r):
            for i in range(2):
                one[r + i, :, at] = new[i]
                value = new[i] if first else 2.0 * new[i] - old[r + i - SKIP, :, at]
                middle[r + i - SKIP, :, at] = value
                if at.start < cols:
                    source = current[r + i, :, at]
                    cross += value * source
                    square += value * value
                    if first:
                        start += source * source
        out = (carry[0] + cross, carry[1] + square)
        return out + ((carry[2] + start,) if first else ())

    found = pairs(own_low, own_high, first_rows, (zero,) * (3 if first else 2))

    if last:

        def final_rows(r, carry):
            total = zero
            for at, v, near in walk(middle, r - SKIP, 2, wide):
                if at.start < cols:
                    for i in range(2):
                        k = kap[r + i, :, at] * v[i] - near[i]
                        total += tau[r + i, :, at] * k * k + cur[r + i, :, at] * v[i] * v[i]
            return carry + total

        found += (pairs(own_low, own_high, final_rows, zero),)
        entries = [earlier[0][4]]
        for s in earlier:
            entries += [s[i] for i in range(4)]
        lane = lax.broadcasted_iota(jnp.int32, (F, LANES), 1)
        table = zero
        for k, entry in enumerate(entries + list(found)):
            table = jnp.where(lane == k, jnp.sum(entry, axis=1, keepdims=True), table)
        total = table[0:1]
        for f in range(1, F):
            total = total + pltpu.roll(table[f : f + 1], 2 * ITERS * f, 1)
        line[...] = total
        return

    sums[0] = found[0]
    sums[1] = found[1]
    if first:
        sums[4] = found[2]

    scale(one, own_low - 1, own_high + 1)

    def second_rows(r, carry):
        cross = square = zero
        for at, new in image(one, r):
            for i in range(2):
                value = 2.0 * new[i] - current[r + i, :, at]
                if not first:
                    value = 2.0 * value - older[r + i, :, at]
                newest[r + i - PAD, :, at] = value
                if at.start < cols:
                    cross += value * middle[r + i - SKIP, :, at]
                    square += value * value
        return carry[0] + cross, carry[1] + square

    sums[2], sums[3] = pairs(own_low, own_high, second_rows, (zero, zero))
    to_up[...] = newest[:PAD]
    to_down[...] = newest[rows - PAD :]


def phase(p, rows, cols, flags, mask, up, down, state, earlier=()):
    first, last = p == 0, p == ITERS // 2 - 1
    f32 = jnp.float32
    wide = cols + LANES
    ext = (rows + 2 * PAD, F, wide)
    out_shape = [pltpu.VMEM(ext, f32)] * (4 if first else 1) + [pltpu.VMEM((rows + 2, F, wide), f32)]
    if last:
        out_shape = [jax.ShapeDtypeStruct((1, LANES), f32)] + out_shape
    else:
        out_shape += [pltpu.VMEM((rows, F, wide), f32)]
        out_shape += [jax.ShapeDtypeStruct((PAD, F, wide), f32)] * 2
        out_shape += [jax.ShapeDtypeStruct((5 if first else 4, F, LANES), f32)]
    operands = list(state) if first else [held(x) for x in state]
    return pl.pallas_call(
        functools.partial(phase_kernel, p, rows, cols),
        in_specs=[SMEM] + [VMEM] * (3 + len(operands) + len(earlier)),
        out_specs=[VMEM] * len(out_shape),
        out_shape=out_shape,
        scratch_shapes=[pltpu.VMEM(ext, f32), pltpu.VMEM(ext, f32)],
        compiler_params=PARAMS,
        name=f"phase{p}",
    )(flags, mask, up, down, *operands, *earlier)


def coefficients(line):
    raw = [jnp.sum(jnp.where(lax.broadcasted_iota(jnp.int32, (F, LANES), 1)
                             == 2 * ITERS * lax.broadcasted_iota(jnp.int32, (F, LANES), 0) + k,
                             jnp.broadcast_to(line, (F, LANES)), 0.0), axis=1, keepdims=True)
           for k in range(2 * ITERS)]
    raw = [jnp.broadcast_to(v, (F, LANES)) for v in raw]
    m = [raw[0], raw[1]] + [2.0 * raw[k] - raw[k % 2] for k in range(2, 2 * ITERS - 1)]
    m.append(4.0 * raw[2 * ITERS - 1] - m[2 * ITERS - 3] - 2.0 * m[1])
    zero = jnp.zeros((F, LANES), jnp.float32)
    one = jnp.ones((F, LANES), jnp.float32)

    def moved(v):
        out = [MID * e for e in v] + [zero]
        out[1] = out[1] + HALF * v[0]
        for k in range(1, len(v)):
            out[k - 1] = out[k - 1] + 0.5 * HALF * v[k]
            out[k + 1] = out[k + 1] + 0.5 * HALF * v[k]
        return out

    def against(v, l):
        return MID * v[l] + 0.5 * HALF * (v[l + 1] + v[abs(l - 1)])

    res, way = list(m), list(m)
    res_in, way_in, lat_in = [one], [one], [zero] * ITERS
    lead = one
    now = m[0]
    pivots = []
    for it in range(ITERS):
        image = [against(way, l) for l in range(len(way) - 1)]
        alpha = now / (lead * image[it])
        for k in range(it + 1):
            lat_in[k] = lat_in[k] + alpha * way_in[k]
        if it == ITERS - 1:
            break
        res = [res[l] - alpha * image[l] for l in range(len(image))]
        step = moved(way_in)
        res_in = [a - alpha * b for a, b in zip(res_in + [zero], step)]
        lead = res_in[it + 1]
        new = lead * res[it + 1]
        pivots.append(res[it + 1] / (lead * m[0]))
        beta = new / now
        way = [res[l] + beta * way[l] for l in range(len(res))]
        way_in = [a + beta * b for a, b in zip(res_in, way_in + [zero])]
        now = new
    fine = pivots[-1] >= 0.3 * pivots[0]
    for pivot in pivots:
        fine = fine & (pivot >= 5e-3) & (pivot <= 20.0)
    return lat_in, fine


CHUNK = 4 * LANES


def columns_hot_kernel(cols, cells, hot):
    col = lax.rem(cells[...], cols)

    def step(b, carry):
        at = pl.ds(pl.multiple_of(b * LANES, LANES), LANES)
        row = lax.broadcasted_iota(jnp.int32, (LANES, cells.shape[1]), 0) + b * LANES
        hot[at] = jnp.where(row == col, 1.0, 0.0).astype(jnp.bfloat16)
        return carry

    lax.fori_loop(0, hot.shape[0] // LANES, step, 0)


def columns_hot(cells, cols):
    return pl.pallas_call(
        functools.partial(columns_hot_kernel, cols),
        in_specs=[VMEM],
        out_specs=VMEM,
        out_shape=pltpu.VMEM((cols + LANES, cells.shape[1]), jnp.bfloat16),
        compiler_params=PARAMS,
        name="columns_hot",
    )(cells)


def finish_kernel(rows, cols, line, cells, row_frac, col_frac, hot, *refs):
    basis, refs = refs[:ITERS], refs[ITERS:]
    latent, predictor, fine, parts, keep = refs
    wide = cols + LANES
    lat_in, good = coefficients(line[...])
    fine[...] = jnp.where(good, 1.0, 0.0)
    for k in range(ITERS):
        keep[k] = lat_in[k]
    tall = (rows + 2) * F
    lane = lax.broadcasted_iota(jnp.int32, (rows + 2, F, LANES), 2)

    def split(x, at, base):
        part = x.astype(jnp.bfloat16)
        rest = (x - part.astype(jnp.float32)).astype(jnp.bfloat16)
        parts[base : base + tall, at] = part.reshape(tall, LANES)
        parts[base + tall : base + 2 * tall, at] = rest.reshape(tall, LANES)

    def step(c, after):
        c = wide // LANES - 1 - c
        at = pl.ds(pl.multiple_of(c * LANES, LANES), LANES)
        total = None
        for k in range(ITERS):
            begin = PAD - SKIP * (k % 2)
            term = keep[k] * basis[k][begin : begin + rows + 1, :, at]
            total = term if total is None else total + term
        total = jnp.concatenate([total, jnp.zeros((1, F, LANES), jnp.float32)], axis=0)
        turned = pltpu.roll(total, LANES - 1, 2)
        split(total, at, 0)
        split(jnp.where(lane == LANES - 1, after, turned), at, 2 * tall)

        @pl.when(c < cols // LANES)
        def _():
            latent[:, :, at] = jnp.swapaxes(total[:rows], 0, 1)

        return turned

    lax.fori_loop(0, wide // LANES, step, jnp.zeros((rows + 2, F, LANES), jnp.float32))
    for c in range(0, cells.shape[1], CHUNK):
        at = slice(c, c + CHUNK)
        both = jnp.dot(parts[...], hot[:, at], preferred_element_type=jnp.float32)
        here = both[:tall] + both[tall : 2 * tall]
        beside = both[2 * tall : 3 * tall] + both[3 * tall :]
        row = cells[:, at] // cols
        frac = row_frac[:, at]
        low = jnp.zeros((F, CHUNK), jnp.float32)
        high = jnp.zeros((F, CHUNK), jnp.float32)
        for r in range(rows + 1):
            w = jnp.where(row == r, 1.0 - frac, jnp.where(row + 1 == r, frac, 0.0))
            low = low + w * here[r * F : (r + 1) * F]
            high = high + w * beside[r * F : (r + 1) * F]
        side = col_frac[:, at]
        out = (1.0 - side) * low + side * high
        for i in range(CHUNK // LANES):
            base = (c // LANES + i) * F
            predictor[base : base + F] = out[:, i * LANES : (i + 1) * LANES]


def finish(rows, cols, line, cells, row_frac, col_frac, hot, basis):
    f32 = jnp.float32
    wide = cols + LANES
    return pl.pallas_call(
        functools.partial(finish_kernel, rows, cols),
        in_specs=[VMEM] * (5 + ITERS),
        out_specs=[VMEM] * 3,
        out_shape=[
            jax.ShapeDtypeStruct((F, rows, cols), f32),
            jax.ShapeDtypeStruct((cells.shape[1] // LANES * F, LANES), f32),
            jax.ShapeDtypeStruct((F, LANES), f32),
        ],
        scratch_shapes=[
            pltpu.VMEM((4 * (rows + 2) * F, wide), jnp.bfloat16),
            pltpu.VMEM((ITERS, F, LANES), f32),
        ],
        compiler_params=PARAMS,
        name="finish",
    )(line, cells, row_frac, col_frac, *[held(x) for x in (hot, *basis)])


def extended(x, sides, width):
    for axis, dim in sides:
        size, length = (lax.axis_size(axis), x.shape[dim])
        up = [(i, (i + 1) % size) for i in range(size - 1)]
        down = [(j, i) for i, j in up]
        last = lax.slice_in_dim(x, length - width, length, axis=dim)
        leading = lax.slice_in_dim(x, 0, width, axis=dim)
        before = lax.ppermute(last, axis, up)
        after = lax.ppermute(leading, axis, down)
        x = jnp.concatenate([before, x, after], axis=dim)
    return x


def passed_along(x, axis, by):
    length = lax.axis_size(axis)
    pairs = [(i, i + by) for i in range(length) if 0 <= i + by < length]
    return lax.ppermute(x, axis, pairs)


def neighbours(padded):
    return padded[:, 2:, 1:-1] + padded[:, :-2, 1:-1] + padded[:, 1:-1, 2:] + padded[:, 1:-1, :-2]


def plain(right_side, kappa_field, tau_field, curvature, got_cells, got_row, got_col):
    def squares(values):
        return lax.psum(jnp.sum(values * values, axis=(1, 2)), ("tile", "field"))[:, None, None]

    def sweep(_, state):
        latent, residual, direction, norm_now = state
        padded = extended(direction, (("tile", 1), ("field", 2)), 1)
        scaled = tau_field * ((kappa_field + 4.0) * direction - neighbours(padded))
        spread = extended(scaled, (("tile", 1), ("field", 2)), 1)
        image = (kappa_field + 4.0) * scaled - neighbours(spread) + curvature * direction
        inner = lax.psum(jnp.sum(direction * image, axis=(1, 2)), ("tile", "field"))[:, None, None]
        alpha = norm_now / inner
        latent = latent + alpha * direction
        residual = residual - alpha * image
        norm_next = squares(residual)
        direction = residual + norm_next / norm_now * direction
        return latent, residual, direction, norm_next

    state = (jnp.zeros_like(right_side), right_side, right_side, squares(right_side))
    latent = lax.fori_loop(0, ITERS, sweep, state)[0]
    upper = passed_along(latent[:, :1, :], "tile", -1)
    tall = jnp.concatenate([latent, upper], axis=1)
    beside = passed_along(tall[:, :, :1], "field", -1)
    wide = jnp.concatenate([tall, beside], axis=2)
    columns = latent.shape[2]
    width = columns + 1
    flat = wide.reshape(wide.shape[0], -1)
    base = (got_cells // columns * width + got_cells % columns).astype(jnp.int32)

    def corner(offset):
        return jnp.take(flat, base + offset, axis=1)

    row_frac = got_row[None]
    col_frac = got_col[None]
    predictor = (
        (1.0 - row_frac) * (1.0 - col_frac) * corner(0)
        + row_frac * (1.0 - col_frac) * corner(width)
        + (1.0 - row_frac) * col_frac * corner(1)
        + row_frac * col_frac * corner(width + 1)
    )
    return latent, jnp.transpose(predictor, (1, 0, 2)).reshape(-1, predictor.shape[2])


def turned(x, axis, by):
    size = lax.axis_size(axis)
    return lax.ppermute(x, axis, [(i, (i + by) % size) for i in range(size)])


def summed(x, axis):
    size, stride = lax.axis_size(axis), 1
    while stride < size:
        if size // stride in (4, 16):
            for by in (1, -1):
                x = x + lax.ppermute(
                    x, axis, [(i, other(i, stride, by)) for i in range(size)]
                )
            stride *= 4
        else:
            x = x + lax.ppermute(x, axis, [(i, i ^ stride) for i in range(size)])
            stride *= 2
    return x


def other(i, stride, by):
    place = i // stride % 4
    partner = (place + (by if place % 2 == 0 else -by)) % 4
    return i + (partner - place) * stride


def local(
    right_side,
    kappa_field,
    tau_field,
    curvature,
    detect_prob,
    site_cells,
    site_offsets,
    site_count,
    visit_count,
    detections,
    surveyed,
):
    rows, cols = right_side.shape[1:]
    wide = cols + LANES
    tiles, bands = lax.axis_size("tile"), lax.axis_size("field")
    tile, band = lax.axis_index("tile"), lax.axis_index("field")
    flags = jnp.stack([band > 0, band < bands - 1, tile > 0, tile < tiles - 1]).astype(jnp.float32)
    lane = lax.broadcasted_iota(jnp.int32, (F, LANES), 1)
    mask = jnp.where(lane < SIDE, flags[1], jnp.where(lane >= LANES - SIDE, flags[0], 0.0))

    fields = (right_side, kappa_field, tau_field, curvature)
    to_left, to_right = columns_of(fields)
    from_right = turned(to_left, "field", -1)
    from_left = turned(to_right, "field", 1)
    *mains, top, bottom = prepare(fields)
    to_up, to_down = sides(flags, from_left, from_right, top, bottom)

    cells = site_cells[0, 0]
    sent = jnp.concatenate([cells.astype(jnp.float32)[:, None], site_offsets[0, 0]], axis=1)
    sent, to_up, to_down = lax.optimization_barrier((sent, to_up, to_down))
    got = lax.all_to_all(sent, "tile", split_axis=0, concat_axis=0, tiled=True)
    got_cells = got[:, 0].astype(jnp.int32)
    got_row, got_col = got[:, 1], got[:, 2]
    sites = (got_cells.reshape(1, -1), got_row.reshape(1, -1), got_col.reshape(1, -1))

    mask, got_row = lax.optimization_barrier((mask, got_row))
    common = (rows, cols, flags, mask)

    def exchanged(to_up, to_down):
        return turned(to_down, "tile", 1), turned(to_up, "tile", -1)

    up, down = exchanged(to_up, to_down)
    *coefs, older, old, own, to_up, to_down, part = phase(
        0, *common, up, down, (from_left, from_right, *mains)
    )
    basis, sums = [older, old], [part]
    for p in range(1, ITERS // 2 - 1):
        up, down = exchanged(to_up, to_down)
        older, old, own, to_up, to_down, part = phase(p, *common, up, down, (own, *coefs, older, old))
        basis += [older, old]
        sums.append(part)
    up, down = exchanged(to_up, to_down)
    line, older, old = phase(ITERS // 2 - 1, *common, up, down, (own, *coefs, older, old), earlier=sums)
    basis += [older, old]

    line, got_cells = lax.optimization_barrier((line, got_cells))
    hot = columns_hot(got_cells.reshape(1, -1), cols)
    line = summed(summed(line, "field"), "tile")
    latent, predictor, fine = finish(rows, cols, line, *sites, hot, basis)
    latent, predictor, _ = lax.while_loop(
        lambda state: state[2],
        lambda state: plain(*fields, got_cells, got_row, got_col) + (False,),
        (latent, predictor, jnp.logical_not(jnp.all(fine > 0.5))),
    )
    predictor = predictor.reshape(tiles, F, LANES)
    returned = lax.all_to_all(predictor, "tile", split_axis=0, concat_axis=0, tiled=True)

    slots = lax.broadcasted_iota(jnp.int32, cells.shape, 1)
    live = (slots < site_count[0, 0][:, None]).astype(jnp.float32)[:, None, :]
    visits = visit_count[0, 0].astype(jnp.float32)[:, None, :]
    miss_prob = jnp.exp(visits * jnp.log(1.0 - detect_prob)[:, None])
    expo = jnp.exp(returned)
    seen_grad = 1.0 / (1.0 + expo)
    miss_grad = -(1.0 - miss_prob) * expo / ((1.0 + expo) * (1.0 + miss_prob * expo))
    site_grad = (
        jnp.where(detections[0, 0] > 0, seen_grad, miss_grad)
        * surveyed[0, 0].astype(jnp.float32)
        * live
    )
    return (latent, site_grad[None, None])


def solution(mesh):
    in_specs = (
        P(None, "tile", "field"),
        P(None, "tile", "field"),
        P(None, "tile", "field"),
        P(None, "tile", "field"),
        P(),
        P("tile", "field", None, None),
        P("tile", "field", None, None, None),
        P("tile", "field", None),
        P("tile", "field", None, None),
        P("tile", "field", None, None, None),
        P("tile", "field", None, None, None),
    )
    out_specs = (P(None, "tile", "field"), P("tile", "field", None, None, None))
    return jax.shard_map(local, mesh=mesh, in_specs=in_specs, out_specs=out_specs, check_vma=False)
```

```python
import functools

import jax
import jax.numpy as jnp
from jax import lax
from jax.experimental import pallas as pl
from jax.experimental.pallas import tpu as pltpu
from jax.sharding import PartitionSpec as P

ITERS = 8
F = 8
PAD = 4
SKIP = PAD - 1
SIDE = 16
LANES = 128
LOW, HIGH = 0.2, 15.0
MID, HALF = 0.5 * (HIGH + LOW), 0.5 * (HIGH - LOW)
VMEM = pl.BlockSpec(memory_space=pltpu.VMEM)
SMEM = pl.BlockSpec(memory_space=pltpu.SMEM)
HBM = pl.BlockSpec(memory_space=pl.ANY)
PARAMS = pltpu.CompilerParams(vmem_limit_bytes=12 * 1024 * 1024)


def held(x):
    return pltpu.with_memory_space_constraint(x, pltpu.VMEM)


def columns_kernel(*refs):
    firsts, lasts, (to_left, to_right) = refs[0:4], refs[4:8], refs[8:]
    lane = lax.broadcasted_iota(jnp.int32, (16, F, LANES), 2)
    for out, blocks, start in ((to_left, firsts, 0), (to_right, lasts, LANES - SIDE)):
        packed = jnp.zeros((16, F, LANES), jnp.float32)
        for a, ref in enumerate(blocks):
            block = jnp.swapaxes(ref[...], 0, 1)
            shift = (SIDE * a - start) % LANES
            moved = pltpu.roll(block, shift, 2) if shift else block
            mine = (lane >= SIDE * a) & (lane < SIDE * (a + 1))
            packed = jnp.where(mine, moved, packed)
        out[...] = packed


def columns_of(fields):
    rows, cols = fields[0].shape[1:]
    first = pl.BlockSpec((F, rows, LANES), lambda i: (0, 0, 0))
    last = pl.BlockSpec((F, rows, LANES), lambda i: (0, 0, cols // LANES - 1))
    out = pl.BlockSpec((rows, F, LANES), lambda i: (0, 0, 0))
    shape = jax.ShapeDtypeStruct((rows, F, LANES), jnp.float32)
    return pl.pallas_call(
        columns_kernel,
        grid=(1,),
        in_specs=[first] * 4 + [last] * 4,
        out_specs=[out, out],
        out_shape=[shape, shape],
        name="columns",
    )(*fields, *fields)


DEPTHS = (4, 3, 3, 2)


def shaped(a, x):
    if a == 1:
        return x + 4.0
    if a == 2:
        return x * (1.0 / HALF)
    if a == 3:
        return (x - MID) * (1.0 / HALF)
    return x


def extra_tile(a, flags, left, right):
    lane = lax.broadcasted_iota(jnp.int32, left.shape, 2)
    shift = (-SIDE * a) % LANES
    after = shaped(a, pltpu.roll(right[...], shift, 2) if shift else right[...])
    before = shaped(a, pltpu.roll(left[...], LANES - SIDE * (a + 1), 2))
    return jnp.where(lane < SIDE, after * flags[1], 0.0) + jnp.where(lane >= LANES - SIDE, before * flags[0], 0.0)


def prepare_kernel(flags, left, right, *refs):
    fields, outs, (to_up, to_down) = refs[0:4], refs[4:8], refs[8:]
    rows, cols = fields[0].shape[1:]

    def place(a, at, block):
        outs[a][:, :, at] = block
        base, depth = sum(DEPTHS[:a]), DEPTHS[a]
        to_up[base : base + depth, :, at] = block[:depth]
        to_down[base : base + depth, :, at] = block[rows - depth :]

    def step(c, carry):
        at = pl.ds(pl.multiple_of(c * LANES, LANES), LANES)
        for a in range(4):
            place(a, at, shaped(a, jnp.swapaxes(fields[a][:, :, at], 0, 1)))
        return carry

    lax.fori_loop(0, cols // LANES, step, 0, unroll=4)
    for a in range(4):
        place(a, slice(cols, cols + LANES), extra_tile(a, flags, left, right))


def prepare(flags, left, right, fields):
    rows, cols = fields[0].shape[1:]
    wide = cols + LANES
    f32 = jnp.float32
    return pl.pallas_call(
        prepare_kernel,
        in_specs=[SMEM] + [VMEM] * 6,
        out_specs=[VMEM] * 6,
        out_shape=[pltpu.VMEM((rows, F, wide), f32)] * 4 + [jax.ShapeDtypeStruct((sum(DEPTHS), F, wide), f32)] * 2,
        compiler_params=PARAMS,
        name="prepare",
    )(flags, left, right, *fields)


def walk(ref, r, count, wide):
    tiles = wide // LANES
    lane = lax.broadcasted_iota(jnp.int32, (F, LANES), 1)
    leftmost, rightmost = lane == 0, lane == LANES - 1

    def load(c):
        return [ref[r - 1 + i, :, c * LANES : (c + 1) * LANES] for i in range(count + 2)]

    def turn(tile, by):
        return [pltpu.roll(v, by, 1) for v in tile[1:-1]]

    now = load(0)
    before = turn([ref[r - 1 + i, :, wide - LANES :] for i in range(count + 2)], 1)
    right, left = turn(now, 1), turn(now, LANES - 1)
    start = left
    for c in range(tiles):
        after = load(c + 1) if c + 1 < tiles else None
        following = turn(after, LANES - 1) if after else start
        near = [
            (now[i] + now[i + 2])
            + (jnp.where(leftmost, before[i], right[i]) + jnp.where(rightmost, following[i], left[i]))
            for i in range(count)
        ]
        yield slice(c * LANES, (c + 1) * LANES), now[1:-1], near
        if after:
            before, right, left, now = right, turn(after, 1), following, after


def pairs(low, high, body, carry):
    return lax.fori_loop(0, (high - low) // 2, lambda i, carry: body(low + 2 * i, carry), carry, unroll=True)


def phase_kernel(p, rows, cols, *refs):
    first, last = p == 0, p == ITERS // 2 - 1
    refs = list(refs)
    take = lambda n: [refs.pop(0) for _ in range(n)]
    flags, mask, up, down = take(4)
    if first:
        mains = take(4)
    else:
        own, kap, tau, cur, older, old = take(6)
    if last:
        earlier = take(ITERS // 2 - 1)
        line, current, middle = take(3)
    elif first:
        kap, tau, cur, current, middle, newest, to_up, to_down, sums = take(9)
    else:
        current, middle, newest, to_up, to_down, sums = take(6)
    scaled, one = refs
    wide = cols + LANES
    own_low, own_high = PAD, PAD + rows

    work = (current, kap, tau, cur)
    if first:
        for a, source in enumerate(mains):
            work[a][own_low:own_high] = source[...]
    else:
        current[own_low:own_high] = own[...]
    base = 0
    for a, depth in enumerate(DEPTHS if first else (up.shape[0],)):
        for i in range(depth):
            work[a][own_low - depth + i] = up[base + i] * flags[2]
            work[a][own_high + i] = down[base + i] * flags[3]
        base += depth

    zero = jnp.zeros((F, LANES), jnp.float32)

    def scale(ref, low, high):
        def body(r, carry):
            for at, v, near in walk(ref, r, 2, wide):
                for i in range(2):
                    scaled[r + i, :, at] = tau[r + i, :, at] * (kap[r + i, :, at] * v[i] - near[i])
            return carry

        pairs(low, high, body, 0)

    def image(ref, r):
        for at, s, near in walk(scaled, r, 2, wide):
            out = []
            for i in range(2):
                new = (kap[r + i, :, at] * s[i] - near[i]) + cur[r + i, :, at] * ref[r + i, :, at]
                out.append(new * mask[...] if at.start == cols else new)
            yield at, out

    reach = 2 if last else 3
    scale(current, own_low - reach, own_high + reach)
    for r, flag, inner in ((own_low - 2, flags[2], 1), (own_high, flags[3], 0)):
        for at, new in image(current, r):
            for i in range(2):
                value = new[i] * flag
                one[r + i, :, at] = value
                if i == inner:
                    middle[r + i - SKIP, :, at] = value if first else 2.0 * value - old[r + i - SKIP, :, at]

    def first_rows(r, carry):
        cross = square = start = zero
        for at, new in image(current, r):
            for i in range(2):
                one[r + i, :, at] = new[i]
                value = new[i] if first else 2.0 * new[i] - old[r + i - SKIP, :, at]
                middle[r + i - SKIP, :, at] = value
                if at.start < cols:
                    source = current[r + i, :, at]
                    cross += value * source
                    square += value * value
                    if first:
                        start += source * source
        out = (carry[0] + cross, carry[1] + square)
        return out + ((carry[2] + start,) if first else ())

    found = pairs(own_low, own_high, first_rows, (zero,) * (3 if first else 2))

    if last:

        def final_rows(r, carry):
            total = zero
            for at, v, near in walk(middle, r - SKIP, 2, wide):
                if at.start < cols:
                    for i in range(2):
                        k = kap[r + i, :, at] * v[i] - near[i]
                        total += tau[r + i, :, at] * k * k + cur[r + i, :, at] * v[i] * v[i]
            return carry + total

        found += (pairs(own_low, own_high, final_rows, zero),)
        entries = [earlier[0][4]]
        for s in earlier:
            entries += [s[i] for i in range(4)]
        lane = lax.broadcasted_iota(jnp.int32, (F, LANES), 1)
        table = zero
        for k, entry in enumerate(entries + list(found)):
            table = jnp.where(lane == k, jnp.sum(entry, axis=1, keepdims=True), table)
        total = table[0:1]
        for f in range(1, F):
            total = total + pltpu.roll(table[f : f + 1], 2 * ITERS * f, 1)
        line[...] = total
        return

    sums[0] = found[0]
    sums[1] = found[1]
    if first:
        sums[4] = found[2]

    scale(one, own_low - 1, own_high + 1)

    def second_rows(r, carry):
        cross = square = zero
        for at, new in image(one, r):
            for i in range(2):
                value = 2.0 * new[i] - current[r + i, :, at]
                if not first:
                    value = 2.0 * value - older[r + i, :, at]
                newest[r + i - PAD, :, at] = value
                if at.start < cols:
                    cross += value * middle[r + i - SKIP, :, at]
                    square += value * value
        return carry[0] + cross, carry[1] + square

    sums[2], sums[3] = pairs(own_low, own_high, second_rows, (zero, zero))
    depth = to_up.shape[0]
    to_up[...] = newest[:depth]
    to_down[...] = newest[rows - depth :]


def phase(p, rows, cols, flags, mask, up, down, state, earlier=()):
    first, last = p == 0, p == ITERS // 2 - 1
    f32 = jnp.float32
    wide = cols + LANES
    ext = (rows + 2 * PAD, F, wide)
    out_shape = [pltpu.VMEM(ext, f32)] * (4 if first else 1) + [pltpu.VMEM((rows + 2, F, wide), f32)]
    if last:
        out_shape = [jax.ShapeDtypeStruct((1, LANES), f32)] + out_shape
    else:
        out_shape += [pltpu.VMEM((rows, F, wide), f32)]
        depth = PAD - 1 if p == ITERS // 2 - 2 else PAD
        out_shape += [jax.ShapeDtypeStruct((depth, F, wide), f32)] * 2
        out_shape += [jax.ShapeDtypeStruct((5 if first else 4, F, LANES), f32)]
    operands = [held(x) for x in state]
    return pl.pallas_call(
        functools.partial(phase_kernel, p, rows, cols),
        in_specs=[SMEM] + [VMEM] * (3 + len(operands) + len(earlier)),
        out_specs=[VMEM] * len(out_shape),
        out_shape=out_shape,
        scratch_shapes=[pltpu.VMEM(ext, f32), pltpu.VMEM(ext, f32)],
        compiler_params=PARAMS,
        name=f"phase{p}",
    )(flags, mask, up, down, *operands, *earlier)


def coefficients(line):
    raw = [jnp.sum(jnp.where(lax.broadcasted_iota(jnp.int32, (F, LANES), 1)
                             == 2 * ITERS * lax.broadcasted_iota(jnp.int32, (F, LANES), 0) + k,
                             jnp.broadcast_to(line, (F, LANES)), 0.0), axis=1, keepdims=True)
           for k in range(2 * ITERS)]
    raw = [jnp.broadcast_to(v, (F, LANES)) for v in raw]
    m = [raw[0], raw[1]] + [2.0 * raw[k] - raw[k % 2] for k in range(2, 2 * ITERS - 1)]
    m.append(4.0 * raw[2 * ITERS - 1] - m[2 * ITERS - 3] - 2.0 * m[1])
    zero = jnp.zeros((F, LANES), jnp.float32)
    one = jnp.ones((F, LANES), jnp.float32)

    def moved(v):
        out = [MID * e for e in v] + [zero]
        out[1] = out[1] + HALF * v[0]
        for k in range(1, len(v)):
            out[k - 1] = out[k - 1] + 0.5 * HALF * v[k]
            out[k + 1] = out[k + 1] + 0.5 * HALF * v[k]
        return out

    def against(v, l):
        return MID * v[l] + 0.5 * HALF * (v[l + 1] + v[abs(l - 1)])

    res, way = list(m), list(m)
    res_in, way_in, lat_in = [one], [one], [zero] * ITERS
    lead = one
    now = m[0]
    pivots = []
    for it in range(ITERS):
        image = [against(way, l) for l in range(len(way) - 1)]
        alpha = now / (lead * image[it])
        for k in range(it + 1):
            lat_in[k] = lat_in[k] + alpha * way_in[k]
        if it == ITERS - 1:
            break
        res = [res[l] - alpha * image[l] for l in range(len(image))]
        step = moved(way_in)
        res_in = [a - alpha * b for a, b in zip(res_in + [zero], step)]
        lead = res_in[it + 1]
        new = lead * res[it + 1]
        pivots.append(res[it + 1] / (lead * m[0]))
        beta = new / now
        way = [res[l] + beta * way[l] for l in range(len(res))]
        way_in = [a + beta * b for a, b in zip(res_in, way_in + [zero])]
        now = new
    fine = pivots[-1] >= 0.3 * pivots[0]
    for pivot in pivots:
        fine = fine & (pivot >= 5e-3) & (pivot <= 20.0)
    return lat_in, fine


CHUNK = 4 * LANES


def columns_hot_kernel(cols, cells, hot):
    col = lax.rem(cells[...], cols)

    def step(b, carry):
        at = pl.ds(pl.multiple_of(b * LANES, LANES), LANES)
        row = lax.broadcasted_iota(jnp.int32, (LANES, cells.shape[1]), 0) + b * LANES
        hot[at] = jnp.where(row == col, 1.0, 0.0).astype(jnp.bfloat16)
        return carry

    lax.fori_loop(0, hot.shape[0] // LANES, step, 0)


def columns_hot(cells, cols):
    return pl.pallas_call(
        functools.partial(columns_hot_kernel, cols),
        in_specs=[VMEM],
        out_specs=VMEM,
        out_shape=pltpu.VMEM((cols, cells.shape[1]), jnp.bfloat16),
        compiler_params=PARAMS,
        name="columns_hot",
    )(cells)


def finish_kernel(rows, cols, line, cells, row_frac, col_frac, hot, *refs):
    basis, refs = refs[:ITERS], refs[ITERS:]
    latent, predictor, fine, parts, keep = refs
    wide = cols + LANES
    lat_in, good = coefficients(line[...])
    fine[...] = jnp.where(good, 1.0, 0.0)
    for k in range(ITERS):
        keep[k] = lat_in[k]
    tall = (rows + 2) * F
    lane = lax.broadcasted_iota(jnp.int32, (rows + 2, F, LANES), 2)

    def split(x, at, base):
        part = x.astype(jnp.bfloat16)
        rest = (x - part.astype(jnp.float32)).astype(jnp.bfloat16)
        parts[base : base + tall, at] = part.reshape(tall, LANES)
        parts[base + tall : base + 2 * tall, at] = rest.reshape(tall, LANES)

    def step(c, after):
        c = wide // LANES - 1 - c
        at = pl.ds(pl.multiple_of(c * LANES, LANES), LANES)
        total = None
        for k in range(ITERS):
            begin = PAD - SKIP * (k % 2)
            term = keep[k] * basis[k][begin : begin + rows + 1, :, at]
            total = term if total is None else total + term
        total = jnp.concatenate([total, jnp.zeros((1, F, LANES), jnp.float32)], axis=0)
        turned = pltpu.roll(total, LANES - 1, 2)

        @pl.when(c < cols // LANES)
        def _():
            split(total, at, 0)
            split(jnp.where(lane == LANES - 1, after, turned), at, 2 * tall)
            latent[:, :, at] = jnp.swapaxes(total[:rows], 0, 1)

        return turned

    lax.fori_loop(0, wide // LANES, step, jnp.zeros((rows + 2, F, LANES), jnp.float32))
    for c in range(0, cells.shape[1], CHUNK):
        at = slice(c, c + CHUNK)
        both = jnp.dot(parts[...], hot[:, at], preferred_element_type=jnp.float32)
        here = both[:tall] + both[tall : 2 * tall]
        beside = both[2 * tall : 3 * tall] + both[3 * tall :]
        row = cells[:, at] // cols
        frac = row_frac[:, at]
        low = jnp.zeros((F, CHUNK), jnp.float32)
        high = jnp.zeros((F, CHUNK), jnp.float32)
        for r in range(rows + 1):
            w = jnp.where(row == r, 1.0 - frac, jnp.where(row + 1 == r, frac, 0.0))
            low = low + w * here[r * F : (r + 1) * F]
            high = high + w * beside[r * F : (r + 1) * F]
        side = col_frac[:, at]
        out = (1.0 - side) * low + side * high
        for i in range(CHUNK // LANES):
            base = (c // LANES + i) * F
            predictor[base : base + F] = out[:, i * LANES : (i + 1) * LANES]


def finish(rows, cols, line, cells, row_frac, col_frac, hot, basis):
    f32 = jnp.float32
    wide = cols + LANES
    return pl.pallas_call(
        functools.partial(finish_kernel, rows, cols),
        in_specs=[VMEM] * (5 + ITERS),
        out_specs=[VMEM] * 3,
        out_shape=[
            jax.ShapeDtypeStruct((F, rows, cols), f32),
            jax.ShapeDtypeStruct((cells.shape[1] // LANES * F, LANES), f32),
            jax.ShapeDtypeStruct((F, LANES), f32),
        ],
        scratch_shapes=[
            pltpu.VMEM((4 * (rows + 2) * F, cols), jnp.bfloat16),
            pltpu.VMEM((ITERS, F, LANES), f32),
        ],
        compiler_params=PARAMS,
        name="finish",
    )(line, cells, row_frac, col_frac, *[held(x) for x in (hot, *basis)])


def extended(x, sides, width):
    for axis, dim in sides:
        size, length = (lax.axis_size(axis), x.shape[dim])
        up = [(i, (i + 1) % size) for i in range(size - 1)]
        down = [(j, i) for i, j in up]
        last = lax.slice_in_dim(x, length - width, length, axis=dim)
        leading = lax.slice_in_dim(x, 0, width, axis=dim)
        before = lax.ppermute(last, axis, up)
        after = lax.ppermute(leading, axis, down)
        x = jnp.concatenate([before, x, after], axis=dim)
    return x


def passed_along(x, axis, by):
    length = lax.axis_size(axis)
    pairs = [(i, i + by) for i in range(length) if 0 <= i + by < length]
    return lax.ppermute(x, axis, pairs)


def neighbours(padded):
    return padded[:, 2:, 1:-1] + padded[:, :-2, 1:-1] + padded[:, 1:-1, 2:] + padded[:, 1:-1, :-2]


def plain(right_side, kappa_field, tau_field, curvature, got_cells, got_row, got_col):
    def squares(values):
        return lax.psum(jnp.sum(values * values, axis=(1, 2)), ("tile", "field"))[:, None, None]

    def sweep(_, state):
        latent, residual, direction, norm_now = state
        padded = extended(direction, (("tile", 1), ("field", 2)), 1)
        scaled = tau_field * ((kappa_field + 4.0) * direction - neighbours(padded))
        spread = extended(scaled, (("tile", 1), ("field", 2)), 1)
        image = (kappa_field + 4.0) * scaled - neighbours(spread) + curvature * direction
        inner = lax.psum(jnp.sum(direction * image, axis=(1, 2)), ("tile", "field"))[:, None, None]
        alpha = norm_now / inner
        latent = latent + alpha * direction
        residual = residual - alpha * image
        norm_next = squares(residual)
        direction = residual + norm_next / norm_now * direction
        return latent, residual, direction, norm_next

    state = (jnp.zeros_like(right_side), right_side, right_side, squares(right_side))
    latent = lax.fori_loop(0, ITERS, sweep, state)[0]
    upper = passed_along(latent[:, :1, :], "tile", -1)
    tall = jnp.concatenate([latent, upper], axis=1)
    beside = passed_along(tall[:, :, :1], "field", -1)
    wide = jnp.concatenate([tall, beside], axis=2)
    columns = latent.shape[2]
    width = columns + 1
    flat = wide.reshape(wide.shape[0], -1)
    base = (got_cells // columns * width + got_cells % columns).astype(jnp.int32)

    def corner(offset):
        return jnp.take(flat, base + offset, axis=1)

    row_frac = got_row[None]
    col_frac = got_col[None]
    predictor = (
        (1.0 - row_frac) * (1.0 - col_frac) * corner(0)
        + row_frac * (1.0 - col_frac) * corner(width)
        + (1.0 - row_frac) * col_frac * corner(1)
        + row_frac * col_frac * corner(width + 1)
    )
    return latent, jnp.transpose(predictor, (1, 0, 2)).reshape(-1, predictor.shape[2])


def turned(x, axis, by):
    size = lax.axis_size(axis)
    return lax.ppermute(x, axis, [(i, (i + by) % size) for i in range(size)])


def summed(x, axis):
    size, stride = lax.axis_size(axis), 1
    while stride < size:
        if size // stride in (4, 16):
            for by in (1, -1):
                x = x + lax.ppermute(
                    x, axis, [(i, other(i, stride, by)) for i in range(size)]
                )
            stride *= 4
        else:
            x = x + lax.ppermute(x, axis, [(i, i ^ stride) for i in range(size)])
            stride *= 2
    return x


def other(i, stride, by):
    place = i // stride % 4
    partner = (place + (by if place % 2 == 0 else -by)) % 4
    return i + (partner - place) * stride


def local(
    right_side,
    kappa_field,
    tau_field,
    curvature,
    detect_prob,
    site_cells,
    site_offsets,
    site_count,
    visit_count,
    detections,
    surveyed,
):
    rows, cols = right_side.shape[1:]
    wide = cols + LANES
    tiles, bands = lax.axis_size("tile"), lax.axis_size("field")
    tile, band = lax.axis_index("tile"), lax.axis_index("field")
    flags = jnp.stack([band > 0, band < bands - 1, tile > 0, tile < tiles - 1]).astype(jnp.float32)
    lane = lax.broadcasted_iota(jnp.int32, (F, LANES), 1)
    mask = jnp.where(lane < SIDE, flags[1], jnp.where(lane >= LANES - SIDE, flags[0], 0.0))

    fields = (right_side, kappa_field, tau_field, curvature)
    to_left, to_right = columns_of(fields)
    cells = site_cells[0, 0]
    sent = jnp.concatenate([cells.astype(jnp.float32)[:, None], site_offsets[0, 0]], axis=1)
    sent, to_left, to_right = lax.optimization_barrier((sent, to_left, to_right))
    from_right = turned(to_left, "field", -1)
    from_left = turned(to_right, "field", 1)
    got = lax.all_to_all(sent, "tile", split_axis=0, concat_axis=0, tiled=True)
    flags, got = lax.optimization_barrier((flags, got))
    got_cells = got[:, 0].astype(jnp.int32)
    got_row, got_col = got[:, 1], got[:, 2]
    sites = (got_cells.reshape(1, -1), got_row.reshape(1, -1), got_col.reshape(1, -1))
    *mains, to_up, to_down = prepare(flags, from_left, from_right, fields)
    common = (rows, cols, flags, mask)

    def exchanged(to_up, to_down):
        return turned(to_down, "tile", 1), turned(to_up, "tile", -1)

    up, down = exchanged(to_up, to_down)
    *coefs, older, old, own, to_up, to_down, part = phase(
        0, *common, up, down, mains
    )
    basis, sums = [older, old], [part]
    for p in range(1, ITERS // 2 - 1):
        up, down = exchanged(to_up, to_down)
        older, old, own, to_up, to_down, part = phase(p, *common, up, down, (own, *coefs, older, old))
        basis += [older, old]
        sums.append(part)
    up, down = exchanged(to_up, to_down)
    line, older, old = phase(ITERS // 2 - 1, *common, up, down, (own, *coefs, older, old), earlier=sums)
    basis += [older, old]

    line, got_cells = lax.optimization_barrier((line, got_cells))
    hot = columns_hot(got_cells.reshape(1, -1), cols)
    line = summed(summed(line, "field"), "tile")
    latent, predictor, fine = finish(rows, cols, line, *sites, hot, basis)
    latent, predictor, _ = lax.while_loop(
        lambda state: state[2],
        lambda state: plain(*fields, got_cells, got_row, got_col) + (False,),
        (latent, predictor, jnp.logical_not(jnp.all(fine > 0.5))),
    )
    predictor = predictor.reshape(tiles, F, LANES)
    returned = lax.all_to_all(predictor, "tile", split_axis=0, concat_axis=0, tiled=True)

    slots = lax.broadcasted_iota(jnp.int32, cells.shape, 1)
    live = (slots < site_count[0, 0][:, None]).astype(jnp.float32)[:, None, :]
    visits = visit_count[0, 0].astype(jnp.float32)[:, None, :]
    miss_prob = jnp.exp(visits * jnp.log(1.0 - detect_prob)[:, None])
    expo = jnp.exp(returned)
    seen_grad = 1.0 / (1.0 + expo)
    miss_grad = -(1.0 - miss_prob) * expo / ((1.0 + expo) * (1.0 + miss_prob * expo))
    site_grad = (
        jnp.where(detections[0, 0] > 0, seen_grad, miss_grad)
        * surveyed[0, 0].astype(jnp.float32)
        * live
    )
    return (latent, site_grad[None, None])


def solution(mesh):
    in_specs = (
        P(None, "tile", "field"),
        P(None, "tile", "field"),
        P(None, "tile", "field"),
        P(None, "tile", "field"),
        P(),
        P("tile", "field", None, None),
        P("tile", "field", None, None, None),
        P("tile", "field", None),
        P("tile", "field", None, None),
        P("tile", "field", None, None, None),
        P("tile", "field", None, None, None),
    )
    out_specs = (P(None, "tile", "field"), P("tile", "field", None, None, None))
    return jax.shard_map(local, mesh=mesh, in_specs=in_specs, out_specs=out_specs, check_vma=False)
```

```python
import functools

import jax
import jax.numpy as jnp
from jax import lax
from jax.experimental import pallas as pl
from jax.experimental.pallas import tpu as pltpu
from jax.sharding import PartitionSpec as P

ITERS = 8
F = 8
PAD = 4
SKIP = PAD - 1
SIDE = 16
LANES = 128
LOW, HIGH = 0.2, 15.0
MID, HALF = 0.5 * (HIGH + LOW), 0.5 * (HIGH - LOW)
VMEM = pl.BlockSpec(memory_space=pltpu.VMEM)
SMEM = pl.BlockSpec(memory_space=pltpu.SMEM)
HBM = pl.BlockSpec(memory_space=pl.ANY)
PARAMS = pltpu.CompilerParams(vmem_limit_bytes=12 * 1024 * 1024)


def held(x):
    return pltpu.with_memory_space_constraint(x, pltpu.VMEM)


def columns_kernel(*refs):
    firsts, lasts, (cells, offsets, to_left, to_right, sent) = refs[0:4], refs[4:8], refs[8:]
    for i in range(cells.shape[0]):
        sent[i, 0:1] = cells[i : i + 1].astype(jnp.float32)
        sent[i, 1:3] = offsets[i]
    lane = lax.broadcasted_iota(jnp.int32, (16, F, LANES), 2)
    for out, blocks, start in ((to_left, firsts, 0), (to_right, lasts, LANES - SIDE)):
        packed = jnp.zeros((16, F, LANES), jnp.float32)
        for a, ref in enumerate(blocks):
            block = jnp.swapaxes(ref[...], 0, 1)
            shift = (SIDE * a - start) % LANES
            moved = pltpu.roll(block, shift, 2) if shift else block
            mine = (lane >= SIDE * a) & (lane < SIDE * (a + 1))
            packed = jnp.where(mine, moved, packed)
        out[...] = packed


def columns_of(fields, cells, offsets):
    rows, cols = fields[0].shape[1:]
    first = pl.BlockSpec((F, rows, LANES), lambda i: (0, 0, 0))
    last = pl.BlockSpec((F, rows, LANES), lambda i: (0, 0, cols // LANES - 1))
    out = pl.BlockSpec((rows, F, LANES), lambda i: (0, 0, 0))
    shape = jax.ShapeDtypeStruct((rows, F, LANES), jnp.float32)
    sent = (cells.shape[0], 3, cells.shape[1])

    def whole(shape):
        return pl.BlockSpec(shape, lambda i: (0,) * len(shape))

    return pl.pallas_call(
        columns_kernel,
        grid=(1,),
        in_specs=[first] * 4 + [last] * 4 + [whole(cells.shape), whole(offsets.shape)],
        out_specs=[out, out, whole(sent)],
        out_shape=[shape, shape, jax.ShapeDtypeStruct(sent, jnp.float32)],
        name="columns",
    )(*fields, *fields, cells, offsets)


DEPTHS = (4, 3, 3, 2)


def shaped(a, x):
    if a == 1:
        return x + 4.0
    if a == 2:
        return x * (1.0 / HALF)
    if a == 3:
        return (x - MID) * (1.0 / HALF)
    return x


def extra_tile(a, flags, left, right):
    lane = lax.broadcasted_iota(jnp.int32, left.shape, 2)
    shift = (-SIDE * a) % LANES
    after = shaped(a, pltpu.roll(right[...], shift, 2) if shift else right[...])
    before = shaped(a, pltpu.roll(left[...], LANES - SIDE * (a + 1), 2))
    return jnp.where(lane < SIDE, after * flags[1], 0.0) + jnp.where(lane >= LANES - SIDE, before * flags[0], 0.0)


def prepare_kernel(flags, left, right, *refs):
    fields, outs, (to_up, to_down) = refs[0:4], refs[4:8], refs[8:]
    rows, cols = fields[0].shape[1:]

    def place(a, at, block):
        outs[a][:, :, at] = block
        base, depth = sum(DEPTHS[:a]), DEPTHS[a]
        to_up[base : base + depth, :, at] = block[:depth]
        to_down[base : base + depth, :, at] = block[rows - depth :]

    def step(c, carry):
        at = pl.ds(pl.multiple_of(c * LANES, LANES), LANES)
        for a in range(4):
            place(a, at, shaped(a, jnp.swapaxes(fields[a][:, :, at], 0, 1)))
        return carry

    lax.fori_loop(0, cols // LANES, step, 0, unroll=4)
    for a in range(4):
        place(a, slice(cols, cols + LANES), extra_tile(a, flags, left, right))


def prepare(flags, left, right, fields):
    rows, cols = fields[0].shape[1:]
    wide = cols + LANES
    f32 = jnp.float32
    return pl.pallas_call(
        prepare_kernel,
        in_specs=[SMEM] + [VMEM] * 6,
        out_specs=[VMEM] * 6,
        out_shape=[pltpu.VMEM((rows, F, wide), f32)] * 4 + [jax.ShapeDtypeStruct((sum(DEPTHS), F, wide), f32)] * 2,
        compiler_params=PARAMS,
        name="prepare",
    )(flags, left, right, *fields)


def walk(ref, r, count, wide):
    tiles = wide // LANES
    lane = lax.broadcasted_iota(jnp.int32, (F, LANES), 1)
    leftmost, rightmost = lane == 0, lane == LANES - 1

    def load(c):
        return [ref[r - 1 + i, :, c * LANES : (c + 1) * LANES] for i in range(count + 2)]

    def turn(tile, by):
        return [pltpu.roll(v, by, 1) for v in tile[1:-1]]

    now = load(0)
    before = turn([ref[r - 1 + i, :, wide - LANES :] for i in range(count + 2)], 1)
    right, left = turn(now, 1), turn(now, LANES - 1)
    start = left
    for c in range(tiles):
        after = load(c + 1) if c + 1 < tiles else None
        following = turn(after, LANES - 1) if after else start
        near = [
            (now[i] + now[i + 2])
            + (jnp.where(leftmost, before[i], right[i]) + jnp.where(rightmost, following[i], left[i]))
            for i in range(count)
        ]
        yield slice(c * LANES, (c + 1) * LANES), now[1:-1], near
        if after:
            before, right, left, now = right, turn(after, 1), following, after


def pairs(low, high, body, carry):
    return lax.fori_loop(0, (high - low) // 2, lambda i, carry: body(low + 2 * i, carry), carry, unroll=True)


class Rows:
    def __init__(self, ref, shift):
        self.ref, self.shift = ref, shift

    def __getitem__(self, key):
        return self.ref[(key[0] + self.shift, *key[1:])]

    def __setitem__(self, key, value):
        self.ref[(key[0] + self.shift, *key[1:])] = value


def rows_of(ref, shift):
    return None if ref is None else Rows(ref, shift)


INSIDE = dict(scale=[(1, 15)], first=[(2, 14)], again=[(3, 13)], second=[(4, 12)])
OUTSIDE = dict(
    scale=[(-3, 3), (13, 19)], first=[(0, 2), (14, 16)], again=[(-1, 5), (11, 17)], second=[(0, 4), (12, 16)]
)


def apply_twice(p, cols, where, ring, mask, current, kap, tau, cur, older, old, scaled, one, middle, newest):
    first, last = p == 0, p == ITERS // 2 - 1
    wide = cols + LANES
    zero = jnp.zeros((F, LANES), jnp.float32)

    def scale(ref, low, high):
        def body(r, carry):
            for at, v, near in walk(ref, r, 2, wide):
                for i in range(2):
                    scaled[r + i, :, at] = tau[r + i, :, at] * (kap[r + i, :, at] * v[i] - near[i])
            return carry

        pairs(low, high, body, 0)

    def image(ref, r):
        for at, s, near in walk(scaled, r, 2, wide):
            out = []
            for i in range(2):
                new = (kap[r + i, :, at] * s[i] - near[i]) + cur[r + i, :, at] * ref[r + i, :, at]
                out.append(new * mask[...] if at.start == cols else new)
            yield at, out

    for low, high in where["scale"]:
        scale(current, low, high)
    for r, flag, inner in ring:
        for at, new in image(current, r):
            for i in range(2):
                value = new[i] * flag
                one[r + i, :, at] = value
                if i == inner:
                    middle[r + i, :, at] = value if first else 2.0 * value - old[r + i, :, at]

    def first_rows(r, carry):
        cross = square = start = zero
        for at, new in image(current, r):
            for i in range(2):
                if not last:
                    one[r + i, :, at] = new[i]
                value = new[i] if first else 2.0 * new[i] - old[r + i, :, at]
                middle[r + i, :, at] = value
                if at.start < cols:
                    source = current[r + i, :, at]
                    cross += value * source
                    square += value * value
                    if first:
                        start += source * source
        out = (carry[0] + cross, carry[1] + square)
        return out + ((carry[2] + start,) if first else ())

    found = (zero,) * (3 if first else 2)
    for low, high in where["first"]:
        found = pairs(low, high, first_rows, found)

    if last:
        def final_rows(r, carry):
            total = zero
            for at, v, near in walk(middle, r, 2, wide):
                if at.start < cols:
                    for i in range(2):
                        k = kap[r + i, :, at] * v[i] - near[i]
                        total += tau[r + i, :, at] * k * k + cur[r + i, :, at] * v[i] * v[i]
            return carry + total

        total = zero
        for low, high in where["second"]:
            total = pairs(low, high, final_rows, total)
        return [*found, total]

    for low, high in where["again"]:
        scale(one, low, high)

    def second_rows(r, carry):
        cross = square = zero
        for at, new in image(one, r):
            for i in range(2):
                value = 2.0 * new[i] - current[r + i, :, at]
                if not first:
                    value = 2.0 * value - older[r + i, :, at]
                newest[r + i, :, at] = value
                if at.start < cols:
                    cross += value * middle[r + i, :, at]
                    square += value * value
        return carry[0] + cross, carry[1] + square

    more = (zero, zero)
    for low, high in where["second"]:
        more = pairs(low, high, second_rows, more)
    return [found[0], found[1], *more, *found[2:]]


def inside_kernel(p, cols, *refs):
    first, last = p == 0, p == ITERS // 2 - 1
    refs = list(refs)
    take = lambda n: [refs.pop(0) for _ in range(n)]
    mask, own, kap, tau, cur = take(5)
    older, old = (None, None) if first else take(2)
    shift = 0 if first else PAD
    coefs = [Rows(x, shift) for x in (kap, tau, cur)]
    older, old = rows_of(older, PAD), rows_of(old, 1)
    (middle,) = take(1)
    one, newest = (None, None) if last else take(2)
    sums, scaled = refs
    found = apply_twice(
        p, cols, INSIDE, (), mask, Rows(own, 0), *coefs, older, old, Rows(scaled, 0),
        rows_of(one, -2), Rows(middle, -2), rows_of(newest, -4),
    )
    for i, total in enumerate(found):
        sums[i] = total


def outside_kernel(p, rows, cols, *refs):
    first, last = p == 0, p == ITERS // 2 - 1
    refs = list(refs)
    take = lambda n: [refs.pop(0) for _ in range(n)]
    flags, mask, up, down, own, kap_in, tau_in, cur_in = take(8)
    older, old = (None, None) if first else take(2)
    (middle_in,) = take(1)
    one_in, newest_in = (None, None) if last else take(2)
    (part,) = take(1)
    if last:
        earlier = take(ITERS // 2 - 1)
        (line,) = take(1)
    current, middle = take(2)
    kap, tau, cur = take(3) if first else (kap_in, tau_in, cur_in)
    if not last:
        newest, to_up, to_down, sums = take(4)
    scaled, one = refs
    own_low, own_high = PAD, PAD + rows

    work = (current, kap, tau, cur)
    for a, source in enumerate((own, kap_in, tau_in, cur_in) if first else (own,)):
        work[a][own_low:own_high] = source[...]
    base = 0
    for a, depth in enumerate(DEPTHS if first else (up.shape[0],)):
        for i in range(depth):
            work[a][own_low - depth + i] = up[base + i] * flags[2]
            work[a][own_high + i] = down[base + i] * flags[3]
        base += depth
    middle[1 + 2 : 1 + rows - 2] = middle_in[...]
    if not last:
        one[own_low + 2 : own_low + 6] = one_in[:4]
        one[own_high - 6 : own_high - 2] = one_in[8:]
        newest[4 : rows - 4] = newest_in[...]

    found = apply_twice(
        p, cols, OUTSIDE, ((-2, flags[2], 1), (rows, flags[3], 0)), mask,
        *[Rows(x, PAD) for x in (current, kap, tau, cur)], rows_of(older, PAD), rows_of(old, 1),
        Rows(scaled, PAD), Rows(one, PAD), Rows(middle, 1), None if last else Rows(newest, 0),
    )
    found = [x + part[i] for i, x in enumerate(found)]
    if last:
        entries = [earlier[0][4]]
        for s in earlier:
            entries += [s[i] for i in range(4)]
        lane = lax.broadcasted_iota(jnp.int32, (F, LANES), 1)
        table = jnp.zeros((F, LANES), jnp.float32)
        for k, entry in enumerate(entries + found):
            table = jnp.where(lane == k, jnp.sum(entry, axis=1, keepdims=True), table)
        total = table[0:1]
        for f in range(1, F):
            total = total + pltpu.roll(table[f : f + 1], 2 * ITERS * f, 1)
        line[...] = total
        return
    for i, total in enumerate(found):
        sums[i] = total
    depth = to_up.shape[0]
    to_up[...] = newest[:depth]
    to_down[...] = newest[rows - depth :]


def phase(p, rows, cols, flags, mask, up, down, state, earlier=()):
    first, last = p == 0, p == ITERS // 2 - 1
    f32 = jnp.float32
    wide = cols + LANES
    ext = (rows + 2 * PAD, F, wide)
    state = [held(x) for x in state]
    counted = jax.ShapeDtypeStruct((5 if first else 3 if last else 4, F, LANES), f32)
    part_shape = [pltpu.VMEM((rows - 4, F, wide), f32)]
    if not last:
        part_shape += [pltpu.VMEM((rows - 4, F, wide), f32), pltpu.VMEM((rows - 8, F, wide), f32)]
    inside = pl.pallas_call(
        functools.partial(inside_kernel, p, cols),
        in_specs=[VMEM] * (1 + len(state)),
        out_specs=[VMEM] * (len(part_shape) + 1),
        out_shape=part_shape + [counted],
        scratch_shapes=[pltpu.VMEM((rows, F, wide), f32)],
        compiler_params=PARAMS,
        cost_estimate=pl.CostEstimate(flops=100_000_000, bytes_accessed=8_000_000, transcendentals=0),
        name=f"inside{p}",
    )(mask, *state)
    out_shape = [pltpu.VMEM(ext, f32), pltpu.VMEM((rows + 2, F, wide), f32)]
    if first:
        out_shape += [pltpu.VMEM(ext, f32)] * 3
    if last:
        out_shape = [jax.ShapeDtypeStruct((1, LANES), f32)] + out_shape
    else:
        out_shape += [pltpu.VMEM((rows, F, wide), f32)]
        depth = PAD - 1 if p == ITERS // 2 - 2 else PAD
        out_shape += [jax.ShapeDtypeStruct((depth, F, wide), f32)] * 2 + [counted]
    return pl.pallas_call(
        functools.partial(outside_kernel, p, rows, cols),
        in_specs=[SMEM] + [VMEM] * (3 + len(state) + len(inside) + len(earlier)),
        out_specs=[VMEM] * len(out_shape),
        out_shape=out_shape,
        scratch_shapes=[pltpu.VMEM(ext, f32), pltpu.VMEM(ext, f32)],
        compiler_params=PARAMS,
        name=f"outside{p}",
    )(flags, mask, up, down, *state, *[held(x) for x in inside[:-1]], inside[-1], *earlier)


def coefficients(line):
    raw = [jnp.sum(jnp.where(lax.broadcasted_iota(jnp.int32, (F, LANES), 1)
                             == 2 * ITERS * lax.broadcasted_iota(jnp.int32, (F, LANES), 0) + k,
                             jnp.broadcast_to(line, (F, LANES)), 0.0), axis=1, keepdims=True)
           for k in range(2 * ITERS)]
    raw = [jnp.broadcast_to(v, (F, LANES)) for v in raw]
    m = [raw[0], raw[1]] + [2.0 * raw[k] - raw[k % 2] for k in range(2, 2 * ITERS - 1)]
    m.append(4.0 * raw[2 * ITERS - 1] - m[2 * ITERS - 3] - 2.0 * m[1])
    zero = jnp.zeros((F, LANES), jnp.float32)
    one = jnp.ones((F, LANES), jnp.float32)

    def moved(v):
        out = [MID * e for e in v] + [zero]
        out[1] = out[1] + HALF * v[0]
        for k in range(1, len(v)):
            out[k - 1] = out[k - 1] + 0.5 * HALF * v[k]
            out[k + 1] = out[k + 1] + 0.5 * HALF * v[k]
        return out

    def against(v, l):
        return MID * v[l] + 0.5 * HALF * (v[l + 1] + v[abs(l - 1)])

    res, way = list(m), list(m)
    res_in, way_in, lat_in = [one], [one], [zero] * ITERS
    lead = one
    now = m[0]
    pivots = []
    for it in range(ITERS):
        image = [against(way, l) for l in range(len(way) - 1)]
        alpha = now / (lead * image[it])
        for k in range(it + 1):
            lat_in[k] = lat_in[k] + alpha * way_in[k]
        if it == ITERS - 1:
            break
        res = [res[l] - alpha * image[l] for l in range(len(image))]
        step = moved(way_in)
        res_in = [a - alpha * b for a, b in zip(res_in + [zero], step)]
        lead = res_in[it + 1]
        new = lead * res[it + 1]
        pivots.append(res[it + 1] / (lead * m[0]))
        beta = new / now
        way = [res[l] + beta * way[l] for l in range(len(res))]
        way_in = [a + beta * b for a, b in zip(res_in, way_in + [zero])]
        now = new
    fine = pivots[-1] >= 0.3 * pivots[0]
    for pivot in pivots:
        fine = fine & (pivot >= 5e-3) & (pivot <= 20.0)
    return lat_in, fine


CHUNK = 4 * LANES


def columns_hot_kernel(cols, cells, hot):
    col = lax.rem(cells[...], cols)

    def step(b, carry):
        at = pl.ds(pl.multiple_of(b * LANES, LANES), LANES)
        row = lax.broadcasted_iota(jnp.int32, (LANES, cells.shape[1]), 0) + b * LANES
        hot[at] = jnp.where(row == col, 1.0, 0.0).astype(jnp.bfloat16)
        return carry

    lax.fori_loop(0, hot.shape[0] // LANES, step, 0)


def columns_hot(cells, cols):
    return pl.pallas_call(
        functools.partial(columns_hot_kernel, cols),
        in_specs=[VMEM],
        out_specs=VMEM,
        out_shape=pltpu.VMEM((cols, cells.shape[1]), jnp.bfloat16),
        compiler_params=PARAMS,
        name="columns_hot",
    )(cells)


def finish_kernel(rows, cols, line, cells, row_frac, col_frac, hot, *refs):
    basis, refs = refs[:ITERS], refs[ITERS:]
    latent, predictor, fine, parts, keep = refs
    wide = cols + LANES
    lat_in, good = coefficients(line[...])
    fine[...] = jnp.where(good, 1.0, 0.0)
    for k in range(ITERS):
        keep[k] = lat_in[k]
    tall = (rows + 2) * F
    lane = lax.broadcasted_iota(jnp.int32, (rows + 2, F, LANES), 2)

    def split(x, at, base):
        part = x.astype(jnp.bfloat16)
        rest = (x - part.astype(jnp.float32)).astype(jnp.bfloat16)
        parts[base : base + tall, at] = part.reshape(tall, LANES)
        parts[base + tall : base + 2 * tall, at] = rest.reshape(tall, LANES)

    def step(c, after):
        c = wide // LANES - 1 - c
        at = pl.ds(pl.multiple_of(c * LANES, LANES), LANES)
        total = None
        for k in range(ITERS):
            begin = PAD - SKIP * (k % 2)
            term = keep[k] * basis[k][begin : begin + rows + 1, :, at]
            total = term if total is None else total + term
        total = jnp.concatenate([total, jnp.zeros((1, F, LANES), jnp.float32)], axis=0)
        turned = pltpu.roll(total, LANES - 1, 2)

        @pl.when(c < cols // LANES)
        def _():
            split(total, at, 0)
            split(jnp.where(lane == LANES - 1, after, turned), at, 2 * tall)
            latent[:, :, at] = jnp.swapaxes(total[:rows], 0, 1)

        return turned

    lax.fori_loop(0, wide // LANES, step, jnp.zeros((rows + 2, F, LANES), jnp.float32))
    for c in range(0, cells.shape[1], CHUNK):
        at = slice(c, c + CHUNK)
        both = jnp.dot(parts[...], hot[:, at], preferred_element_type=jnp.float32)
        here = both[:tall] + both[tall : 2 * tall]
        beside = both[2 * tall : 3 * tall] + both[3 * tall :]
        row = cells[:, at] // cols
        frac = row_frac[:, at]
        low = jnp.zeros((F, CHUNK), jnp.float32)
        high = jnp.zeros((F, CHUNK), jnp.float32)
        for r in range(rows + 1):
            w = jnp.where(row == r, 1.0 - frac, jnp.where(row + 1 == r, frac, 0.0))
            low = low + w * here[r * F : (r + 1) * F]
            high = high + w * beside[r * F : (r + 1) * F]
        side = col_frac[:, at]
        out = (1.0 - side) * low + side * high
        for i in range(CHUNK // LANES):
            base = (c // LANES + i) * F
            predictor[base : base + F] = out[:, i * LANES : (i + 1) * LANES]


def finish(rows, cols, line, cells, row_frac, col_frac, hot, basis):
    f32 = jnp.float32
    wide = cols + LANES
    return pl.pallas_call(
        functools.partial(finish_kernel, rows, cols),
        in_specs=[VMEM] * (5 + ITERS),
        out_specs=[VMEM] * 3,
        out_shape=[
            jax.ShapeDtypeStruct((F, rows, cols), f32),
            jax.ShapeDtypeStruct((cells.shape[1] // LANES * F, LANES), f32),
            jax.ShapeDtypeStruct((F, LANES), f32),
        ],
        scratch_shapes=[
            pltpu.VMEM((4 * (rows + 2) * F, cols), jnp.bfloat16),
            pltpu.VMEM((ITERS, F, LANES), f32),
        ],
        compiler_params=PARAMS,
        name="finish",
    )(line, cells, row_frac, col_frac, *[held(x) for x in (hot, *basis)])


def extended(x, sides, width):
    for axis, dim in sides:
        size, length = (lax.axis_size(axis), x.shape[dim])
        up = [(i, (i + 1) % size) for i in range(size - 1)]
        down = [(j, i) for i, j in up]
        last = lax.slice_in_dim(x, length - width, length, axis=dim)
        leading = lax.slice_in_dim(x, 0, width, axis=dim)
        before = lax.ppermute(last, axis, up)
        after = lax.ppermute(leading, axis, down)
        x = jnp.concatenate([before, x, after], axis=dim)
    return x


def passed_along(x, axis, by):
    length = lax.axis_size(axis)
    pairs = [(i, i + by) for i in range(length) if 0 <= i + by < length]
    return lax.ppermute(x, axis, pairs)


def neighbours(padded):
    return padded[:, 2:, 1:-1] + padded[:, :-2, 1:-1] + padded[:, 1:-1, 2:] + padded[:, 1:-1, :-2]


def plain(right_side, kappa_field, tau_field, curvature, got_cells, got_row, got_col):
    def squares(values):
        return lax.psum(jnp.sum(values * values, axis=(1, 2)), ("tile", "field"))[:, None, None]

    def sweep(_, state):
        latent, residual, direction, norm_now = state
        padded = extended(direction, (("tile", 1), ("field", 2)), 1)
        scaled = tau_field * ((kappa_field + 4.0) * direction - neighbours(padded))
        spread = extended(scaled, (("tile", 1), ("field", 2)), 1)
        image = (kappa_field + 4.0) * scaled - neighbours(spread) + curvature * direction
        inner = lax.psum(jnp.sum(direction * image, axis=(1, 2)), ("tile", "field"))[:, None, None]
        alpha = norm_now / inner
        latent = latent + alpha * direction
        residual = residual - alpha * image
        norm_next = squares(residual)
        direction = residual + norm_next / norm_now * direction
        return latent, residual, direction, norm_next

    state = (jnp.zeros_like(right_side), right_side, right_side, squares(right_side))
    latent = lax.fori_loop(0, ITERS, sweep, state)[0]
    upper = passed_along(latent[:, :1, :], "tile", -1)
    tall = jnp.concatenate([latent, upper], axis=1)
    beside = passed_along(tall[:, :, :1], "field", -1)
    wide = jnp.concatenate([tall, beside], axis=2)
    columns = latent.shape[2]
    width = columns + 1
    flat = wide.reshape(wide.shape[0], -1)
    base = (got_cells // columns * width + got_cells % columns).astype(jnp.int32)

    def corner(offset):
        return jnp.take(flat, base + offset, axis=1)

    row_frac = got_row[None]
    col_frac = got_col[None]
    predictor = (
        (1.0 - row_frac) * (1.0 - col_frac) * corner(0)
        + row_frac * (1.0 - col_frac) * corner(width)
        + (1.0 - row_frac) * col_frac * corner(1)
        + row_frac * col_frac * corner(width + 1)
    )
    return latent, jnp.transpose(predictor, (1, 0, 2)).reshape(-1, predictor.shape[2])


def turned(x, axis, by):
    size = lax.axis_size(axis)
    return lax.ppermute(x, axis, [(i, (i + by) % size) for i in range(size)])


def summed(x, axis):
    size, stride = lax.axis_size(axis), 1
    while stride < size:
        if size // stride in (4, 16):
            for by in (1, -1):
                x = x + lax.ppermute(
                    x, axis, [(i, other(i, stride, by)) for i in range(size)]
                )
            stride *= 4
        else:
            x = x + lax.ppermute(x, axis, [(i, i ^ stride) for i in range(size)])
            stride *= 2
    return x


def other(i, stride, by):
    place = i // stride % 4
    partner = (place + (by if place % 2 == 0 else -by)) % 4
    return i + (partner - place) * stride


def local(
    right_side,
    kappa_field,
    tau_field,
    curvature,
    detect_prob,
    site_cells,
    site_offsets,
    site_count,
    visit_count,
    detections,
    surveyed,
):
    rows, cols = right_side.shape[1:]
    wide = cols + LANES
    tiles, bands = lax.axis_size("tile"), lax.axis_size("field")
    tile, band = lax.axis_index("tile"), lax.axis_index("field")
    flags = jnp.stack([band > 0, band < bands - 1, tile > 0, tile < tiles - 1]).astype(jnp.float32)
    lane = lax.broadcasted_iota(jnp.int32, (F, LANES), 1)
    mask = jnp.where(lane < SIDE, flags[1], jnp.where(lane >= LANES - SIDE, flags[0], 0.0))

    fields = (right_side, kappa_field, tau_field, curvature)
    cells = site_cells[0, 0]
    to_left, to_right, sent = columns_of(fields, cells, site_offsets[0, 0])
    from_right = turned(to_left, "field", -1)
    from_left = turned(to_right, "field", 1)
    got = lax.all_to_all(sent, "tile", split_axis=0, concat_axis=0, tiled=True)
    flags, got = lax.optimization_barrier((flags, got))
    got_cells = got[:, 0].astype(jnp.int32)
    got_row, got_col = got[:, 1], got[:, 2]
    sites = (got_cells.reshape(1, -1), got_row.reshape(1, -1), got_col.reshape(1, -1))
    *mains, to_up, to_down = prepare(flags, from_left, from_right, fields)
    common = (rows, cols, flags, mask)

    def exchanged(to_up, to_down):
        return turned(to_down, "tile", 1), turned(to_up, "tile", -1)

    up, down = exchanged(to_up, to_down)
    older, old, *coefs, own, to_up, to_down, part = phase(0, *common, up, down, mains)
    basis, sums = [older, old], [part]
    for p in range(1, ITERS // 2 - 1):
        up, down = exchanged(to_up, to_down)
        older, old, own, to_up, to_down, part = phase(p, *common, up, down, (own, *coefs, older, old))
        basis += [older, old]
        sums.append(part)
    up, down = exchanged(to_up, to_down)
    line, older, old = phase(ITERS // 2 - 1, *common, up, down, (own, *coefs, older, old), earlier=sums)
    basis += [older, old]

    line, got_cells = lax.optimization_barrier((line, got_cells))
    hot = columns_hot(got_cells.reshape(1, -1), cols)
    line = summed(summed(line, "field"), "tile")
    latent, predictor, fine = finish(rows, cols, line, *sites, hot, basis)
    latent, predictor, _ = lax.while_loop(
        lambda state: state[2],
        lambda state: plain(*fields, got_cells, got_row, got_col) + (False,),
        (latent, predictor, jnp.logical_not(jnp.all(fine > 0.5))),
    )
    predictor = predictor.reshape(tiles, F, LANES)
    returned = lax.all_to_all(predictor, "tile", split_axis=0, concat_axis=0, tiled=True)

    slots = lax.broadcasted_iota(jnp.int32, cells.shape, 1)
    live = (slots < site_count[0, 0][:, None]).astype(jnp.float32)[:, None, :]
    visits = visit_count[0, 0].astype(jnp.float32)[:, None, :]
    miss_prob = jnp.exp(visits * jnp.log(1.0 - detect_prob)[:, None])
    expo = jnp.exp(returned)
    seen_grad = 1.0 / (1.0 + expo)
    miss_grad = -(1.0 - miss_prob) * expo / ((1.0 + expo) * (1.0 + miss_prob * expo))
    site_grad = (
        jnp.where(detections[0, 0] > 0, seen_grad, miss_grad)
        * surveyed[0, 0].astype(jnp.float32)
        * live
    )
    return (latent, site_grad[None, None])


def solution(mesh):
    in_specs = (
        P(None, "tile", "field"),
        P(None, "tile", "field"),
        P(None, "tile", "field"),
        P(None, "tile", "field"),
        P(),
        P("tile", "field", None, None),
        P("tile", "field", None, None, None),
        P("tile", "field", None),
        P("tile", "field", None, None),
        P("tile", "field", None, None, None),
        P("tile", "field", None, None, None),
    )
    out_specs = (P(None, "tile", "field"), P("tile", "field", None, None, None))
    return jax.shard_map(local, mesh=mesh, in_specs=in_specs, out_specs=out_specs, check_vma=False)
```

```python
import functools

import jax
import jax.numpy as jnp
from jax import lax
from jax.experimental import pallas as pl
from jax.experimental.pallas import tpu as pltpu
from jax.sharding import PartitionSpec as P

ITERS = 8
F = 8
PAD = 4
SKIP = PAD - 1
SIDE = 16
LANES = 128
LOW, HIGH = 0.2, 15.0
MID, HALF = 0.5 * (HIGH + LOW), 0.5 * (HIGH - LOW)
VMEM = pl.BlockSpec(memory_space=pltpu.VMEM)
SMEM = pl.BlockSpec(memory_space=pltpu.SMEM)
HBM = pl.BlockSpec(memory_space=pl.ANY)
PARAMS = pltpu.CompilerParams(vmem_limit_bytes=12 * 1024 * 1024)


def held(x):
    return pltpu.with_memory_space_constraint(x, pltpu.VMEM)


def columns_kernel(*refs):
    firsts, lasts, (cells, offsets, to_left, to_right, sent) = refs[0:4], refs[4:8], refs[8:]
    for i in range(cells.shape[0]):
        sent[i, 0:1] = cells[i : i + 1].astype(jnp.float32)
        sent[i, 1:3] = offsets[i]
    lane = lax.broadcasted_iota(jnp.int32, (16, F, LANES), 2)
    for out, blocks, start in ((to_left, firsts, 0), (to_right, lasts, LANES - SIDE)):
        packed = jnp.zeros((16, F, LANES), jnp.float32)
        for a, ref in enumerate(blocks):
            block = jnp.swapaxes(ref[...], 0, 1)
            shift = (SIDE * a - start) % LANES
            moved = pltpu.roll(block, shift, 2) if shift else block
            mine = (lane >= SIDE * a) & (lane < SIDE * (a + 1))
            packed = jnp.where(mine, moved, packed)
        out[...] = packed


def columns_of(fields, cells, offsets):
    rows, cols = fields[0].shape[1:]
    first = pl.BlockSpec((F, rows, LANES), lambda i: (0, 0, 0))
    last = pl.BlockSpec((F, rows, LANES), lambda i: (0, 0, cols // LANES - 1))
    out = pl.BlockSpec((rows, F, LANES), lambda i: (0, 0, 0))
    shape = jax.ShapeDtypeStruct((rows, F, LANES), jnp.float32)
    sent = (cells.shape[0], 3, cells.shape[1])

    def whole(shape):
        return pl.BlockSpec(shape, lambda i: (0,) * len(shape))

    return pl.pallas_call(
        columns_kernel,
        grid=(1,),
        in_specs=[first] * 4 + [last] * 4 + [whole(cells.shape), whole(offsets.shape)],
        out_specs=[out, out, whole(sent)],
        out_shape=[shape, shape, jax.ShapeDtypeStruct(sent, jnp.float32)],
        name="columns",
    )(*fields, *fields, cells, offsets)


DEPTHS = (4, 3, 3, 2)


def shaped(a, x):
    if a == 1:
        return x + 4.0
    if a == 2:
        return x * (1.0 / HALF)
    if a == 3:
        return (x - MID) * (1.0 / HALF)
    return x


def extra_tile(a, flags, left, right):
    lane = lax.broadcasted_iota(jnp.int32, left.shape, 2)
    shift = (-SIDE * a) % LANES
    after = shaped(a, pltpu.roll(right[...], shift, 2) if shift else right[...])
    before = shaped(a, pltpu.roll(left[...], LANES - SIDE * (a + 1), 2))
    return jnp.where(lane < SIDE, after * flags[1], 0.0) + jnp.where(lane >= LANES - SIDE, before * flags[0], 0.0)


def prepare_kernel(flags, left, right, *refs):
    fields, outs, (to_up, to_down) = refs[0:4], refs[4:8], refs[8:]
    rows, cols = fields[0].shape[1:]

    def place(a, at, block):
        outs[a][:, :, at] = block
        base, depth = sum(DEPTHS[:a]), DEPTHS[a]
        to_up[base : base + depth, :, at] = block[:depth]
        to_down[base : base + depth, :, at] = block[rows - depth :]

    def step(c, carry):
        at = pl.ds(pl.multiple_of(c * LANES, LANES), LANES)
        for a in range(4):
            place(a, at, shaped(a, jnp.swapaxes(fields[a][:, :, at], 0, 1)))
        return carry

    lax.fori_loop(0, cols // LANES, step, 0, unroll=4)
    for a in range(4):
        place(a, slice(cols, cols + LANES), extra_tile(a, flags, left, right))


def prepare(flags, left, right, fields):
    rows, cols = fields[0].shape[1:]
    wide = cols + LANES
    f32 = jnp.float32
    return pl.pallas_call(
        prepare_kernel,
        in_specs=[SMEM] + [VMEM] * 6,
        out_specs=[VMEM] * 6,
        out_shape=[pltpu.VMEM((rows, F, wide), f32)] * 4 + [jax.ShapeDtypeStruct((sum(DEPTHS), F, wide), f32)] * 2,
        compiler_params=PARAMS,
        name="prepare",
    )(flags, left, right, *fields)


def walk(ref, r, count, wide):
    tiles = wide // LANES
    lane = lax.broadcasted_iota(jnp.int32, (F, LANES), 1)
    leftmost, rightmost = lane == 0, lane == LANES - 1

    def load(c):
        return [ref[r - 1 + i, :, c * LANES : (c + 1) * LANES] for i in range(count + 2)]

    def turn(tile, by):
        return [pltpu.roll(v, by, 1) for v in tile[1:-1]]

    now = load(0)
    before = turn([ref[r - 1 + i, :, wide - LANES :] for i in range(count + 2)], 1)
    right, left = turn(now, 1), turn(now, LANES - 1)
    start = left
    for c in range(tiles):
        after = load(c + 1) if c + 1 < tiles else None
        following = turn(after, LANES - 1) if after else start
        near = [
            (now[i] + now[i + 2])
            + (jnp.where(leftmost, before[i], right[i]) + jnp.where(rightmost, following[i], left[i]))
            for i in range(count)
        ]
        yield slice(c * LANES, (c + 1) * LANES), now[1:-1], near
        if after:
            before, right, left, now = right, turn(after, 1), following, after


def pairs(low, high, body, carry):
    return lax.fori_loop(0, (high - low) // 2, lambda i, carry: body(low + 2 * i, carry), carry, unroll=True)


class Rows:
    def __init__(self, ref, shift):
        self.ref, self.shift = ref, shift

    def __getitem__(self, key):
        return self.ref[(key[0] + self.shift, *key[1:])]

    def __setitem__(self, key, value):
        self.ref[(key[0] + self.shift, *key[1:])] = value


def rows_of(ref, shift):
    return None if ref is None else Rows(ref, shift)


INSIDE = dict(scale=[(1, 15)], first=[(2, 14)], again=[(3, 13)], second=[(4, 12)])
OUTSIDE = dict(
    scale=[(-3, 3), (13, 19)], first=[(0, 2), (14, 16)], again=[(-1, 5), (11, 17)], second=[(0, 4), (12, 16)]
)


def apply_twice(p, cols, where, ring, mask, current, kap, tau, cur, older, old, scaled, one, middle, newest):
    first, last = p == 0, p == ITERS // 2 - 1
    wide = cols + LANES
    zero = jnp.zeros((F, LANES), jnp.float32)

    def scale(ref, low, high):
        def body(r, carry):
            for at, v, near in walk(ref, r, 2, wide):
                for i in range(2):
                    scaled[r + i, :, at] = tau[r + i, :, at] * (kap[r + i, :, at] * v[i] - near[i])
            return carry

        pairs(low, high, body, 0)

    def image(ref, r):
        for at, s, near in walk(scaled, r, 2, wide):
            out = []
            for i in range(2):
                new = (kap[r + i, :, at] * s[i] - near[i]) + cur[r + i, :, at] * ref[r + i, :, at]
                out.append(new * mask[...] if at.start == cols else new)
            yield at, out

    for low, high in where["scale"]:
        scale(current, low, high)
    for r, flag, inner in ring:
        for at, new in image(current, r):
            for i in range(2):
                value = new[i] * flag
                one[r + i, :, at] = value
                if i == inner:
                    middle[r + i, :, at] = value if first else 2.0 * value - old[r + i, :, at]

    def first_rows(r, carry):
        cross = square = start = zero
        for at, new in image(current, r):
            for i in range(2):
                if not last:
                    one[r + i, :, at] = new[i]
                value = new[i] if first else 2.0 * new[i] - old[r + i, :, at]
                middle[r + i, :, at] = value
                if at.start < cols:
                    source = current[r + i, :, at]
                    cross += value * source
                    square += value * value
                    if first:
                        start += source * source
        out = (carry[0] + cross, carry[1] + square)
        return out + ((carry[2] + start,) if first else ())

    found = (zero,) * (3 if first else 2)
    for low, high in where["first"]:
        found = pairs(low, high, first_rows, found)

    if last:
        def final_rows(r, carry):
            total = zero
            for at, v, near in walk(middle, r, 2, wide):
                if at.start < cols:
                    for i in range(2):
                        k = kap[r + i, :, at] * v[i] - near[i]
                        total += tau[r + i, :, at] * k * k + cur[r + i, :, at] * v[i] * v[i]
            return carry + total

        total = zero
        for low, high in where["second"]:
            total = pairs(low, high, final_rows, total)
        return [*found, total]

    for low, high in where["again"]:
        scale(one, low, high)

    def second_rows(r, carry):
        cross = square = zero
        for at, new in image(one, r):
            for i in range(2):
                value = 2.0 * new[i] - current[r + i, :, at]
                if not first:
                    value = 2.0 * value - older[r + i, :, at]
                newest[r + i, :, at] = value
                if at.start < cols:
                    cross += value * middle[r + i, :, at]
                    square += value * value
        return carry[0] + cross, carry[1] + square

    more = (zero, zero)
    for low, high in where["second"]:
        more = pairs(low, high, second_rows, more)
    return [found[0], found[1], *more, *found[2:]]


def inside_kernel(p, cols, *refs):
    first, last = p == 0, p == ITERS // 2 - 1
    refs = list(refs)
    take = lambda n: [refs.pop(0) for _ in range(n)]
    mask, own, kap, tau, cur = take(5)
    older, old = (None, None) if first else take(2)
    shift = 0 if first else PAD
    coefs = [Rows(x, shift) for x in (kap, tau, cur)]
    older, old = rows_of(older, PAD), rows_of(old, 1)
    (middle,) = take(1)
    one, newest = (None, None) if last else take(2)
    sums, scaled = refs
    found = apply_twice(
        p, cols, INSIDE, (), mask, Rows(own, 0), *coefs, older, old, Rows(scaled, 0),
        rows_of(one, -2), Rows(middle, -2), rows_of(newest, -4),
    )
    for i, total in enumerate(found):
        sums[i] = total


def outside_kernel(p, rows, cols, *refs):
    first, last = p == 0, p == ITERS // 2 - 1
    refs = list(refs)
    take = lambda n: [refs.pop(0) for _ in range(n)]
    flags, mask, up, down, own, kap_in, tau_in, cur_in = take(8)
    older, old = (None, None) if first else take(2)
    (middle_in,) = take(1)
    one_in, newest_in = (None, None) if last else take(2)
    (part,) = take(1)
    if last:
        earlier = take(ITERS // 2 - 1)
        (line,) = take(1)
    current, middle = take(2)
    kap, tau, cur = take(3) if first else (kap_in, tau_in, cur_in)
    if not last:
        newest, to_up, to_down, sums = take(4)
    scaled, one = refs
    own_low, own_high = PAD, PAD + rows

    work = (current, kap, tau, cur)
    for a, source in enumerate((own, kap_in, tau_in, cur_in) if first else (own,)):
        work[a][own_low:own_high] = source[...]
    base = 0
    for a, depth in enumerate(DEPTHS if first else (up.shape[0],)):
        for i in range(depth):
            work[a][own_low - depth + i] = up[base + i] * flags[2]
            work[a][own_high + i] = down[base + i] * flags[3]
        base += depth
    middle[1 + 2 : 1 + rows - 2] = middle_in[...]
    if not last:
        one[own_low + 2 : own_low + 6] = one_in[:4]
        one[own_high - 6 : own_high - 2] = one_in[8:]
        newest[4 : rows - 4] = newest_in[...]

    found = apply_twice(
        p, cols, OUTSIDE, ((-2, flags[2], 1), (rows, flags[3], 0)), mask,
        *[Rows(x, PAD) for x in (current, kap, tau, cur)], rows_of(older, PAD), rows_of(old, 1),
        Rows(scaled, PAD), Rows(one, PAD), Rows(middle, 1), None if last else Rows(newest, 0),
    )
    found = [x + part[i] for i, x in enumerate(found)]
    if last:
        entries = [earlier[0][4]]
        for s in earlier:
            entries += [s[i] for i in range(4)]
        lane = lax.broadcasted_iota(jnp.int32, (F, LANES), 1)
        table = jnp.zeros((F, LANES), jnp.float32)
        for k, entry in enumerate(entries + found):
            table = jnp.where(lane == k, jnp.sum(entry, axis=1, keepdims=True), table)
        total = table[0:1]
        for f in range(1, F):
            total = total + pltpu.roll(table[f : f + 1], 2 * ITERS * f, 1)
        line[...] = total
        return
    for i, total in enumerate(found):
        sums[i] = total
    depth = to_up.shape[0]
    to_up[...] = newest[:depth]
    to_down[...] = newest[rows - depth :]


def phase(p, rows, cols, flags, mask, up, down, state, earlier=()):
    first, last = p == 0, p == ITERS // 2 - 1
    f32 = jnp.float32
    wide = cols + LANES
    ext = (rows + 2 * PAD, F, wide)
    state = [held(x) for x in state]
    counted = jax.ShapeDtypeStruct((5 if first else 3 if last else 4, F, LANES), f32)
    part_shape = [pltpu.VMEM((rows - 4, F, wide), f32)]
    if not last:
        part_shape += [pltpu.VMEM((rows - 4, F, wide), f32), pltpu.VMEM((rows - 8, F, wide), f32)]
    inside = pl.pallas_call(
        functools.partial(inside_kernel, p, cols),
        in_specs=[VMEM] * (1 + len(state)),
        out_specs=[VMEM] * (len(part_shape) + 1),
        out_shape=part_shape + [counted],
        scratch_shapes=[pltpu.VMEM((rows, F, wide), f32)],
        compiler_params=PARAMS,
        cost_estimate=pl.CostEstimate(flops=100_000_000, bytes_accessed=8_000_000, transcendentals=0),
        name=f"inside{p}",
    )(mask, *state)
    out_shape = [pltpu.VMEM(ext, f32), pltpu.VMEM((rows + 2, F, wide), f32)]
    if first:
        out_shape += [pltpu.VMEM(ext, f32)] * 3
    if last:
        out_shape = [jax.ShapeDtypeStruct((1, LANES), f32)] + out_shape
    else:
        out_shape += [pltpu.VMEM((rows, F, wide), f32)]
        depth = PAD - 1 if p == ITERS // 2 - 2 else PAD
        out_shape += [jax.ShapeDtypeStruct((depth, F, wide), f32)] * 2 + [counted]
    return pl.pallas_call(
        functools.partial(outside_kernel, p, rows, cols),
        in_specs=[SMEM] + [VMEM] * (3 + len(state) + len(inside) + len(earlier)),
        out_specs=[VMEM] * len(out_shape),
        out_shape=out_shape,
        scratch_shapes=[pltpu.VMEM(ext, f32), pltpu.VMEM(ext, f32)],
        compiler_params=PARAMS,
        name=f"outside{p}",
    )(flags, mask, up, down, *state, *[held(x) for x in inside[:-1]], inside[-1], *earlier)


def coefficients(line):
    raw = [jnp.sum(jnp.where(lax.broadcasted_iota(jnp.int32, (F, LANES), 1)
                             == 2 * ITERS * lax.broadcasted_iota(jnp.int32, (F, LANES), 0) + k,
                             jnp.broadcast_to(line, (F, LANES)), 0.0), axis=1, keepdims=True)
           for k in range(2 * ITERS)]
    raw = [jnp.broadcast_to(v, (F, LANES)) for v in raw]
    m = [raw[0], raw[1]] + [2.0 * raw[k] - raw[k % 2] for k in range(2, 2 * ITERS - 1)]
    m.append(4.0 * raw[2 * ITERS - 1] - m[2 * ITERS - 3] - 2.0 * m[1])
    zero = jnp.zeros((F, LANES), jnp.float32)
    one = jnp.ones((F, LANES), jnp.float32)

    def moved(v):
        out = [MID * e for e in v] + [zero]
        out[1] = out[1] + HALF * v[0]
        for k in range(1, len(v)):
            out[k - 1] = out[k - 1] + 0.5 * HALF * v[k]
            out[k + 1] = out[k + 1] + 0.5 * HALF * v[k]
        return out

    def against(v, l):
        return MID * v[l] + 0.5 * HALF * (v[l + 1] + v[abs(l - 1)])

    res, way = list(m), list(m)
    res_in, way_in, lat_in = [one], [one], [zero] * ITERS
    lead = one
    now = m[0]
    pivots = []
    for it in range(ITERS):
        image = [against(way, l) for l in range(len(way) - 1)]
        alpha = now / (lead * image[it])
        for k in range(it + 1):
            lat_in[k] = lat_in[k] + alpha * way_in[k]
        if it == ITERS - 1:
            break
        res = [res[l] - alpha * image[l] for l in range(len(image))]
        step = moved(way_in)
        res_in = [a - alpha * b for a, b in zip(res_in + [zero], step)]
        lead = res_in[it + 1]
        new = lead * res[it + 1]
        pivots.append(res[it + 1] / (lead * m[0]))
        beta = new / now
        way = [res[l] + beta * way[l] for l in range(len(res))]
        way_in = [a + beta * b for a, b in zip(res_in, way_in + [zero])]
        now = new
    fine = pivots[-1] >= 0.3 * pivots[0]
    for pivot in pivots:
        fine = fine & (pivot >= 5e-3) & (pivot <= 20.0)
    return lat_in, fine


CHUNK = 4 * LANES


def columns_hot_kernel(cols, cells, hot):
    col = lax.rem(cells[...], cols)

    def step(b, carry):
        at = pl.ds(pl.multiple_of(b * LANES, LANES), LANES)
        row = lax.broadcasted_iota(jnp.int32, (LANES, cells.shape[1]), 0) + b * LANES
        hot[at] = jnp.where(row == col, 1.0, 0.0).astype(jnp.bfloat16)
        return carry

    lax.fori_loop(0, hot.shape[0] // LANES, step, 0)


def columns_hot(cells, cols):
    return pl.pallas_call(
        functools.partial(columns_hot_kernel, cols),
        in_specs=[VMEM],
        out_specs=VMEM,
        out_shape=pltpu.VMEM((cols, cells.shape[1]), jnp.bfloat16),
        compiler_params=PARAMS,
        name="columns_hot",
    )(cells)


def finish_kernel(rows, cols, line, cells, row_frac, col_frac, hot, *refs):
    basis, refs = refs[:ITERS], refs[ITERS:]
    latent, predictor, fine, parts, keep, laid, sent = refs
    lat_in, good = coefficients(line[...])
    fine[...] = jnp.where(good, 1.0, 0.0)
    for k in range(ITERS):
        keep[k] = lat_in[k]
    tall = (rows + 2) * F
    lane = lax.broadcasted_iota(jnp.int32, (rows + 2, F, LANES), 2)

    def split(x, at, base):
        part = x.astype(jnp.bfloat16)
        rest = (x - part.astype(jnp.float32)).astype(jnp.bfloat16)
        parts[base : base + tall, at] = part.reshape(tall, LANES)
        parts[base + tall : base + 2 * tall, at] = rest.reshape(tall, LANES)

    def combined(at):
        total = None
        for k in range(ITERS):
            begin = PAD - SKIP * (k % 2)
            term = keep[k] * basis[k][begin : begin + rows + 1, :, at]
            total = term if total is None else total + term
        return jnp.concatenate([total, jnp.zeros((1, F, LANES), jnp.float32)], axis=0)

    def step(c, after):
        at = pl.ds(pl.multiple_of((cols // LANES - 1 - c) * LANES, LANES), LANES)
        total = combined(at)
        turned = pltpu.roll(total, LANES - 1, 2)
        split(total, at, 0)
        split(jnp.where(lane == LANES - 1, after, turned), at, 2 * tall)
        laid[:, :, at] = jnp.swapaxes(total[:rows], 0, 1)
        return turned

    beyond = pltpu.roll(combined(slice(cols, cols + LANES)), LANES - 1, 2)
    lax.fori_loop(0, cols // LANES, step, beyond, unroll=2)
    copy = pltpu.make_async_copy(laid, latent, sent)
    copy.start()
    for c in range(0, cells.shape[1], CHUNK):
        at = slice(c, c + CHUNK)
        both = jnp.dot(parts[...], hot[:, at], preferred_element_type=jnp.float32)
        here = both[:tall] + both[tall : 2 * tall]
        beside = both[2 * tall : 3 * tall] + both[3 * tall :]
        row = cells[:, at] // cols
        frac = row_frac[:, at]
        low = jnp.zeros((F, CHUNK), jnp.float32)
        high = jnp.zeros((F, CHUNK), jnp.float32)
        for r in range(rows + 1):
            w = jnp.where(row == r, 1.0 - frac, jnp.where(row + 1 == r, frac, 0.0))
            low = low + w * here[r * F : (r + 1) * F]
            high = high + w * beside[r * F : (r + 1) * F]
        side = col_frac[:, at]
        out = (1.0 - side) * low + side * high
        for i in range(CHUNK // LANES):
            base = (c // LANES + i) * F
            predictor[base : base + F] = out[:, i * LANES : (i + 1) * LANES]
    copy.wait()


def finish(rows, cols, line, cells, row_frac, col_frac, hot, basis):
    f32 = jnp.float32
    return pl.pallas_call(
        functools.partial(finish_kernel, rows, cols),
        in_specs=[VMEM] * (5 + ITERS),
        out_specs=[HBM, VMEM, VMEM],
        out_shape=[
            pltpu.HBM((F, rows, cols), f32),
            jax.ShapeDtypeStruct((cells.shape[1] // LANES * F, LANES), f32),
            jax.ShapeDtypeStruct((F, LANES), f32),
        ],
        scratch_shapes=[
            pltpu.VMEM((4 * (rows + 2) * F, cols), jnp.bfloat16),
            pltpu.VMEM((ITERS, F, LANES), f32),
            pltpu.VMEM((F, rows, cols), f32),
            pltpu.SemaphoreType.DMA,
        ],
        compiler_params=PARAMS,
        name="finish",
    )(line, cells, row_frac, col_frac, *[held(x) for x in (hot, *basis)])


def extended(x, sides, width):
    for axis, dim in sides:
        size, length = (lax.axis_size(axis), x.shape[dim])
        up = [(i, (i + 1) % size) for i in range(size - 1)]
        down = [(j, i) for i, j in up]
        last = lax.slice_in_dim(x, length - width, length, axis=dim)
        leading = lax.slice_in_dim(x, 0, width, axis=dim)
        before = lax.ppermute(last, axis, up)
        after = lax.ppermute(leading, axis, down)
        x = jnp.concatenate([before, x, after], axis=dim)
    return x


def passed_along(x, axis, by):
    length = lax.axis_size(axis)
    pairs = [(i, i + by) for i in range(length) if 0 <= i + by < length]
    return lax.ppermute(x, axis, pairs)


def neighbours(padded):
    return padded[:, 2:, 1:-1] + padded[:, :-2, 1:-1] + padded[:, 1:-1, 2:] + padded[:, 1:-1, :-2]


def plain(right_side, kappa_field, tau_field, curvature, got_cells, got_row, got_col):
    def squares(values):
        return lax.psum(jnp.sum(values * values, axis=(1, 2)), ("tile", "field"))[:, None, None]

    def sweep(_, state):
        latent, residual, direction, norm_now = state
        padded = extended(direction, (("tile", 1), ("field", 2)), 1)
        scaled = tau_field * ((kappa_field + 4.0) * direction - neighbours(padded))
        spread = extended(scaled, (("tile", 1), ("field", 2)), 1)
        image = (kappa_field + 4.0) * scaled - neighbours(spread) + curvature * direction
        inner = lax.psum(jnp.sum(direction * image, axis=(1, 2)), ("tile", "field"))[:, None, None]
        alpha = norm_now / inner
        latent = latent + alpha * direction
        residual = residual - alpha * image
        norm_next = squares(residual)
        direction = residual + norm_next / norm_now * direction
        return latent, residual, direction, norm_next

    state = (jnp.zeros_like(right_side), right_side, right_side, squares(right_side))
    latent = lax.fori_loop(0, ITERS, sweep, state)[0]
    upper = passed_along(latent[:, :1, :], "tile", -1)
    tall = jnp.concatenate([latent, upper], axis=1)
    beside = passed_along(tall[:, :, :1], "field", -1)
    wide = jnp.concatenate([tall, beside], axis=2)
    columns = latent.shape[2]
    width = columns + 1
    flat = wide.reshape(wide.shape[0], -1)
    base = (got_cells // columns * width + got_cells % columns).astype(jnp.int32)

    def corner(offset):
        return jnp.take(flat, base + offset, axis=1)

    row_frac = got_row[None]
    col_frac = got_col[None]
    predictor = (
        (1.0 - row_frac) * (1.0 - col_frac) * corner(0)
        + row_frac * (1.0 - col_frac) * corner(width)
        + (1.0 - row_frac) * col_frac * corner(1)
        + row_frac * col_frac * corner(width + 1)
    )
    return latent, jnp.transpose(predictor, (1, 0, 2)).reshape(-1, predictor.shape[2])


def turned(x, axis, by):
    size = lax.axis_size(axis)
    return lax.ppermute(x, axis, [(i, (i + by) % size) for i in range(size)])


def summed(x, axis):
    size, stride = lax.axis_size(axis), 1
    while stride < size:
        if size // stride in (4, 16):
            for by in (1, -1):
                x = x + lax.ppermute(
                    x, axis, [(i, other(i, stride, by)) for i in range(size)]
                )
            stride *= 4
        else:
            x = x + lax.ppermute(x, axis, [(i, i ^ stride) for i in range(size)])
            stride *= 2
    return x


def other(i, stride, by):
    place = i // stride % 4
    partner = (place + (by if place % 2 == 0 else -by)) % 4
    return i + (partner - place) * stride


def local(
    right_side,
    kappa_field,
    tau_field,
    curvature,
    detect_prob,
    site_cells,
    site_offsets,
    site_count,
    visit_count,
    detections,
    surveyed,
):
    rows, cols = right_side.shape[1:]
    wide = cols + LANES
    tiles, bands = lax.axis_size("tile"), lax.axis_size("field")
    tile, band = lax.axis_index("tile"), lax.axis_index("field")
    flags = jnp.stack([band > 0, band < bands - 1, tile > 0, tile < tiles - 1]).astype(jnp.float32)
    lane = lax.broadcasted_iota(jnp.int32, (F, LANES), 1)
    mask = jnp.where(lane < SIDE, flags[1], jnp.where(lane >= LANES - SIDE, flags[0], 0.0))

    fields = (right_side, kappa_field, tau_field, curvature)
    cells = site_cells[0, 0]
    to_left, to_right, sent = columns_of(fields, cells, site_offsets[0, 0])
    from_right = turned(to_left, "field", -1)
    from_left = turned(to_right, "field", 1)
    got = lax.all_to_all(sent, "tile", split_axis=0, concat_axis=0, tiled=True)
    flags, got = lax.optimization_barrier((flags, got))
    got_cells = got[:, 0].astype(jnp.int32)
    got_row, got_col = got[:, 1], got[:, 2]
    sites = (got_cells.reshape(1, -1), got_row.reshape(1, -1), got_col.reshape(1, -1))
    *mains, to_up, to_down = prepare(flags, from_left, from_right, fields)
    common = (rows, cols, flags, mask)

    def exchanged(to_up, to_down):
        return turned(to_down, "tile", 1), turned(to_up, "tile", -1)

    up, down = exchanged(to_up, to_down)
    older, old, *coefs, own, to_up, to_down, part = phase(0, *common, up, down, mains)
    basis, sums = [older, old], [part]
    for p in range(1, ITERS // 2 - 1):
        up, down = exchanged(to_up, to_down)
        older, old, own, to_up, to_down, part = phase(p, *common, up, down, (own, *coefs, older, old))
        basis += [older, old]
        sums.append(part)
    up, down = exchanged(to_up, to_down)
    line, older, old = phase(ITERS // 2 - 1, *common, up, down, (own, *coefs, older, old), earlier=sums)
    basis += [older, old]

    line, got_cells = lax.optimization_barrier((line, got_cells))
    hot = columns_hot(got_cells.reshape(1, -1), cols)
    line = summed(line, "field")
    line, hot = lax.optimization_barrier((line, hot))
    line = summed(line, "tile")
    latent, predictor, fine = finish(rows, cols, line, *sites, hot, basis)
    latent, predictor, _ = lax.while_loop(
        lambda state: state[2],
        lambda state: plain(*fields, got_cells, got_row, got_col) + (False,),
        (latent, predictor, jnp.logical_not(jnp.all(fine > 0.5))),
    )
    predictor = predictor.reshape(tiles, F, LANES)
    returned = lax.all_to_all(predictor, "tile", split_axis=0, concat_axis=0, tiled=True)

    slots = lax.broadcasted_iota(jnp.int32, cells.shape, 1)
    live = (slots < site_count[0, 0][:, None]).astype(jnp.float32)[:, None, :]
    visits = visit_count[0, 0].astype(jnp.float32)[:, None, :]
    miss_prob = jnp.exp(visits * jnp.log(1.0 - detect_prob)[:, None])
    expo = jnp.exp(returned)
    seen_grad = 1.0 / (1.0 + expo)
    miss_grad = -(1.0 - miss_prob) * expo / ((1.0 + expo) * (1.0 + miss_prob * expo))
    site_grad = (
        jnp.where(detections[0, 0] > 0, seen_grad, miss_grad)
        * surveyed[0, 0].astype(jnp.float32)
        * live
    )
    return (latent, site_grad[None, None])


def solution(mesh):
    in_specs = (
        P(None, "tile", "field"),
        P(None, "tile", "field"),
        P(None, "tile", "field"),
        P(None, "tile", "field"),
        P(),
        P("tile", "field", None, None),
        P("tile", "field", None, None, None),
        P("tile", "field", None),
        P("tile", "field", None, None),
        P("tile", "field", None, None, None),
        P("tile", "field", None, None, None),
    )
    out_specs = (P(None, "tile", "field"), P("tile", "field", None, None, None))
    return jax.shard_map(local, mesh=mesh, in_specs=in_specs, out_specs=out_specs, check_vma=False)
```

```python
import functools

import jax
import jax.numpy as jnp
from jax import lax
from jax.experimental import pallas as pl
from jax.experimental.pallas import tpu as pltpu
from jax.sharding import PartitionSpec as P

ITERS = 8
F = 8
PAD = 4
SKIP = PAD - 1
SIDE = 16
LANES = 128
LOW, HIGH = 0.2, 15.0
MID, HALF = 0.5 * (HIGH + LOW), 0.5 * (HIGH - LOW)
VMEM = pl.BlockSpec(memory_space=pltpu.VMEM)
SMEM = pl.BlockSpec(memory_space=pltpu.SMEM)
HBM = pl.BlockSpec(memory_space=pl.ANY)
PARAMS = pltpu.CompilerParams(vmem_limit_bytes=12 * 1024 * 1024)


def held(x):
    return pltpu.with_memory_space_constraint(x, pltpu.VMEM)


def columns_kernel(*refs):
    firsts, lasts, (cells, offsets, to_left, to_right, sent) = refs[0:4], refs[4:8], refs[8:]
    for i in range(cells.shape[0]):
        sent[i, 0:1] = cells[i : i + 1].astype(jnp.float32)
        sent[i, 1:3] = offsets[i]
    lane = lax.broadcasted_iota(jnp.int32, (16, F, LANES), 2)
    for out, blocks, start in ((to_left, firsts, 0), (to_right, lasts, LANES - SIDE)):
        packed = jnp.zeros((16, F, LANES), jnp.float32)
        for a, ref in enumerate(blocks):
            block = jnp.swapaxes(ref[...], 0, 1)
            shift = (SIDE * a - start) % LANES
            moved = pltpu.roll(block, shift, 2) if shift else block
            mine = (lane >= SIDE * a) & (lane < SIDE * (a + 1))
            packed = jnp.where(mine, moved, packed)
        out[...] = packed


def columns_of(fields, cells, offsets):
    rows, cols = fields[0].shape[1:]
    first = pl.BlockSpec((F, rows, LANES), lambda i: (0, 0, 0))
    last = pl.BlockSpec((F, rows, LANES), lambda i: (0, 0, cols // LANES - 1))
    out = pl.BlockSpec((rows, F, LANES), lambda i: (0, 0, 0))
    shape = jax.ShapeDtypeStruct((rows, F, LANES), jnp.float32)
    sent = (cells.shape[0], 3, cells.shape[1])

    def whole(shape):
        return pl.BlockSpec(shape, lambda i: (0,) * len(shape))

    return pl.pallas_call(
        columns_kernel,
        grid=(1,),
        in_specs=[first] * 4 + [last] * 4 + [whole(cells.shape), whole(offsets.shape)],
        out_specs=[out, out, whole(sent)],
        out_shape=[shape, shape, jax.ShapeDtypeStruct(sent, jnp.float32)],
        name="columns",
    )(*fields, *fields, cells, offsets)


DEPTHS = (4, 3, 3, 2)


def shaped(a, x):
    if a == 1:
        return x + 4.0
    if a == 2:
        return x * (1.0 / HALF)
    if a == 3:
        return (x - MID) * (1.0 / HALF)
    return x


def extra_tile(a, flags, left, right):
    lane = lax.broadcasted_iota(jnp.int32, left.shape, 2)
    shift = (-SIDE * a) % LANES
    after = shaped(a, pltpu.roll(right[...], shift, 2) if shift else right[...])
    before = shaped(a, pltpu.roll(left[...], LANES - SIDE * (a + 1), 2))
    return jnp.where(lane < SIDE, after * flags[1], 0.0) + jnp.where(lane >= LANES - SIDE, before * flags[0], 0.0)


def prepare_kernel(flags, left, right, *refs):
    fields, outs, (to_up, to_down) = refs[0:4], refs[4:8], refs[8:]
    rows, cols = fields[0].shape[1:]

    def place(a, at, block):
        outs[a][:, :, at] = block
        base, depth = sum(DEPTHS[:a]), DEPTHS[a]
        to_up[base : base + depth, :, at] = block[:depth]
        to_down[base : base + depth, :, at] = block[rows - depth :]

    def step(c, carry):
        at = pl.ds(pl.multiple_of(c * LANES, LANES), LANES)
        for a in range(4):
            place(a, at, shaped(a, jnp.swapaxes(fields[a][:, :, at], 0, 1)))
        return carry

    lax.fori_loop(0, cols // LANES, step, 0, unroll=4)
    for a in range(4):
        place(a, slice(cols, cols + LANES), extra_tile(a, flags, left, right))


def prepare(flags, left, right, fields):
    rows, cols = fields[0].shape[1:]
    wide = cols + LANES
    f32 = jnp.float32
    return pl.pallas_call(
        prepare_kernel,
        in_specs=[SMEM] + [VMEM] * 6,
        out_specs=[VMEM] * 6,
        out_shape=[pltpu.VMEM((rows, F, wide), f32)] * 4 + [jax.ShapeDtypeStruct((sum(DEPTHS), F, wide), f32)] * 2,
        compiler_params=PARAMS,
        name="prepare",
    )(flags, left, right, *fields)


def walk(ref, r, count, wide):
    tiles = wide // LANES
    lane = lax.broadcasted_iota(jnp.int32, (F, LANES), 1)
    leftmost, rightmost = lane == 0, lane == LANES - 1

    def load(c):
        return [ref[r - 1 + i, :, c * LANES : (c + 1) * LANES] for i in range(count + 2)]

    def turn(tile, by):
        return [pltpu.roll(v, by, 1) for v in tile[1:-1]]

    now = load(0)
    before = turn([ref[r - 1 + i, :, wide - LANES :] for i in range(count + 2)], 1)
    right, left = turn(now, 1), turn(now, LANES - 1)
    start = left
    for c in range(tiles):
        after = load(c + 1) if c + 1 < tiles else None
        following = turn(after, LANES - 1) if after else start
        near = [
            (now[i] + now[i + 2])
            + (jnp.where(leftmost, before[i], right[i]) + jnp.where(rightmost, following[i], left[i]))
            for i in range(count)
        ]
        yield slice(c * LANES, (c + 1) * LANES), now[1:-1], near
        if after:
            before, right, left, now = right, turn(after, 1), following, after


def pairs(low, high, body, carry):
    return lax.fori_loop(0, (high - low) // 2, lambda i, carry: body(low + 2 * i, carry), carry, unroll=True)


class Rows:
    def __init__(self, ref, shift):
        self.ref, self.shift = ref, shift

    def __getitem__(self, key):
        return self.ref[(key[0] + self.shift, *key[1:])]

    def __setitem__(self, key, value):
        self.ref[(key[0] + self.shift, *key[1:])] = value


def rows_of(ref, shift):
    return None if ref is None else Rows(ref, shift)


INSIDE = dict(scale=[(1, 15)], first=[(2, 14)], again=[(3, 13)], second=[(4, 12)])
OUTSIDE = dict(
    scale=[(-3, 3), (13, 19)], first=[(0, 2), (14, 16)], again=[(-1, 5), (11, 17)], second=[(0, 4), (12, 16)]
)


def apply_twice(p, cols, where, ring, mask, current, kap, tau, cur, older, old, scaled, one, middle, newest):
    first, last = p == 0, p == ITERS // 2 - 1
    wide = cols + LANES
    zero = jnp.zeros((F, LANES), jnp.float32)

    def scale(ref, low, high):
        def body(r, carry):
            for at, v, near in walk(ref, r, 2, wide):
                for i in range(2):
                    scaled[r + i, :, at] = tau[r + i, :, at] * (kap[r + i, :, at] * v[i] - near[i])
            return carry

        pairs(low, high, body, 0)

    def image(ref, r):
        for at, s, near in walk(scaled, r, 2, wide):
            out = []
            for i in range(2):
                new = (kap[r + i, :, at] * s[i] - near[i]) + cur[r + i, :, at] * ref[r + i, :, at]
                out.append(new * mask[...] if at.start == cols else new)
            yield at, out

    for low, high in where["scale"]:
        scale(current, low, high)
    for r, flag, inner in ring:
        for at, new in image(current, r):
            for i in range(2):
                value = new[i] * flag
                one[r + i, :, at] = value
                if i == inner:
                    middle[r + i, :, at] = value if first else 2.0 * value - old[r + i, :, at]

    def first_rows(r, carry):
        cross = square = start = zero
        for at, new in image(current, r):
            for i in range(2):
                if not last:
                    one[r + i, :, at] = new[i]
                value = new[i] if first else 2.0 * new[i] - old[r + i, :, at]
                middle[r + i, :, at] = value
                if at.start < cols:
                    source = current[r + i, :, at]
                    cross += value * source
                    square += value * value
                    if first:
                        start += source * source
        out = (carry[0] + cross, carry[1] + square)
        return out + ((carry[2] + start,) if first else ())

    found = (zero,) * (3 if first else 2)
    for low, high in where["first"]:
        found = pairs(low, high, first_rows, found)

    if last:
        def final_rows(r, carry):
            total = zero
            for at, v, near in walk(middle, r, 2, wide):
                if at.start < cols:
                    for i in range(2):
                        k = kap[r + i, :, at] * v[i] - near[i]
                        total += tau[r + i, :, at] * k * k + cur[r + i, :, at] * v[i] * v[i]
            return carry + total

        total = zero
        for low, high in where["second"]:
            total = pairs(low, high, final_rows, total)
        return [*found, total]

    for low, high in where["again"]:
        scale(one, low, high)

    def second_rows(r, carry):
        cross = square = zero
        for at, new in image(one, r):
            for i in range(2):
                value = 2.0 * new[i] - current[r + i, :, at]
                if not first:
                    value = 2.0 * value - older[r + i, :, at]
                newest[r + i, :, at] = value
                if at.start < cols:
                    cross += value * middle[r + i, :, at]
                    square += value * value
        return carry[0] + cross, carry[1] + square

    more = (zero, zero)
    for low, high in where["second"]:
        more = pairs(low, high, second_rows, more)
    return [found[0], found[1], *more, *found[2:]]


def inside_kernel(p, cols, *refs):
    first, last = p == 0, p == ITERS // 2 - 1
    refs = list(refs)
    take = lambda n: [refs.pop(0) for _ in range(n)]
    mask, own, kap, tau, cur = take(5)
    older, old = (None, None) if first else take(2)
    shift = 0 if first else PAD
    coefs = [Rows(x, shift) for x in (kap, tau, cur)]
    older, old = rows_of(older, PAD), rows_of(old, 1)
    (middle,) = take(1)
    one, newest = (None, None) if last else take(2)
    sums, scaled = refs
    found = apply_twice(
        p, cols, INSIDE, (), mask, Rows(own, 0), *coefs, older, old, Rows(scaled, 0),
        rows_of(one, -2), Rows(middle, -2), rows_of(newest, -4),
    )
    for i, total in enumerate(found):
        sums[i] = total


def outside_kernel(p, rows, cols, *refs):
    first, last = p == 0, p == ITERS // 2 - 1
    refs = list(refs)
    take = lambda n: [refs.pop(0) for _ in range(n)]
    flags, mask, up, down, own, kap_in, tau_in, cur_in = take(8)
    older, old = (None, None) if first else take(2)
    (middle_in,) = take(1)
    one_in, newest_in = (None, None) if last else take(2)
    (part,) = take(1)
    if last:
        earlier = take(ITERS // 2 - 1)
        (line,) = take(1)
    current, middle = take(2)
    kap, tau, cur = take(3) if first else (kap_in, tau_in, cur_in)
    if not last:
        newest, to_up, to_down, sums = take(4)
    scaled, one = refs
    own_low, own_high = PAD, PAD + rows

    work = (current, kap, tau, cur)
    for a, source in enumerate((own, kap_in, tau_in, cur_in) if first else (own,)):
        work[a][own_low:own_high] = source[...]
    base = 0
    for a, depth in enumerate(DEPTHS if first else (up.shape[0],)):
        for i in range(depth):
            work[a][own_low - depth + i] = up[base + i] * flags[2]
            work[a][own_high + i] = down[base + i] * flags[3]
        base += depth
    middle[1 + 2 : 1 + rows - 2] = middle_in[...]
    if not last:
        one[own_low + 2 : own_low + 6] = one_in[:4]
        one[own_high - 6 : own_high - 2] = one_in[8:]
        newest[4 : rows - 4] = newest_in[...]

    found = apply_twice(
        p, cols, OUTSIDE, ((-2, flags[2], 1), (rows, flags[3], 0)), mask,
        *[Rows(x, PAD) for x in (current, kap, tau, cur)], rows_of(older, PAD), rows_of(old, 1),
        Rows(scaled, PAD), Rows(one, PAD), Rows(middle, 1), None if last else Rows(newest, 0),
    )
    found = [x + part[i] for i, x in enumerate(found)]
    if last:
        entries = [earlier[0][4]]
        for s in earlier:
            entries += [s[i] for i in range(4)]
        lane = lax.broadcasted_iota(jnp.int32, (F, LANES), 1)
        table = jnp.zeros((F, LANES), jnp.float32)
        for k, entry in enumerate(entries + found):
            table = jnp.where(lane == k, jnp.sum(entry, axis=1, keepdims=True), table)
        total = table[0:1]
        for f in range(1, F):
            total = total + pltpu.roll(table[f : f + 1], 2 * ITERS * f, 1)
        line[...] = total
        return
    for i, total in enumerate(found):
        sums[i] = total
    depth = to_up.shape[0]
    to_up[...] = newest[:depth]
    to_down[...] = newest[rows - depth :]


def phase(p, rows, cols, flags, mask, up, down, state, earlier=()):
    first, last = p == 0, p == ITERS // 2 - 1
    f32 = jnp.float32
    wide = cols + LANES
    ext = (rows + 2 * PAD, F, wide)
    state = [held(x) for x in state]
    counted = jax.ShapeDtypeStruct((5 if first else 3 if last else 4, F, LANES), f32)
    part_shape = [pltpu.VMEM((rows - 4, F, wide), f32)]
    if not last:
        part_shape += [pltpu.VMEM((rows - 4, F, wide), f32), pltpu.VMEM((rows - 8, F, wide), f32)]
    inside = pl.pallas_call(
        functools.partial(inside_kernel, p, cols),
        in_specs=[VMEM] * (1 + len(state)),
        out_specs=[VMEM] * (len(part_shape) + 1),
        out_shape=part_shape + [counted],
        scratch_shapes=[pltpu.VMEM((rows, F, wide), f32)],
        compiler_params=PARAMS,
        cost_estimate=pl.CostEstimate(flops=100_000_000, bytes_accessed=8_000_000, transcendentals=0),
        name=f"inside{p}",
    )(mask, *state)
    out_shape = [pltpu.VMEM(ext, f32), pltpu.VMEM((rows + 2, F, wide), f32)]
    if first:
        out_shape += [pltpu.VMEM(ext, f32)] * 3
    if last:
        out_shape = [jax.ShapeDtypeStruct((1, LANES), f32)] + out_shape
    else:
        out_shape += [pltpu.VMEM((rows, F, wide), f32)]
        depth = PAD - 1 if p == ITERS // 2 - 2 else PAD
        out_shape += [jax.ShapeDtypeStruct((depth, F, wide), f32)] * 2 + [counted]
    return pl.pallas_call(
        functools.partial(outside_kernel, p, rows, cols),
        in_specs=[SMEM] + [VMEM] * (3 + len(state) + len(inside) + len(earlier)),
        out_specs=[VMEM] * len(out_shape),
        out_shape=out_shape,
        scratch_shapes=[pltpu.VMEM(ext, f32), pltpu.VMEM(ext, f32)],
        compiler_params=PARAMS,
        name=f"outside{p}",
    )(flags, mask, up, down, *state, *[held(x) for x in inside[:-1]], inside[-1], *earlier)


def coefficients(line):
    raw = [jnp.sum(jnp.where(lax.broadcasted_iota(jnp.int32, (F, LANES), 1)
                             == 2 * ITERS * lax.broadcasted_iota(jnp.int32, (F, LANES), 0) + k,
                             jnp.broadcast_to(line, (F, LANES)), 0.0), axis=1, keepdims=True)
           for k in range(2 * ITERS)]
    raw = [jnp.broadcast_to(v, (F, LANES)) for v in raw]
    m = [raw[0], raw[1]] + [2.0 * raw[k] - raw[k % 2] for k in range(2, 2 * ITERS - 1)]
    m.append(4.0 * raw[2 * ITERS - 1] - m[2 * ITERS - 3] - 2.0 * m[1])
    zero = jnp.zeros((F, LANES), jnp.float32)
    one = jnp.ones((F, LANES), jnp.float32)

    def moved(v):
        out = [MID * e for e in v] + [zero]
        out[1] = out[1] + HALF * v[0]
        for k in range(1, len(v)):
            out[k - 1] = out[k - 1] + 0.5 * HALF * v[k]
            out[k + 1] = out[k + 1] + 0.5 * HALF * v[k]
        return out

    def against(v, l):
        return MID * v[l] + 0.5 * HALF * (v[l + 1] + v[abs(l - 1)])

    res, way = list(m), list(m)
    res_in, way_in, lat_in = [one], [one], [zero] * ITERS
    lead = one
    now = m[0]
    pivots = []
    for it in range(ITERS):
        image = [against(way, l) for l in range(len(way) - 1)]
        alpha = now / (lead * image[it])
        for k in range(it + 1):
            lat_in[k] = lat_in[k] + alpha * way_in[k]
        if it == ITERS - 1:
            break
        res = [res[l] - alpha * image[l] for l in range(len(image))]
        step = moved(way_in)
        res_in = [a - alpha * b for a, b in zip(res_in + [zero], step)]
        lead = res_in[it + 1]
        new = lead * res[it + 1]
        pivots.append(res[it + 1] / (lead * m[0]))
        beta = new / now
        way = [res[l] + beta * way[l] for l in range(len(res))]
        way_in = [a + beta * b for a, b in zip(res_in, way_in + [zero])]
        now = new
    fine = pivots[-1] >= 0.3 * pivots[0]
    for pivot in pivots:
        fine = fine & (pivot >= 5e-3) & (pivot <= 20.0)
    return lat_in, fine


CHUNK = 4 * LANES


def columns_hot_kernel(cols, cells, hot):
    col = lax.rem(cells[...], cols)

    def step(b, carry):
        at = pl.ds(pl.multiple_of(b * LANES, LANES), LANES)
        row = lax.broadcasted_iota(jnp.int32, (LANES, cells.shape[1]), 0) + b * LANES
        hot[at] = jnp.where(row == col, 1.0, 0.0).astype(jnp.bfloat16)
        return carry

    lax.fori_loop(0, hot.shape[0] // LANES, step, 0)


def columns_hot(cells, cols):
    return pl.pallas_call(
        functools.partial(columns_hot_kernel, cols),
        in_specs=[VMEM],
        out_specs=VMEM,
        out_shape=pltpu.VMEM((cols, cells.shape[1]), jnp.bfloat16),
        compiler_params=PARAMS,
        name="columns_hot",
    )(cells)


def finish_kernel(rows, cols, line, cells, row_frac, col_frac, hot, *refs):
    basis, refs = refs[:ITERS], refs[ITERS:]
    latent, predictor, fine, parts, keep, laid, sent = refs
    lat_in, good = coefficients(line[...])
    fine[...] = jnp.where(good, 1.0, 0.0)
    for k in range(ITERS):
        keep[k] = lat_in[k]
    tall = (rows + 2) * F
    lane = lax.broadcasted_iota(jnp.int32, (rows + 2, F, LANES), 2)

    def split(x, at, base):
        part = x.astype(jnp.bfloat16)
        rest = (x - part.astype(jnp.float32)).astype(jnp.bfloat16)
        parts[base : base + tall, at] = part.reshape(tall, LANES)
        parts[base + tall : base + 2 * tall, at] = rest.reshape(tall, LANES)

    def combined(at):
        total = None
        for k in range(ITERS):
            begin = PAD - SKIP * (k % 2)
            term = keep[k] * basis[k][begin : begin + rows + 1, :, at]
            total = term if total is None else total + term
        return jnp.concatenate([total, jnp.zeros((1, F, LANES), jnp.float32)], axis=0)

    def step(c, after):
        at = pl.ds(pl.multiple_of((cols // LANES - 1 - c) * LANES, LANES), LANES)
        total = combined(at)
        turned = pltpu.roll(total, LANES - 1, 2)
        split(total, at, 0)
        split(jnp.where(lane == LANES - 1, after, turned), at, 2 * tall)
        laid[:, :, at] = jnp.swapaxes(total[:rows], 0, 1)
        return turned

    beyond = pltpu.roll(combined(slice(cols, cols + LANES)), LANES - 1, 2)
    lax.fori_loop(0, cols // LANES, step, beyond, unroll=2)
    copy = pltpu.make_async_copy(laid, latent, sent)
    copy.start()
    for c in range(0, cells.shape[1], CHUNK):
        at = slice(c, c + CHUNK)
        both = jnp.dot(parts[...], hot[:, at], preferred_element_type=jnp.float32)
        here = both[:tall] + both[tall : 2 * tall]
        beside = both[2 * tall : 3 * tall] + both[3 * tall :]
        row = cells[:, at] // cols
        frac = row_frac[:, at]
        low = jnp.zeros((F, CHUNK), jnp.float32)
        high = jnp.zeros((F, CHUNK), jnp.float32)
        for r in range(rows + 1):
            w = jnp.where(row == r, 1.0 - frac, jnp.where(row + 1 == r, frac, 0.0))
            low = low + w * here[r * F : (r + 1) * F]
            high = high + w * beside[r * F : (r + 1) * F]
        side = col_frac[:, at]
        out = (1.0 - side) * low + side * high
        for i in range(CHUNK // LANES):
            base = (c // LANES + i) * F
            predictor[base : base + F] = out[:, i * LANES : (i + 1) * LANES]
    copy.wait()


def finish(rows, cols, line, cells, row_frac, col_frac, hot, basis):
    f32 = jnp.float32
    return pl.pallas_call(
        functools.partial(finish_kernel, rows, cols),
        in_specs=[VMEM] * (5 + ITERS),
        out_specs=[HBM, VMEM, VMEM],
        out_shape=[
            pltpu.HBM((F, rows, cols), f32),
            jax.ShapeDtypeStruct((cells.shape[1] // LANES * F, LANES), f32),
            jax.ShapeDtypeStruct((F, LANES), f32),
        ],
        scratch_shapes=[
            pltpu.VMEM((4 * (rows + 2) * F, cols), jnp.bfloat16),
            pltpu.VMEM((ITERS, F, LANES), f32),
            pltpu.VMEM((F, rows, cols), f32),
            pltpu.SemaphoreType.DMA,
        ],
        compiler_params=PARAMS,
        name="finish",
    )(line, cells, row_frac, col_frac, *[held(x) for x in (hot, *basis)])


def extended(x, sides, width):
    for axis, dim in sides:
        size, length = (lax.axis_size(axis), x.shape[dim])
        up = [(i, (i + 1) % size) for i in range(size - 1)]
        down = [(j, i) for i, j in up]
        last = lax.slice_in_dim(x, length - width, length, axis=dim)
        leading = lax.slice_in_dim(x, 0, width, axis=dim)
        before = lax.ppermute(last, axis, up)
        after = lax.ppermute(leading, axis, down)
        x = jnp.concatenate([before, x, after], axis=dim)
    return x


def passed_along(x, axis, by):
    length = lax.axis_size(axis)
    pairs = [(i, i + by) for i in range(length) if 0 <= i + by < length]
    return lax.ppermute(x, axis, pairs)


def neighbours(padded):
    return padded[:, 2:, 1:-1] + padded[:, :-2, 1:-1] + padded[:, 1:-1, 2:] + padded[:, 1:-1, :-2]


def plain(right_side, kappa_field, tau_field, curvature, got_cells, got_row, got_col):
    def squares(values):
        return lax.psum(jnp.sum(values * values, axis=(1, 2)), ("tile", "field"))[:, None, None]

    def sweep(_, state):
        latent, residual, direction, norm_now = state
        padded = extended(direction, (("tile", 1), ("field", 2)), 1)
        scaled = tau_field * ((kappa_field + 4.0) * direction - neighbours(padded))
        spread = extended(scaled, (("tile", 1), ("field", 2)), 1)
        image = (kappa_field + 4.0) * scaled - neighbours(spread) + curvature * direction
        inner = lax.psum(jnp.sum(direction * image, axis=(1, 2)), ("tile", "field"))[:, None, None]
        alpha = norm_now / inner
        latent = latent + alpha * direction
        residual = residual - alpha * image
        norm_next = squares(residual)
        direction = residual + norm_next / norm_now * direction
        return latent, residual, direction, norm_next

    state = (jnp.zeros_like(right_side), right_side, right_side, squares(right_side))
    latent = lax.fori_loop(0, ITERS, sweep, state)[0]
    upper = passed_along(latent[:, :1, :], "tile", -1)
    tall = jnp.concatenate([latent, upper], axis=1)
    beside = passed_along(tall[:, :, :1], "field", -1)
    wide = jnp.concatenate([tall, beside], axis=2)
    columns = latent.shape[2]
    width = columns + 1
    flat = wide.reshape(wide.shape[0], -1)
    base = (got_cells // columns * width + got_cells % columns).astype(jnp.int32)

    def corner(offset):
        return jnp.take(flat, base + offset, axis=1)

    row_frac = got_row[None]
    col_frac = got_col[None]
    predictor = (
        (1.0 - row_frac) * (1.0 - col_frac) * corner(0)
        + row_frac * (1.0 - col_frac) * corner(width)
        + (1.0 - row_frac) * col_frac * corner(1)
        + row_frac * col_frac * corner(width + 1)
    )
    return latent, jnp.transpose(predictor, (1, 0, 2)).reshape(-1, predictor.shape[2])


def turned(x, axis, by):
    size = lax.axis_size(axis)
    return lax.ppermute(x, axis, [(i, (i + by) % size) for i in range(size)])


def summed(x, axis):
    size, stride = lax.axis_size(axis), 1
    while stride < size:
        if size // stride in (4, 16):
            for by in (1, -1):
                x = x + lax.ppermute(
                    x, axis, [(i, other(i, stride, by)) for i in range(size)]
                )
            stride *= 4
        else:
            x = x + lax.ppermute(x, axis, [(i, i ^ stride) for i in range(size)])
            stride *= 2
    return x


def other(i, stride, by):
    place = i // stride % 4
    partner = (place + (by if place % 2 == 0 else -by)) % 4
    return i + (partner - place) * stride


def local(
    right_side,
    kappa_field,
    tau_field,
    curvature,
    detect_prob,
    site_cells,
    site_offsets,
    site_count,
    visit_count,
    detections,
    surveyed,
):
    rows, cols = right_side.shape[1:]
    wide = cols + LANES
    tiles, bands = lax.axis_size("tile"), lax.axis_size("field")
    tile, band = lax.axis_index("tile"), lax.axis_index("field")
    flags = jnp.stack([band > 0, band < bands - 1, tile > 0, tile < tiles - 1]).astype(jnp.float32)
    lane = lax.broadcasted_iota(jnp.int32, (F, LANES), 1)
    mask = jnp.where(lane < SIDE, flags[1], jnp.where(lane >= LANES - SIDE, flags[0], 0.0))

    fields = (right_side, kappa_field, tau_field, curvature)
    cells = site_cells[0, 0]
    to_left, to_right, sent = columns_of(fields, cells, site_offsets[0, 0])
    from_right = turned(to_left, "field", -1)
    from_left = turned(to_right, "field", 1)
    *mains, to_up, to_down = prepare(flags, from_left, from_right, fields)
    sent, to_up, to_down = lax.optimization_barrier((sent, to_up, to_down))
    got = lax.all_to_all(sent, "tile", split_axis=0, concat_axis=0, tiled=True)
    flags, got = lax.optimization_barrier((flags, got))
    got_cells = got[:, 0].astype(jnp.int32)
    got_row, got_col = got[:, 1], got[:, 2]
    sites = (got_cells.reshape(1, -1), got_row.reshape(1, -1), got_col.reshape(1, -1))
    common = (rows, cols, flags, mask)

    def exchanged(to_up, to_down):
        return turned(to_down, "tile", 1), turned(to_up, "tile", -1)

    up, down = exchanged(to_up, to_down)
    older, old, *coefs, own, to_up, to_down, part = phase(0, *common, up, down, mains)
    basis, sums = [older, old], [part]
    for p in range(1, ITERS // 2 - 1):
        up, down = exchanged(to_up, to_down)
        older, old, own, to_up, to_down, part = phase(p, *common, up, down, (own, *coefs, older, old))
        basis += [older, old]
        sums.append(part)
    up, down = exchanged(to_up, to_down)
    line, older, old = phase(ITERS // 2 - 1, *common, up, down, (own, *coefs, older, old), earlier=sums)
    basis += [older, old]

    line, got_cells = lax.optimization_barrier((line, got_cells))
    hot = columns_hot(got_cells.reshape(1, -1), cols)
    line = summed(line, "field")
    line, hot = lax.optimization_barrier((line, hot))
    line = summed(line, "tile")
    latent, predictor, fine = finish(rows, cols, line, *sites, hot, basis)
    latent, predictor, _ = lax.while_loop(
        lambda state: state[2],
        lambda state: plain(*fields, got_cells, got_row, got_col) + (False,),
        (latent, predictor, jnp.logical_not(jnp.all(fine > 0.5))),
    )
    predictor = predictor.reshape(tiles, F, LANES)
    returned = lax.all_to_all(predictor, "tile", split_axis=0, concat_axis=0, tiled=True)

    slots = lax.broadcasted_iota(jnp.int32, cells.shape, 1)
    live = (slots < site_count[0, 0][:, None]).astype(jnp.float32)[:, None, :]
    visits = visit_count[0, 0].astype(jnp.float32)[:, None, :]
    miss_prob = jnp.exp(visits * jnp.log(1.0 - detect_prob)[:, None])
    expo = jnp.exp(returned)
    seen_grad = 1.0 / (1.0 + expo)
    miss_grad = -(1.0 - miss_prob) * expo / ((1.0 + expo) * (1.0 + miss_prob * expo))
    site_grad = (
        jnp.where(detections[0, 0] > 0, seen_grad, miss_grad)
        * surveyed[0, 0].astype(jnp.float32)
        * live
    )
    return (latent, site_grad[None, None])


def solution(mesh):
    in_specs = (
        P(None, "tile", "field"),
        P(None, "tile", "field"),
        P(None, "tile", "field"),
        P(None, "tile", "field"),
        P(),
        P("tile", "field", None, None),
        P("tile", "field", None, None, None),
        P("tile", "field", None),
        P("tile", "field", None, None),
        P("tile", "field", None, None, None),
        P("tile", "field", None, None, None),
    )
    out_specs = (P(None, "tile", "field"), P("tile", "field", None, None, None))
    return jax.shard_map(local, mesh=mesh, in_specs=in_specs, out_specs=out_specs, check_vma=False)
```
